256 devices in a mesh: lon: 64 (over y, x_lo, z), lat: 4 (over x_hi, core).
Axes of the slice: x: 4 (x_hi: 2, x_lo: 2; x = x_hi * 2 + x_lo), y: 4, z: 8, core: 2. Of those that a mesh axis runs over, the one named last changes fastest.
Arguments:
- height: float32 [4096, 1024], P('lon', 'lat')
- albedo: float32 [4096, 1024], P('lon', 'lat'), may hold values from 0.6 to 1.4
- images: bfloat16 [12, 4096, 1024], P(None, 'lon', 'lat'), may hold values from 0.049804688 to 0.59765625
- lit_mask: int32 [12, 4096, 1024], P(None, 'lon', 'lat'), may hold values from 0 to 1, as said below
- lit_count: int32 [12, 64, 4], P(None, 'lon', 'lat'), may hold values from 0 to 16384, as said below
- geometry: float32 [12, 4], replicated, may hold values from -1 to 1, as said below
- owner_column: int32 [4096, 1024], P('lon', 'lat'), may hold values from 0 to 1023, as said below
- altimetry: float32 [1024, 256], P('lon', 'lat'), may hold values from -30 to 30, as said below
Outputs:
- refined: float32 [4096, 1024], P('lon', 'lat')
The draws below stay inside these ranges and needn't reach their ends.
Inputs may be any that keep to these rules, and one draw needn't show every extreme that they name: lit_mask is 0 or 1; the share of lit cells differs between sectors and images. lit_count[k, a, b] is the number of ones of lit_mask[k] in sector a (rows a * 64 to (a + 1) * 64 - 1) and band b (columns b * 256 to (b + 1) * 256 - 1). owner_column[i, j] = ((i + s_j) // 4) mod 1024, where s_j, from 0 to 3, depends on the column j only; every owner has exactly 4^2 cells. Rows of geometry hold a unit sun direction of low elevation and an emission cosine between 0.8 and 1. `altimetry`: elevations in metres.
All inputs are finite; a program needn't handle non-finite values.
Results may differ from the reference program's by a relative error of at most 0.0003.
Values sent between devices are 32-bit elements; how exact they have to be, the bound alone decides.
No kernel may reach another device: no remote copies, remote signals or barrier semaphores. Data moves between devices by JAX's collectives and lax.ppermute only.
A program may use at most 64 MiB of HBM per device.

```python
import math
import jax
import jax.numpy as jnp
from jax import lax

CLON = 64
CLAT = 256
IMAGES = 12
RAD = 16
OWN = 4
ITERS = 3
NLON = 4096
NLAT = 1024
OLON = 1024
OLAT = 256


def relief_field(key):
    subkeys = jax.random.split(jax.random.fold_in(key, 21), 5)
    lon_pos = jnp.arange(NLON, dtype=jnp.float32)[:, None]
    lat_pos = jnp.arange(NLAT, dtype=jnp.float32)[None, :]
    frequency = jax.random.uniform(subkeys[0], (6, 2), minval=1.0 / 400.0, maxval=1.0 / 60.0)
    signs = jnp.where(jax.random.bernoulli(subkeys[1], 0.5, (6, 2)), 1.0, -1.0)
    frequency = frequency * signs
    phases = jax.random.uniform(subkeys[2], (6,), minval=-math.pi, maxval=math.pi)
    amplitude = jax.random.uniform(subkeys[3], (6,), minval=1.5, maxval=3.5)
    relief = jnp.zeros((NLON, NLAT), jnp.float32)
    for wave_index in range(6):
        relief = relief + amplitude[wave_index] * jnp.sin(2.0 * math.pi * (frequency[wave_index, 0] * lon_pos + frequency[wave_index, 1] * lat_pos) + phases[wave_index])
    roughness = 0.3 * jax.random.normal(subkeys[4], (NLON, NLAT), jnp.float32)
    return (relief + roughness).astype(jnp.float32)


def draw_height(key, part):
    return relief_field(key)


def column_shifts(key):
    return jax.random.randint(jax.random.fold_in(key, 5), (1, NLAT), 0, OWN)


def draw_altimetry(key, part):
    surface = relief_field(key)
    shift_row = column_shifts(key)
    source_rows = ((jnp.arange(NLON, dtype=jnp.int32)[:, None] - shift_row) % NLON).astype(jnp.int32)
    aligned = jnp.take_along_axis(surface, source_rows, axis=0)
    owner_means = aligned.reshape(NLON // OWN, OWN, NLAT // OWN, OWN).mean(axis=(1, 3))
    noise_key = jax.random.fold_in(key, 37)
    noise = 0.3 * jax.random.normal(noise_key, owner_means.shape, jnp.float32)
    return (owner_means + noise).astype(jnp.float32)


def lit_draws(key):
    folded = jax.random.fold_in(key, 11)
    first_key, second_key = jax.random.split(folded)
    sector_count = NLON // CLON
    sectors = (jnp.arange(NLON, dtype=jnp.int32) // CLON)[None, :, None]
    offset = jax.random.randint(first_key, (IMAGES, 1, 1), 0, 100)
    threshold = 200 + 600 * sectors // max(sector_count - 1, 1) + offset
    uniform_draw = jax.random.randint(second_key, (IMAGES, NLON, NLAT), 0, 1000)
    lit_cells = (uniform_draw < threshold).astype(jnp.int32)
    counts = lit_cells.reshape(IMAGES, sector_count, CLON, NLAT // CLAT, CLAT).sum(axis=(2, 4)).astype(jnp.int32)
    return (lit_cells, counts)


def draw_lit_mask(key, part):
    lit_cells, counts = lit_draws(key)
    return lit_cells


def draw_lit_count(key, part):
    lit_cells, counts = lit_draws(key)
    return counts


def draw_owner_column(key, part):
    column_shift = column_shifts(key)
    lon_index = jnp.arange(NLON, dtype=jnp.int32)[:, None]
    return ((lon_index + column_shift) // OWN % (NLON // OWN)).astype(jnp.int32)


def draw_geometry(key, part):
    subkeys = jax.random.split(jax.random.fold_in(key, 3), 3)
    azimuth = jax.random.uniform(subkeys[0], (IMAGES,), minval=-math.pi, maxval=math.pi)
    elevation = jax.random.uniform(subkeys[1], (IMAGES,), minval=0.03, maxval=0.2)
    view_cos = jax.random.uniform(subkeys[2], (IMAGES,), minval=0.85, maxval=1.0)
    return jnp.stack([jnp.cos(elevation) * jnp.cos(azimuth), jnp.cos(elevation) * jnp.sin(azimuth), jnp.sin(elevation), view_cos], axis=1).astype(jnp.float32)


def steps_of(key, shape, cuts, low, largest):
    loudness = 1.0
    for position, shards_of in cuts:
        draws = jax.random.uniform(jax.random.fold_in(jax.random.fold_in(key, 6), position), (shards_of,), jnp.float32, low / len(cuts), largest / len(cuts))
        loudness = loudness * jnp.repeat(jnp.exp(draws), shape[position] // shards_of).reshape((-1,) + (1,) * (len(shape) - 1 - position))
    return loudness


def setup_inputs(seed: int = 0) -> dict:
    keys = jax.random.split(jax.random.key(seed), 9)
    return {
        "height": draw_height(jax.random.fold_in(keys[8], 71), 0),
        "albedo": jnp.clip(0.6 + 0.79999995 * jax.random.uniform(keys[1], (NLON, NLAT), jnp.float32) ** steps_of(keys[1], (NLON, NLAT), ((0, 64), (1, 4)), -0.2, 0.2), 0.6, 1.4),
        "images": jnp.clip(0.049804688 + 0.54785156 * jax.random.uniform(keys[2], (IMAGES, NLON, NLAT), jnp.float32) ** steps_of(keys[2], (IMAGES, NLON, NLAT), ((1, 64), (2, 4)), -0.2, 0.2), 0.049804688, 0.59765625).astype(jnp.bfloat16),
        "lit_mask": draw_lit_mask(jax.random.fold_in(keys[8], 71), 0),
        "lit_count": draw_lit_count(jax.random.fold_in(keys[8], 71), 0),
        "geometry": draw_geometry(jax.random.fold_in(keys[8], 71), 0),
        "owner_column": draw_owner_column(jax.random.fold_in(keys[8], 71), 0),
        "altimetry": draw_altimetry(jax.random.fold_in(keys[8], 71), 0),
    }


STEP_SIZE = 0.05
ALT_WEIGHT = 64.0
DATA_GAIN = 160.0
LUNAR_MIX = 0.6
SHARPNESS = 20.0

def tap_weights():
    offsets = list(range(-RAD, RAD + 1))
    denom = float(sum((value * value for value in offsets)))
    deriv = [float(value) / denom for value in offsets]
    smooth = [1.0 / (2 * RAD + 1) for value in offsets]
    return (deriv, smooth)

def along_lon(values, weights):
    running_sum = jnp.zeros_like(values)
    for tap_index in range(2 * RAD + 1):
        running_sum = running_sum + weights[tap_index] * jnp.roll(values, -(tap_index - RAD), axis=0)
    return running_sum

def along_lat(values, weights):
    padded = jnp.pad(values, ((0, 0), (RAD, RAD)))
    running_sum = jnp.zeros_like(values)
    for tap_index in range(2 * RAD + 1):
        running_sum = running_sum + weights[tap_index] * padded[:, tap_index:tap_index + NLAT]
    return running_sum

def reference(height, albedo, images, lit_mask, lit_count, geometry, owner_column, altimetry):
    deriv, smooth = tap_weights()
    totals = lax.optimization_barrier(jnp.sum(lit_count, axis=(1, 2))).astype(jnp.float32)
    image_weight = DATA_GAIN * float(NLON * NLAT) / totals
    lat_group = (jnp.arange(NLAT, dtype=jnp.int32) // OWN)[None, :]
    owner_id = owner_column * OLAT + lat_group
    surface = height
    for iteration in range(ITERS):
        slope_lon = along_lat(along_lon(surface, deriv), smooth)
        slope_lat = along_lat(along_lon(surface, smooth), deriv)
        norm = jnp.sqrt(1.0 + slope_lon * slope_lon + slope_lat * slope_lat)

        def accumulate(image_index, running):
            grad_lon, grad_lat = running
            sun_row = geometry[image_index]
            observed = lax.dynamic_index_in_dim(images, image_index, 0, keepdims=False).astype(jnp.float32)
            lit_cells = lax.dynamic_index_in_dim(lit_mask, image_index, 0, keepdims=False).astype(jnp.float32)
            weight = lit_cells * image_weight[image_index]
            facing = sun_row[2] - sun_row[0] * slope_lon - sun_row[1] * slope_lat
            lit_part = jax.nn.softplus(SHARPNESS * facing) / SHARPNESS
            view_cos = sun_row[3]
            shading = LUNAR_MIX * lit_part / (lit_part + view_cos) + (1.0 - LUNAR_MIX) * lit_part / norm
            rendered = albedo * shading
            residual_scale = 2.0 * weight * (rendered - observed) * albedo
            lit_slope = (LUNAR_MIX * view_cos / ((lit_part + view_cos) * (lit_part + view_cos)) + (1.0 - LUNAR_MIX) / norm) * jax.nn.sigmoid(SHARPNESS * facing)
            norm_slope = (1.0 - LUNAR_MIX) * lit_part / (norm * norm * norm)
            grad_lon = grad_lon + residual_scale * (-sun_row[0] * lit_slope - norm_slope * slope_lon)
            grad_lat = grad_lat + residual_scale * (-sun_row[1] * lit_slope - norm_slope * slope_lat)
            return (grad_lon, grad_lat)
        zeros_field = jnp.zeros_like(surface)
        grad_lon, grad_lat = lax.fori_loop(0, IMAGES, accumulate, (zeros_field, zeros_field))
        data_grad = -(along_lat(along_lon(grad_lon, deriv), smooth) + along_lat(along_lon(grad_lat, smooth), deriv))
        owner_sums = jax.ops.segment_sum(surface.reshape(-1), owner_id.reshape(-1), num_segments=OLON * OLAT)
        misfit = 2.0 * ALT_WEIGHT * (owner_sums / (OWN * OWN) - altimetry.reshape(-1)) / (OWN * OWN)
        alt_grad = misfit[owner_id]
        surface = surface - STEP_SIZE * (data_grad + alt_grad)
    return surface
```

```python
import functools

import jax
import jax.numpy as jnp
import numpy as np
from jax import lax
from jax.experimental import pallas as pl
from jax.experimental.pallas import tpu as pltpu
from jax.sharding import PartitionSpec as P

IMAGES = 12
RAD = 16
OWN = 4
ITERS = 3
STEP_SIZE = 0.05
ALT_WEIGHT = 64.0
DATA_GAIN = 160.0
LUNAR_MIX = 0.6
SHARPNESS = 20.0

LANES = 128
STRIP = 32
EXT = STRIP + 2 * RAD
TILES = 5
FIELDS = 2 * IMAGES + 3
ALBEDO = 2 * IMAGES
HEIGHT = ALBEDO + 1
AUX = HEIGHT + 1
BINS = 16
DENOM = float(RAD * (RAD + 1) * (2 * RAD + 1)) / 3.0
TAP_SCALE = 1.0 / (DENOM * (2 * RAD + 1))
F32 = jnp.float32
BF16 = jnp.bfloat16
VMEM = pl.BlockSpec(memory_space=pltpu.VMEM)
SMEM = pl.BlockSpec(memory_space=pltpu.SMEM)
PARAMS = pltpu.CompilerParams(vmem_limit_bytes=24 * 2**20)


def band(offset, derivative):
    inside = np.abs(offset) <= RAD
    return np.where(inside, offset if derivative else 1, 0).astype(np.float32)


def constants():
    own = np.arange(STRIP)
    ext = np.arange(EXT) - RAD
    reach = ext[None, :] - own[:, None]
    rows = [band(reach, True), band(reach, False)]
    bins = np.arange(BINS)
    for shift in range(OWN):
        group = (ext[None, :] + shift) // OWN
        rows.append((group == bins[:, None]).astype(np.float32))
    down = np.concatenate(rows, axis=0)
    forward = np.concatenate([down] * 3, axis=1)
    back = own[None, :] - ext[:, None]
    spread = np.zeros((EXT, OWN * BINS), np.float32)
    for shift in range(OWN):
        hit = ((own[:, None] + shift) // OWN) == bins[None, :]
        spread[RAD : RAD + STRIP, shift * BINS : (shift + 1) * BINS] = hit
    filters = np.concatenate([band(back, True), band(back, False)], axis=1)
    backward = np.concatenate([filters, filters, spread, spread], axis=1)
    lane = np.arange(LANES)
    side = np.where(lane < LANES // 2, lane + LANES, lane - LANES)
    source = np.concatenate([lane, side])
    across = source[:, None] - lane[None, :]
    quads = (lane[:, None] // OWN == lane[None, :] // OWN).astype(np.float32)
    return [
        jnp.asarray(m, BF16)
        for m in (forward, backward, band(across, False), band(across, True), quads)
    ]


def pieces(value, count):
    out = []
    for _ in range(count - 1):
        part = value.astype(BF16)
        value = value - part.astype(F32)
        out.append(part)
    out.append(value.astype(BF16))
    return out


def dot(left, right):
    return jnp.dot(left, right, preferred_element_type=F32)


def with_sides(tiles):
    low = lax.broadcasted_iota(jnp.int32, tiles[0].shape, 1) < LANES // 2
    zero = jnp.zeros_like(tiles[0])
    rows = []
    for j, tile in enumerate(tiles):
        after = tiles[j + 1] if j + 1 < len(tiles) else zero
        before = tiles[j - 1] if j > 0 else zero
        rows.append(jnp.concatenate([tile, jnp.where(low, after, before)], axis=1))
    return jnp.concatenate(rows, axis=0)


def filter_lat(tiles, taps, count):
    total = None
    for part in pieces(with_sides(tiles), count):
        term = dot(part, taps)
        total = term if total is None else total + term
    return total


def place():
    lat = lax.axis_index("lat")
    return lat // 2, lat % 2


def own_tile(half, core, t):
    return half + 2 * core + t


def pack_kernel(height, albedo, images, lit_mask, owner, altimetry, expand, kept, sent):
    half, core = place()
    lon = lax.axis_index("lon")
    bins = owner[0:OWN, :] - lon * BINS
    shift = jnp.sum(bins, axis=0, keepdims=True).astype(F32)
    heights = dot(jnp.concatenate(pieces(altimetry[...], 3), axis=1), expand[...])
    for ref, rows_of in ((kept, core), (sent, 1 - core)):
        start = pl.multiple_of(rows_of * STRIP, STRIP)
        aux_rows = jnp.where(rows_of == 0, heights[0:8], heights[8:16])
        for t in range(2):
            rows, cols = pl.ds(start, STRIP), pl.ds(t * LANES, LANES)
            for k in range(IMAGES):
                ref[k, t] = images[k, rows, cols].astype(F32)
                ref[IMAGES + k, t] = lit_mask[k, rows, cols].astype(F32)
            ref[ALBEDO, t] = albedo[rows, cols]
            ref[HEIGHT, t] = height[rows, cols]
            lanes = slice(t * LANES, (t + 1) * LANES)
            ref[AUX, t, 0:8] = aux_rows[:, lanes]
            ref[AUX, t, 8:16] = jnp.broadcast_to(shift[:, lanes], (8, LANES))
            ref[AUX, t, 16:32] = jnp.zeros((16, LANES), F32)


def route(core, up, down, inter, intra):
    inter[...] = jnp.where(core == 0, up, down)
    intra[...] = jnp.where(core == 0, down, up)


def begin_kernel(kept, received, halo, z, aux, inter, intra):
    half, core = place()
    zero = jnp.zeros((TILES, RAD, LANES), F32)
    z[:, 0:RAD] = zero
    z[:, RAD + STRIP : EXT] = zero
    for t in range(2):
        for ref, at in ((kept, own_tile(half, core, t)), (received, own_tile(half, 1 - core, t))):
            z[at, RAD : RAD + STRIP] = ref[HEIGHT, t]
            aux[at] = ref[AUX, t, 0:BINS]
    far = (TILES - 1) * (1 - half)
    z[far, RAD : RAD + STRIP] = halo[HEIGHT]
    aux[far] = halo[AUX, 0:BINS]
    alt = jnp.concatenate([aux[:, 0:8], jnp.zeros((TILES, 8, LANES), F32)], axis=1)
    up = jnp.concatenate([alt, z[:, RAD : 2 * RAD]], axis=1)
    route(core, up, z[:, STRIP:EXT], inter, intra)


def image_sums(coef, observed, lit, albedo, slope_lon, slope_lat):
    inverse = lax.rsqrt(1.0 + slope_lon * slope_lon + slope_lat * slope_lat)
    flat_part = (1.0 - LUNAR_MIX) * inverse
    flat_shade = flat_part * (albedo * (1.0 / SHARPNESS))
    mix_shade = albedo * LUNAR_MIX
    sum_lon = sum_lat = sum_norm = None
    for k in range(IMAGES):
        steep = coef[k, 2] - coef[k, 0] * slope_lon - coef[k, 1] * slope_lat
        decay = jnp.exp(-jnp.abs(steep))
        whole = 1.0 + decay
        part = jnp.maximum(steep, 0.0) + jnp.log(whole)
        ratio = 1.0 / (part + coef[k, 3])
        gate = jnp.where(steep >= 0.0, 1.0, decay) / whole
        rendered = part * (mix_shade * ratio + flat_shade)
        residual = lit(k) * (rendered - observed(k))
        pull = residual * ((coef[k, 4] * (ratio * ratio) + flat_part) * gate)
        add_lon, add_lat = coef[k, 5] * pull, coef[k, 6] * pull
        add_norm = (coef[k, 7] * residual) * part
        if k == 0:
            sum_lon, sum_lat, sum_norm = add_lon, add_lat, add_norm
        else:
            sum_lon, sum_lat, sum_norm = sum_lon + add_lon, sum_lat + add_lat, sum_norm + add_norm
    bend = (1.0 - LUNAR_MIX) / SHARPNESS * (inverse * inverse * inverse) * sum_norm
    return albedo * (sum_lon - slope_lon * bend), albedo * (sum_lat - slope_lat * bend)


def step_kernel(first, *refs):
    (coef, kept, received, halo, z, inter, intra, aux, alt_in, forward, backward) = refs[:11]
    smooth, slope, quads = refs[11:14]
    z_out, inter_out, intra_out = refs[14:17]
    refs = refs[17:]
    if first:
        alt_out, refs = refs[0], refs[1:]
    slope_lon, slope_lat, grad_lon, grad_lat = refs
    half, core = place()
    tiles = range(TILES)
    above = jnp.where(core == 0, inter[...], intra[...])
    below = jnp.where(core == 0, intra[...], inter[...])
    if first:
        alt = jnp.concatenate([aux[:, 0:8], below[:, 0:8]], axis=1)
        alt_out[...] = alt
        below = jnp.concatenate([jnp.zeros((TILES, RAD, LANES), F32), below[:, RAD:]], axis=1)
    else:
        alt = alt_in[...]
    surface = [z[j] + jnp.concatenate([above[j], below[j]], axis=0) for j in tiles]
    stacked = jnp.concatenate(
        [jnp.concatenate(pieces(surface[j], 3), axis=0) for j in tiles], axis=1
    )
    down = dot(forward[...], stacked)

    def part(row, count, j):
        return down[row : row + count, j * LANES : (j + 1) * LANES]

    slope_lon[...] = TAP_SCALE * filter_lat([part(0, STRIP, j) for j in tiles], smooth[...], 3)
    slope_lat[...] = TAP_SCALE * filter_lat([part(STRIP, STRIP, j) for j in tiles], slope[...], 3)

    shifts = [jnp.concatenate([aux[j, 8:16]] * 2, axis=0) for j in tiles]
    sums = []
    for j in tiles:
        chosen = part(2 * STRIP, BINS, j)
        for s in range(1, OWN):
            chosen = jnp.where(shifts[j] == float(s), part(2 * STRIP + s * BINS, BINS, j), chosen)
        sums.append(chosen)
    owner_sum = None
    for p in pieces(jnp.concatenate(sums, axis=0), 3):
        term = dot(p, quads[...])
        owner_sum = term if owner_sum is None else owner_sum + term

    gain = STEP_SIZE * 2.0 * ALT_WEIGHT / (OWN * OWN)
    misfits = []
    for j in tiles:
        pull = gain * alt[j] - (gain / (OWN * OWN)) * owner_sum[j * BINS : (j + 1) * BINS]
        misfits.append(
            jnp.concatenate([jnp.where(shifts[j] == float(s), pull, 0.0) for s in range(OWN)], axis=0)
        )

    def image_tile(ref, at, index):
        rows = pl.ds(pl.multiple_of(at * STRIP, STRIP), STRIP)
        g_lon, g_lat = image_sums(
            coef,
            lambda k: ref[(k, *index)],
            lambda k: ref[(IMAGES + k, *index)],
            ref[(ALBEDO, *index)],
            slope_lon[rows],
            slope_lat[rows],
        )
        grad_lon[rows] = g_lon
        grad_lat[rows] = g_lat

    for t in range(2):
        image_tile(kept, own_tile(half, core, t), (t,))
        image_tile(received, own_tile(half, 1 - core, t), (t,))
    image_tile(halo, (TILES - 1) * (1 - half), ())

    def field(ref):
        return [ref[j * STRIP : (j + 1) * STRIP] for j in tiles]

    scale = STEP_SIZE * TAP_SCALE
    from_lon = scale * filter_lat(field(grad_lon), smooth[...], 2)
    from_lat = scale * filter_lat(field(grad_lat), slope[...], 2)
    columns = []
    for j in tiles:
        rows = slice(j * STRIP, (j + 1) * STRIP)
        data = pieces(jnp.concatenate([from_lon[rows], from_lat[rows]], axis=0), 2)
        columns.append(jnp.concatenate(data + pieces(misfits[j], 2), axis=0))
    spread = dot(backward[...], jnp.concatenate(columns, axis=1))
    for j in tiles:
        change = spread[:, j * LANES : (j + 1) * LANES]
        z_out[j, 0:RAD] = change[0:RAD]
        z_out[j, RAD : RAD + STRIP] = change[RAD : RAD + STRIP] + surface[j][RAD : RAD + STRIP]
        z_out[j, RAD + STRIP : EXT] = change[RAD + STRIP : EXT]
    route(core, z_out[:, 0:STRIP], z_out[:, STRIP:EXT], inter_out, intra_out)


def end_kernel(z, inter, intra, kept, sent):
    half, core = place()
    for ref, side in ((kept, core), (sent, 1 - core)):
        for t in range(2):
            at = own_tile(half, side, t)
            above = jnp.where(core == 0, inter[at], intra[at])
            below = jnp.where(core == 0, intra[at], inter[at])
            cols = slice(t * LANES, (t + 1) * LANES)
            ref[0:RAD, cols] = z[at, RAD : 2 * RAD] + above[RAD:]
            ref[RAD:STRIP, cols] = z[at, 2 * RAD : RAD + STRIP] + below[0:RAD]


def f32(*shape):
    return jax.ShapeDtypeStruct(shape, F32)


def per_device(height, albedo, images, lit_mask, lit_count, geometry, owner_column, altimetry):
    lon_count, lat_count = lax.axis_size("lon"), lax.axis_size("lat")
    axes = ("lon", "lat")
    devices = lon_count * lat_count
    sites = [(a, b) for a in range(lon_count) for b in range(lat_count)]

    def index(a, b):
        return (a % lon_count) * lat_count + b

    across_cores = [(index(a, b), index(a, b ^ 1)) for a, b in sites]
    across_halves = [(index(a, b), index(a, b ^ 2)) for a, b in sites]
    across_strips = [(index(a, b), index(a + 2 * (b % 2) - 1, b ^ 1)) for a, b in sites]

    def exchange(inter, intra):
        return lax.ppermute(inter, axes, across_strips), lax.ppermute(intra, axes, across_cores)

    counts = jnp.broadcast_to(
        jnp.pad(lit_count.reshape(1, 1, IMAGES).astype(F32), ((0, 0), (0, 0), (0, LANES - IMAGES))),
        (devices, 1, LANES),
    )
    totals = jnp.sum(lax.all_to_all(counts, axes, 0, 0), axis=(0, 1))[:IMAGES]
    cells_all = float(height.size * devices)
    weight = 2.0 * DATA_GAIN * cells_all / totals
    sun_lon, sun_lat, sun_up, view = (geometry[:, i] for i in range(4))
    coef = jnp.stack(
        [
            SHARPNESS * sun_lon,
            SHARPNESS * sun_lat,
            SHARPNESS * sun_up,
            SHARPNESS * view,
            (LUNAR_MIX * SHARPNESS * SHARPNESS) * view,
            -weight * sun_lon,
            -weight * sun_lat,
            weight,
        ],
        axis=1,
    )

    expand = np.arange(altimetry.shape[1])[:, None] == np.arange(2 * LANES)[None, :] // OWN
    expand = jnp.asarray(np.concatenate([expand] * 3, axis=0), BF16)
    kept, sent = pl.pallas_call(
        pack_kernel,
        out_shape=(f32(FIELDS, 2, STRIP, LANES),) * 2,
        in_specs=[VMEM] * 7,
        out_specs=(VMEM,) * 2,
        compiler_params=PARAMS,
    )(height, albedo, images, lit_mask, owner_column[:8], altimetry, expand)
    received = lax.ppermute(sent, axes, across_cores)
    half, core = place()
    near = lax.dynamic_index_in_dim(
        jnp.where(half == core, received, kept), 1 - half, axis=1, keepdims=False
    )
    halo = lax.ppermute(near, axes, across_halves)
    z, aux, inter, intra = pl.pallas_call(
        begin_kernel,
        out_shape=(
            f32(TILES, EXT, LANES),
            f32(TILES, BINS, LANES),
            f32(TILES, STRIP, LANES),
            f32(TILES, STRIP, LANES),
        ),
        in_specs=[VMEM] * 3,
        out_specs=(VMEM,) * 4,
        compiler_params=PARAMS,
    )(kept, received, halo)
    inter, intra = exchange(inter, intra)
    tables = constants()
    alt = aux
    for iteration in range(ITERS):
        first = iteration == 0
        shapes = [f32(TILES, EXT, LANES), f32(TILES, STRIP, LANES), f32(TILES, STRIP, LANES)]
        if first:
            shapes.append(f32(TILES, BINS, LANES))
        out = pl.pallas_call(
            functools.partial(step_kernel, first),
            out_shape=tuple(shapes),
            in_specs=[SMEM] + [VMEM] * 13,
            out_specs=(VMEM,) * len(shapes),
            scratch_shapes=[pltpu.VMEM((TILES * STRIP, LANES), F32)] * 4,
            compiler_params=PARAMS,
        )(coef, kept, received, halo, z, inter, intra, aux, alt, *tables)
        z, inter, intra = out[:3]
        if first:
            alt = out[3]
        inter, intra = exchange(inter, intra)
    mine, other = pl.pallas_call(
        end_kernel,
        out_shape=(f32(STRIP, 2 * LANES),) * 2,
        in_specs=[VMEM] * 3,
        out_specs=(VMEM,) * 2,
        compiler_params=PARAMS,
    )(z, inter, intra)
    other = lax.ppermute(other, axes, across_cores)
    upper = jnp.where(core == 0, mine, other)
    lower = jnp.where(core == 0, other, mine)
    return jnp.concatenate([upper, lower], axis=0)


def solution(mesh):
    return jax.shard_map(
        per_device,
        mesh=mesh,
        in_specs=(
            P("lon", "lat"),
            P("lon", "lat"),
            P(None, "lon", "lat"),
            P(None, "lon", "lat"),
            P(None, "lon", "lat"),
            P(),
            P("lon", "lat"),
            P("lon", "lat"),
        ),
        out_specs=P("lon", "lat"),
        check_vma=False,
    )
```

```python
import functools

import jax
import jax.numpy as jnp
import numpy as np
from jax import lax
from jax.experimental import pallas as pl
from jax.experimental.pallas import tpu as pltpu
from jax.sharding import PartitionSpec as P

IMAGES = 12
RAD = 16
OWN = 4
ITERS = 3
ROWS = 4096
COLUMNS = 1024
STEP_SIZE = 0.05
ALT_WEIGHT = 64.0
DATA_GAIN = 160.0
LUNAR_MIX = 0.6
SHARPNESS = 20.0

LANES = 128
STRIP = 32
EXT = STRIP + 2 * RAD
TILES = 5
FIELDS = 2 * IMAGES + 3
ALBEDO = 2 * IMAGES
HEIGHT = ALBEDO + 1
AUX = HEIGHT + 1
BINS = 16
DENOM = float(RAD * (RAD + 1) * (2 * RAD + 1)) / 3.0
TAP_SCALE = 1.0 / (DENOM * (2 * RAD + 1))
F32 = jnp.float32
BF16 = jnp.bfloat16
VMEM = pl.BlockSpec(memory_space=pltpu.VMEM)
SMEM = pl.BlockSpec(memory_space=pltpu.SMEM)
PARAMS = pltpu.CompilerParams(vmem_limit_bytes=24 * 2**20)
LARGE = pltpu.CompilerParams(vmem_limit_bytes=58 * 2**20)


def band(offset, derivative):
    inside = np.abs(offset) <= RAD
    return np.where(inside, offset if derivative else 1, 0).astype(np.float32)


def constants():
    own = np.arange(STRIP)
    ext = np.arange(EXT) - RAD
    reach = ext[None, :] - own[:, None]
    rows = [band(reach, True), band(reach, False)]
    bins = np.arange(BINS)
    for shift in range(OWN):
        group = (ext[None, :] + shift) // OWN
        rows.append((group == bins[:, None]).astype(np.float32))
    down = np.concatenate(rows, axis=0)
    forward = np.concatenate([down] * 3, axis=1)
    back = own[None, :] - ext[:, None]
    spread = np.zeros((EXT, OWN * BINS), np.float32)
    for shift in range(OWN):
        hit = ((own[:, None] + shift) // OWN) == bins[None, :]
        spread[RAD : RAD + STRIP, shift * BINS : (shift + 1) * BINS] = hit
    filters = np.concatenate([band(back, True), band(back, False)], axis=1)
    backward = np.concatenate([filters, filters, spread, spread], axis=1)
    lane = np.arange(LANES)
    side = np.where(lane < LANES // 2, lane + LANES, lane - LANES)
    source = np.concatenate([lane, side])
    across = source[:, None] - lane[None, :]
    quads = (lane[:, None] // OWN == lane[None, :] // OWN).astype(np.float32)
    return [
        jnp.asarray(m, BF16)
        for m in (forward, backward, band(across, False), band(across, True), quads)
    ]


def pieces(value, count):
    out = []
    for _ in range(count - 1):
        part = value.astype(BF16)
        value = value - part.astype(F32)
        out.append(part)
    out.append(value.astype(BF16))
    return out


def dot(left, right):
    return jnp.dot(left, right, preferred_element_type=F32)


def with_sides(tiles):
    low = lax.broadcasted_iota(jnp.int32, tiles[0].shape, 1) < LANES // 2
    zero = jnp.zeros_like(tiles[0])
    rows = []
    for j, tile in enumerate(tiles):
        after = tiles[j + 1] if j + 1 < len(tiles) else zero
        before = tiles[j - 1] if j > 0 else zero
        rows.append(jnp.concatenate([tile, jnp.where(low, after, before)], axis=1))
    return jnp.concatenate(rows, axis=0)


def filter_lat(tiles, taps, count):
    total = None
    for part in pieces(with_sides(tiles), count):
        term = dot(part, taps)
        total = term if total is None else total + term
    return total


def place():
    lat = lax.axis_index("lat")
    return lat // 2, lat % 2


def own_tile(half, core, t):
    return half + 2 * core + t


def pack_kernel(
    images_hbm, mask_hbm, height_hbm, albedo_hbm, owner_hbm, altimetry_hbm, count_hbm, expand_hbm,
    kept, sent,
    images, lit_mask, height, albedo, owner, altimetry, count, expand, sems,
):
    copies = [
        pltpu.make_async_copy(source, target, sems.at[i])
        for i, (source, target) in enumerate(
            (
                (images_hbm, images),
                (mask_hbm, lit_mask),
                (height_hbm, height),
                (albedo_hbm, albedo),
                (owner_hbm.at[pl.ds(0, 8)], owner),
                (altimetry_hbm, altimetry),
                (count_hbm, count),
                (expand_hbm, expand),
            )
        )
    ]
    for copy in copies:
        copy.start()
    core = place()[1]
    lon = lax.axis_index("lon")
    for copy in copies:
        copy.wait()
    bins = owner[0:OWN, :] - lon * BINS
    shift = jnp.sum(bins, axis=0, keepdims=True).astype(F32)
    heights = dot(jnp.concatenate(pieces(altimetry[...], 3), axis=1), expand[...])
    lit = jnp.concatenate([count[...].astype(F32), jnp.zeros((1, LANES - IMAGES), F32)], axis=1)
    lit = jnp.broadcast_to(lit, (8, LANES))
    for ref, rows_of in ((sent, 1 - core), (kept, core)):
        start = pl.multiple_of(rows_of * STRIP, STRIP)
        aux_rows = jnp.where(rows_of == 0, heights[0:8], heights[8:16])
        for t in range(2):
            rows, cols = pl.ds(start, STRIP), pl.ds(t * LANES, LANES)
            for k in range(IMAGES):
                ref[k, t] = images[k, rows, cols].astype(F32)
                ref[IMAGES + k, t] = lit_mask[k, rows, cols].astype(F32)
            ref[ALBEDO, t] = albedo[rows, cols]
            ref[HEIGHT, t] = height[rows, cols]
            lanes = slice(t * LANES, (t + 1) * LANES)
            ref[AUX, t, 0:8] = aux_rows[:, lanes]
            ref[AUX, t, 8:16] = jnp.broadcast_to(shift[:, lanes], (8, LANES))
            ref[AUX, t, 16:24] = lit
            ref[AUX, t, 24:32] = jnp.zeros((8, LANES), F32)


def near_kernel(kept, received, near_small, near):
    half, core = place()
    t = 1 - half
    from_kept = half != core
    for i, field in enumerate((HEIGHT, AUX)):
        near_small[i] = jnp.where(from_kept, kept[field, t], received[field, t])
    near_small[1, 16:24] = kept[AUX, 0, 16:24] + received[AUX, 0, 16:24]

    @pl.when(from_kept)
    def _():
        near[...] = kept[0:HEIGHT, t]

    @pl.when(jnp.logical_not(from_kept))
    def _():
        near[...] = received[0:HEIGHT, t]


def route(core, up, down, inter, intra):
    inter[...] = jnp.where(core == 0, up, down)
    intra[...] = jnp.where(core == 0, down, up)


def begin_kernel(kept, received, halo_small, z, aux, inter, intra, counts):
    half, core = place()
    zero = jnp.zeros((TILES, RAD, LANES), F32)
    z[:, 0:RAD] = zero
    z[:, RAD + STRIP : EXT] = zero
    for t in range(2):
        for ref, at in ((kept, own_tile(half, core, t)), (received, own_tile(half, 1 - core, t))):
            z[at, RAD : RAD + STRIP] = ref[HEIGHT, t]
            aux[at] = ref[AUX, t, 0:BINS]
    far = (TILES - 1) * (1 - half)
    z[far, RAD : RAD + STRIP] = halo_small[0]
    aux[far] = halo_small[1, 0:BINS]
    total = kept[AUX, 0, 16:17] + received[AUX, 0, 16:17] + halo_small[1, 16:17]
    counts[...] = jnp.broadcast_to(total[None], counts.shape)
    alt = jnp.concatenate([aux[:, 0:8], jnp.zeros((TILES, 8, LANES), F32)], axis=1)
    up = jnp.concatenate([alt, z[:, RAD : 2 * RAD]], axis=1)
    route(core, up, z[:, STRIP:EXT], inter, intra)


def image_weights(counts):
    total = jnp.sum(counts[...], axis=0)
    weight = 2.0 * DATA_GAIN * float(ROWS * COLUMNS) / total
    image = lax.broadcasted_iota(jnp.int32, (BINS, LANES), 0)
    lane = lax.broadcasted_iota(jnp.int32, (BINS, LANES), 1)
    diagonal = jnp.where((image == lane) & (image < IMAGES), weight, 0.0)
    ones = jnp.ones((LANES, LANES), BF16)
    first, second, third = pieces(diagonal, 3)
    return dot(first, ones) + dot(second, ones) + dot(third, ones)


def image_sums(coef, weight, observed, lit, albedo, slope_lon, slope_lat):
    inverse = lax.rsqrt(1.0 + slope_lon * slope_lon + slope_lat * slope_lat)
    flat_part = (1.0 - LUNAR_MIX) * inverse
    flat_shade = flat_part * (albedo * (1.0 / SHARPNESS))
    mix_shade = albedo * LUNAR_MIX
    sum_lon = sum_lat = sum_norm = None
    for k in range(IMAGES):
        steep = coef[k, 2] - coef[k, 0] * slope_lon - coef[k, 1] * slope_lat
        decay = jnp.exp(-jnp.abs(steep))
        whole = 1.0 + decay
        part = jnp.maximum(steep, 0.0) + jnp.log(whole)
        ratio = 1.0 / (part + coef[k, 3])
        gate = jnp.where(steep >= 0.0, 1.0, decay) / whole
        rendered = part * (mix_shade * ratio + flat_shade)
        residual = (weight[k : k + 1] * lit(k)) * (rendered - observed(k))
        pull = residual * ((coef[k, 4] * (ratio * ratio) + flat_part) * gate)
        add_lon, add_lat = coef[k, 5] * pull, coef[k, 6] * pull
        add_norm = residual * part
        if k == 0:
            sum_lon, sum_lat, sum_norm = add_lon, add_lat, add_norm
        else:
            sum_lon, sum_lat, sum_norm = sum_lon + add_lon, sum_lat + add_lat, sum_norm + add_norm
    bend = (1.0 - LUNAR_MIX) / SHARPNESS * (inverse * inverse * inverse) * sum_norm
    return albedo * (sum_lon - slope_lon * bend), albedo * (sum_lat - slope_lat * bend)


def step_kernel(first, *refs):
    coef, kept, received, halo, z, inter, intra, aux, alt_in, weight_in = refs[:10]
    forward, backward, smooth, slope, quads = refs[10:15]
    z_out, inter_out, intra_out = refs[15:18]
    refs = refs[18:]
    if first:
        alt_out, weight_out, refs = refs[0], refs[1], refs[2:]
        weight = image_weights(weight_in)
        weight_out[...] = weight
    else:
        weight = weight_in[...]
    slope_lon, slope_lat, grad_lon, grad_lat = refs
    half, core = place()
    tiles = range(TILES)
    above = jnp.where(core == 0, inter[...], intra[...])
    below = jnp.where(core == 0, intra[...], inter[...])
    if first:
        alt = jnp.concatenate([aux[:, 0:8], below[:, 0:8]], axis=1)
        alt_out[...] = alt
        below = jnp.concatenate([jnp.zeros((TILES, RAD, LANES), F32), below[:, RAD:]], axis=1)
    else:
        alt = alt_in[...]
    surface = [z[j] + jnp.concatenate([above[j], below[j]], axis=0) for j in tiles]
    stacked = jnp.concatenate(
        [jnp.concatenate(pieces(surface[j], 3), axis=0) for j in tiles], axis=1
    )
    down = dot(forward[...], stacked)

    def part(row, count, j):
        return down[row : row + count, j * LANES : (j + 1) * LANES]

    slope_lon[...] = TAP_SCALE * filter_lat([part(0, STRIP, j) for j in tiles], smooth[...], 3)
    slope_lat[...] = TAP_SCALE * filter_lat([part(STRIP, STRIP, j) for j in tiles], slope[...], 3)

    shifts = [jnp.concatenate([aux[j, 8:16]] * 2, axis=0) for j in tiles]
    sums = []
    for j in tiles:
        chosen = part(2 * STRIP, BINS, j)
        for s in range(1, OWN):
            chosen = jnp.where(shifts[j] == float(s), part(2 * STRIP + s * BINS, BINS, j), chosen)
        sums.append(chosen)
    owner_sum = None
    for p in pieces(jnp.concatenate(sums, axis=0), 3):
        term = dot(p, quads[...])
        owner_sum = term if owner_sum is None else owner_sum + term

    gain = STEP_SIZE * 2.0 * ALT_WEIGHT / (OWN * OWN)
    misfits = []
    for j in tiles:
        pull = gain * alt[j] - (gain / (OWN * OWN)) * owner_sum[j * BINS : (j + 1) * BINS]
        misfits.append(
            jnp.concatenate([jnp.where(shifts[j] == float(s), pull, 0.0) for s in range(OWN)], axis=0)
        )

    def image_tile(ref, at, index):
        rows = pl.ds(pl.multiple_of(at * STRIP, STRIP), STRIP)
        g_lon, g_lat = image_sums(
            coef,
            weight,
            lambda k: ref[(k, *index)],
            lambda k: ref[(IMAGES + k, *index)],
            ref[(ALBEDO, *index)],
            slope_lon[rows],
            slope_lat[rows],
        )
        grad_lon[rows] = g_lon
        grad_lat[rows] = g_lat

    for t in range(2):
        image_tile(kept, own_tile(half, core, t), (t,))
        image_tile(received, own_tile(half, 1 - core, t), (t,))
    image_tile(halo, (TILES - 1) * (1 - half), ())

    def field(ref):
        return [ref[j * STRIP : (j + 1) * STRIP] for j in tiles]

    scale = STEP_SIZE * TAP_SCALE
    from_lon = scale * filter_lat(field(grad_lon), smooth[...], 2)
    from_lat = scale * filter_lat(field(grad_lat), slope[...], 2)
    columns = []
    for j in tiles:
        rows = slice(j * STRIP, (j + 1) * STRIP)
        data = pieces(jnp.concatenate([from_lon[rows], from_lat[rows]], axis=0), 2)
        columns.append(jnp.concatenate(data + pieces(misfits[j], 2), axis=0))
    spread = dot(backward[...], jnp.concatenate(columns, axis=1))
    for j in tiles:
        change = spread[:, j * LANES : (j + 1) * LANES]
        z_out[j, 0:RAD] = change[0:RAD]
        z_out[j, RAD : RAD + STRIP] = change[RAD : RAD + STRIP] + surface[j][RAD : RAD + STRIP]
        z_out[j, RAD + STRIP : EXT] = change[RAD + STRIP : EXT]
    route(core, z_out[:, 0:STRIP], z_out[:, STRIP:EXT], inter_out, intra_out)


def end_kernel(z, inter, intra, kept, sent):
    half, core = place()
    for ref, side in ((kept, core), (sent, 1 - core)):
        for t in range(2):
            at = own_tile(half, side, t)
            above = jnp.where(core == 0, inter[at], intra[at])
            below = jnp.where(core == 0, intra[at], inter[at])
            cols = slice(t * LANES, (t + 1) * LANES)
            ref[0:RAD, cols] = z[at, RAD : 2 * RAD] + above[RAD:]
            ref[RAD:STRIP, cols] = z[at, 2 * RAD : RAD + STRIP] + below[0:RAD]


def place_kernel(mine, other, out):
    core = place()[1]
    out[pl.ds(pl.multiple_of(core * STRIP, STRIP), STRIP)] = mine[...]
    out[pl.ds(pl.multiple_of((1 - core) * STRIP, STRIP), STRIP)] = other[...]


def f32(*shape):
    return jax.ShapeDtypeStruct(shape, F32)


def per_device(height, albedo, images, lit_mask, lit_count, geometry, owner_column, altimetry):
    lon_count, lat_count = lax.axis_size("lon"), lax.axis_size("lat")
    axes = ("lon", "lat")
    sites = [(a, b) for a in range(lon_count) for b in range(lat_count)]

    def index(a, b):
        return (a % lon_count) * lat_count + b

    across_cores = [(index(a, b), index(a, b ^ 1)) for a, b in sites]
    across_halves = [(index(a, b), index(a, b ^ 2)) for a, b in sites]
    across_strips = [(index(a, b), index(a + 2 * (b % 2) - 1, b ^ 1)) for a, b in sites]

    def exchange(inter, intra):
        return lax.ppermute(inter, axes, across_strips), lax.ppermute(intra, axes, across_cores)

    sun_lon, sun_lat, sun_up, view = (geometry[:, i] for i in range(4))
    coef = jnp.stack(
        [
            SHARPNESS * sun_lon,
            SHARPNESS * sun_lat,
            SHARPNESS * sun_up,
            SHARPNESS * view,
            (LUNAR_MIX * SHARPNESS * SHARPNESS) * view,
            -sun_lon,
            -sun_lat,
        ],
        axis=1,
    )

    expand = np.arange(altimetry.shape[1])[:, None] == np.arange(2 * LANES)[None, :] // OWN
    expand = jnp.asarray(np.concatenate([expand] * 3, axis=0), BF16)
    count = lit_count.reshape(1, IMAGES)
    inputs = (images, lit_mask, height, albedo, owner_column, altimetry, count, expand)
    held = [
        pltpu.VMEM((8,) + a.shape[1:] if a is owner_column else a.shape, a.dtype) for a in inputs
    ]
    kept, sent = pl.pallas_call(
        pack_kernel,
        out_shape=(f32(FIELDS, 2, STRIP, LANES),) * 2,
        in_specs=[pl.BlockSpec(memory_space=pltpu.HBM)] * len(inputs),
        out_specs=(VMEM,) * 2,
        scratch_shapes=held + [pltpu.SemaphoreType.DMA((len(inputs),))],
        compiler_params=LARGE,
    )(*inputs)
    received = lax.ppermute(sent, axes, across_cores)
    near_small, near = pl.pallas_call(
        near_kernel,
        out_shape=(f32(2, STRIP, LANES), f32(HEIGHT, STRIP, LANES)),
        in_specs=[VMEM] * 2,
        out_specs=(VMEM,) * 2,
        compiler_params=PARAMS,
    )(kept, received)
    halo_small = lax.ppermute(near_small, axes, across_halves)
    halo_small, near = lax.optimization_barrier((halo_small, near))
    halo = lax.ppermute(near, axes, across_halves)
    z, aux, inter, intra, counts = pl.pallas_call(
        begin_kernel,
        out_shape=(
            f32(TILES, EXT, LANES),
            f32(TILES, BINS, LANES),
            f32(TILES, STRIP, LANES),
            f32(TILES, STRIP, LANES),
            f32(lon_count, 1, LANES),
        ),
        in_specs=[VMEM] * 3,
        out_specs=(VMEM,) * 5,
        compiler_params=PARAMS,
    )(kept, received, halo_small)
    weight = lax.all_to_all(counts, "lon", 0, 0)
    inter, intra = exchange(inter, intra)
    tables = constants()
    alt = aux
    for iteration in range(ITERS):
        first = iteration == 0
        shapes = [f32(TILES, EXT, LANES), f32(TILES, STRIP, LANES), f32(TILES, STRIP, LANES)]
        if first:
            shapes += [f32(TILES, BINS, LANES), f32(BINS, LANES)]
        out = pl.pallas_call(
            functools.partial(step_kernel, first),
            out_shape=tuple(shapes),
            in_specs=[SMEM] + [VMEM] * 14,
            out_specs=(VMEM,) * len(shapes),
            scratch_shapes=[pltpu.VMEM((TILES * STRIP, LANES), F32)] * 4,
            compiler_params=PARAMS,
        )(coef, kept, received, halo, z, inter, intra, aux, alt, weight, *tables)
        z, inter, intra = out[:3]
        if first:
            alt, weight = out[3:]
        inter, intra = exchange(inter, intra)
    mine, other = pl.pallas_call(
        end_kernel,
        out_shape=(f32(STRIP, 2 * LANES),) * 2,
        in_specs=[VMEM] * 3,
        out_specs=(VMEM,) * 2,
        compiler_params=PARAMS,
    )(z, inter, intra)
    other = lax.ppermute(other, axes, across_cores)
    return pl.pallas_call(
        place_kernel,
        out_shape=f32(2 * STRIP, 2 * LANES),
        in_specs=[VMEM] * 2,
        out_specs=VMEM,
        compiler_params=PARAMS,
    )(mine, other)


def solution(mesh):
    return jax.shard_map(
        per_device,
        mesh=mesh,
        in_specs=(
            P("lon", "lat"),
            P("lon", "lat"),
            P(None, "lon", "lat"),
            P(None, "lon", "lat"),
            P(None, "lon", "lat"),
            P(),
            P("lon", "lat"),
            P("lon", "lat"),
        ),
        out_specs=P("lon", "lat"),
        check_vma=False,
    )
```

```python
import jax
import jax.numpy as jnp
import numpy as np
from jax import lax
from jax.experimental import pallas as pl
from jax.experimental.pallas import tpu as pltpu
from jax.sharding import PartitionSpec as P

IMAGES = 12
RAD = 16
OWN = 4
ITERS = 3
ROWS = 4096
COLUMNS = 1024
STEP_SIZE = 0.05
ALT_WEIGHT = 64.0
DATA_GAIN = 160.0
LUNAR_MIX = 0.6
SHARPNESS = 20.0

LANES = 128
STRIP = 32
EXT = STRIP + 2 * RAD
TILES = 5
FIELDS = 2 * IMAGES + 3
ALBEDO = 2 * IMAGES
HEIGHT = ALBEDO + 1
AUX = HEIGHT + 1
BINS = 16
DENOM = float(RAD * (RAD + 1) * (2 * RAD + 1)) / 3.0
TAP_SCALE = 1.0 / (DENOM * (2 * RAD + 1))
F32 = jnp.float32
BF16 = jnp.bfloat16
VMEM = pl.BlockSpec(memory_space=pltpu.VMEM)
SMEM = pl.BlockSpec(memory_space=pltpu.SMEM)
PARAMS = pltpu.CompilerParams(vmem_limit_bytes=24 * 2**20)
LARGE = pltpu.CompilerParams(vmem_limit_bytes=58 * 2**20)


def band(offset, derivative):
    inside = np.abs(offset) <= RAD
    return np.where(inside, offset if derivative else 1, 0).astype(np.float32)


def constants():
    own = np.arange(STRIP)
    ext = np.arange(EXT) - RAD
    reach = ext[None, :] - own[:, None]
    rows = [band(reach, True), band(reach, False)]
    bins = np.arange(BINS)
    for shift in range(OWN):
        group = (ext[None, :] + shift) // OWN
        rows.append((group == bins[:, None]).astype(np.float32))
    down = np.concatenate(rows, axis=0)
    forward = np.concatenate([down] * 3, axis=1)
    back = own[None, :] - ext[:, None]
    spread = np.zeros((EXT, OWN * BINS), np.float32)
    for shift in range(OWN):
        hit = ((own[:, None] + shift) // OWN) == bins[None, :]
        spread[RAD : RAD + STRIP, shift * BINS : (shift + 1) * BINS] = hit
    filters = np.concatenate([band(back, True), band(back, False)], axis=1)
    backward = np.concatenate([filters, filters, spread, spread], axis=1)
    lane = np.arange(LANES)
    side = np.where(lane < LANES // 2, lane + LANES, lane - LANES)
    source = np.concatenate([lane, side])
    across = source[:, None] - lane[None, :]
    quads = (lane[:, None] // OWN == lane[None, :] // OWN).astype(np.float32)
    return [
        jnp.asarray(m, BF16)
        for m in (forward, backward, band(across, False), band(across, True), quads)
    ]


def pieces(value, count):
    out = []
    for _ in range(count - 1):
        part = value.astype(BF16)
        value = value - part.astype(F32)
        out.append(part)
    out.append(value.astype(BF16))
    return out


def dot(left, right):
    return jnp.dot(left, right, preferred_element_type=F32)


def with_sides(tiles):
    low = lax.broadcasted_iota(jnp.int32, tiles[0].shape, 1) < LANES // 2
    zero = jnp.zeros_like(tiles[0])
    rows = []
    for j, tile in enumerate(tiles):
        after = tiles[j + 1] if j + 1 < len(tiles) else zero
        before = tiles[j - 1] if j > 0 else zero
        rows.append(jnp.concatenate([tile, jnp.where(low, after, before)], axis=1))
    return jnp.concatenate(rows, axis=0)


def filter_lat(tiles, taps, count):
    total = None
    for part in pieces(with_sides(tiles), count):
        term = dot(part, taps)
        total = term if total is None else total + term
    return total


def place():
    lat = lax.axis_index("lat")
    return lat // 2, lat % 2


def own_tile(half, core, t):
    return half + 2 * core + t


def aux_fields(ref, rows_of, owner, altimetry, count, expand):
    bins = owner[0:OWN, :] - lax.axis_index("lon") * BINS
    shift = jnp.sum(bins, axis=0, keepdims=True).astype(F32)
    heights = dot(jnp.concatenate(pieces(altimetry[...], 3), axis=1), expand[...])
    heights = jnp.where(rows_of == 0, heights[0:8], heights[8:16])
    lit = jnp.concatenate([count[...].astype(F32), jnp.zeros((1, LANES - IMAGES), F32)], axis=1)
    for t in range(2):
        lanes = slice(t * LANES, (t + 1) * LANES)
        ref[AUX, t, 0:8] = heights[:, lanes]
        ref[AUX, t, 8:16] = jnp.broadcast_to(shift[:, lanes], (8, LANES))
        ref[AUX, t, 16:24] = jnp.broadcast_to(lit, (8, LANES))
        ref[AUX, t, 24:32] = jnp.zeros((8, LANES), F32)


def send_kernel(
    images_hbm, mask_hbm, height_hbm, albedo_hbm, owner_hbm, altimetry_hbm, count_hbm, expand_hbm,
    sent,
    images, lit_mask, height, albedo, owner, altimetry, count, expand, sems,
):
    other = 1 - place()[1]
    rows = pl.ds(pl.multiple_of(other * STRIP, STRIP), STRIP)
    copies = [
        pltpu.make_async_copy(source, target, sems.at[i])
        for i, (source, target) in enumerate(
            (
                (images_hbm.at[:, rows], images),
                (mask_hbm.at[:, rows], lit_mask),
                (height_hbm.at[rows], height),
                (albedo_hbm.at[rows], albedo),
                (owner_hbm.at[pl.ds(0, 8)], owner),
                (altimetry_hbm, altimetry),
                (count_hbm, count),
                (expand_hbm, expand),
            )
        )
    ]
    for copy in copies:
        copy.start()
    for copy in copies:
        copy.wait()
    aux_fields(sent, other, owner, altimetry, count, expand)
    for t in range(2):
        cols = pl.ds(t * LANES, LANES)
        for k in range(IMAGES):
            sent[k, t] = images[k, :, cols].astype(F32)
            sent[IMAGES + k, t] = lit_mask[k, :, cols].astype(F32)
        sent[ALBEDO, t] = albedo[:, cols]
        sent[HEIGHT, t] = height[:, cols]


def keep_kernel(images, lit_mask, height, albedo, owner, altimetry, count, expand, sent, kept):
    core = place()[1]
    rows = pl.ds(pl.multiple_of(core * STRIP, STRIP), STRIP)
    aux_fields(kept, core, owner, altimetry, count, expand)
    for t in range(2):
        cols = pl.ds(t * LANES, LANES)
        for k in range(IMAGES):
            kept[k, t] = images[k, rows, cols].astype(F32)
            kept[IMAGES + k, t] = lit_mask[k, rows, cols].astype(F32)
        kept[ALBEDO, t] = albedo[rows, cols]
        kept[HEIGHT, t] = height[rows, cols]


def near_small_kernel(kept, received, near_small):
    half, core = place()
    for i, field in enumerate((HEIGHT, AUX)):
        near_small[i] = jnp.where(half != core, kept[field, 1 - half], received[field, 1 - half])


def near_kernel(kept, received, near_small, near):
    half, core = place()

    @pl.when(half != core)
    def _():
        near[...] = kept[0:HEIGHT, 1 - half]

    @pl.when(half == core)
    def _():
        near[...] = received[0:HEIGHT, 1 - half]


def count_kernel(kept, received, near, counts):
    total = kept[0, 0, 16:17] + received[0, 0, 16:17]
    counts[...] = jnp.broadcast_to(total[None], counts.shape)


def route(core, up, down, inter, intra):
    inter[...] = jnp.where(core == 0, up, down)
    intra[...] = jnp.where(core == 0, down, up)


def begin_kernel(kept, received, halo_small, z, aux, inter, intra):
    half, core = place()
    zero = jnp.zeros((TILES, RAD, LANES), F32)
    z[:, 0:RAD] = zero
    z[:, RAD + STRIP : EXT] = zero
    for t in range(2):
        for ref, at in ((kept, own_tile(half, core, t)), (received, own_tile(half, 1 - core, t))):
            z[at, RAD : RAD + STRIP] = ref[HEIGHT, t]
            aux[at] = ref[AUX, t, 0:BINS]
    far = (TILES - 1) * (1 - half)
    z[far, RAD : RAD + STRIP] = halo_small[0]
    aux[far] = halo_small[1, 0:BINS]
    alt = jnp.concatenate([aux[:, 0:8], jnp.zeros((TILES, 8, LANES), F32)], axis=1)
    up = jnp.concatenate([alt, z[:, RAD : 2 * RAD]], axis=1)
    route(core, up, z[:, STRIP:EXT], inter, intra)


def image_weights(counts):
    total = jnp.sum(counts[...], axis=0)
    weight = 2.0 * DATA_GAIN * float(ROWS * COLUMNS) / total
    image = lax.broadcasted_iota(jnp.int32, (BINS, LANES), 0)
    lane = lax.broadcasted_iota(jnp.int32, (BINS, LANES), 1)
    diagonal = jnp.where((image == lane) & (image < IMAGES), weight, 0.0)
    ones = jnp.ones((LANES, LANES), BF16)
    first, second, third = pieces(diagonal, 3)
    return dot(first, ones) + dot(second, ones) + dot(third, ones)


def inverse_of(value):
    guess = pl.reciprocal(value, approx=True)
    return guess * (2.0 - value * guess)


def image_term(coef, k, observed, lit, flat_part, flat_shade, mix_shade, slope_lon, slope_lat):
    steep = coef[k, 2] - coef[k, 0] * slope_lon - coef[k, 1] * slope_lat
    decay = jnp.exp(-jnp.abs(steep))
    whole = 1.0 + decay
    part = jnp.maximum(steep, 0.0) + jnp.log(whole)
    level = part + coef[k, 3]
    both = inverse_of(whole * level)
    ratio = both * whole
    gate = jnp.where(steep >= 0.0, 1.0, decay) * (both * level)
    residual = lit * (part * (mix_shade * ratio + flat_shade) - observed)
    pull = residual * ((coef[k, 4] * (ratio * ratio) + flat_part) * gate)
    return pull, residual * part


def shades(albedo, slope_lon, slope_lat):
    inverse = lax.rsqrt(1.0 + slope_lon * slope_lon + slope_lat * slope_lat)
    flat_part = (1.0 - LUNAR_MIX) * inverse
    return inverse, (flat_part, flat_part * (albedo * (1.0 / SHARPNESS)), albedo * LUNAR_MIX)


def gradients(albedo, inverse, slope_lon, slope_lat, sums):
    sum_lon, sum_lat, sum_norm = sums
    bend = (1.0 - LUNAR_MIX) / SHARPNESS * (inverse * inverse * inverse) * sum_norm
    return albedo * (sum_lon - slope_lon * bend), albedo * (sum_lat - slope_lat * bend)


def add_image(sums, coef, k, pull, norm):
    terms = (coef[k, 5] * pull, coef[k, 6] * pull, norm)
    return terms if sums is None else tuple(a + b for a, b in zip(sums, terms))


def tile_rows(at):
    return pl.ds(pl.multiple_of(at * STRIP, STRIP), STRIP)


def image_tiles(kept, received, halo):
    half, core = place()
    for t in range(2):
        yield kept, (t,), tile_rows(own_tile(half, core, t))
        yield received, (t,), tile_rows(own_tile(half, 1 - core, t))
    yield halo, (), tile_rows((TILES - 1) * (1 - half))


def shift_rows(aux, j):
    return jnp.concatenate([aux[j, 8:16]] * 2, axis=0)


def slopes_and_misfit(surface, aux, alt, tables, slope_lon, slope_lat):
    forward, backward, smooth, slope, quads = tables
    tiles = range(TILES)
    stacked = jnp.concatenate(
        [jnp.concatenate(pieces(surface[j], 3), axis=0) for j in tiles], axis=1
    )
    down = dot(forward[...], stacked)

    def part(row, count, j):
        return down[row : row + count, j * LANES : (j + 1) * LANES]

    slope_lon[...] = TAP_SCALE * filter_lat([part(0, STRIP, j) for j in tiles], smooth[...], 3)
    slope_lat[...] = TAP_SCALE * filter_lat([part(STRIP, STRIP, j) for j in tiles], slope[...], 3)
    sums = []
    for j in tiles:
        shift = shift_rows(aux, j)
        chosen = part(2 * STRIP, BINS, j)
        for s in range(1, OWN):
            chosen = jnp.where(shift == float(s), part(2 * STRIP + s * BINS, BINS, j), chosen)
        sums.append(chosen)
    owner_sum = None
    for p in pieces(jnp.concatenate(sums, axis=0), 3):
        term = dot(p, quads[...])
        owner_sum = term if owner_sum is None else owner_sum + term
    gain = STEP_SIZE * 2.0 * ALT_WEIGHT / (OWN * OWN)
    rows = [slice(j * BINS, (j + 1) * BINS) for j in tiles]
    return [gain * alt[j] - (gain / (OWN * OWN)) * owner_sum[rows[j]] for j in tiles]


def contribute(surface, aux, misfit, grad_lon, grad_lat, tables, z_out, inter_out, intra_out):
    forward, backward, smooth, slope, quads = tables
    tiles = range(TILES)

    def field(ref):
        return [ref[j * STRIP : (j + 1) * STRIP] for j in tiles]

    scale = STEP_SIZE * TAP_SCALE
    from_lon = scale * filter_lat(field(grad_lon), smooth[...], 2)
    from_lat = scale * filter_lat(field(grad_lat), slope[...], 2)
    columns = []
    for j in tiles:
        rows = slice(j * STRIP, (j + 1) * STRIP)
        data = pieces(jnp.concatenate([from_lon[rows], from_lat[rows]], axis=0), 2)
        shift = shift_rows(aux, j)
        pull = [jnp.where(shift == float(s), misfit[j], 0.0) for s in range(OWN)]
        columns.append(jnp.concatenate(data + pieces(jnp.concatenate(pull, axis=0), 2), axis=0))
    spread = dot(backward[...], jnp.concatenate(columns, axis=1))
    for j in tiles:
        change = spread[:, j * LANES : (j + 1) * LANES]
        z_out[j, 0:RAD] = change[0:RAD]
        z_out[j, RAD : RAD + STRIP] = change[RAD : RAD + STRIP] + surface[j][RAD : RAD + STRIP]
        z_out[j, RAD + STRIP : EXT] = change[RAD + STRIP : EXT]
    core = place()[1]
    route(core, z_out[:, 0:STRIP], z_out[:, STRIP:EXT], inter_out, intra_out)


def arrived(inter, intra):
    core = place()[1]
    return (
        jnp.where(core == 0, inter[...], intra[...]),
        jnp.where(core == 0, intra[...], inter[...]),
    )


def surface_step(
    coef, weight, kept, received, halo, surface, aux, alt, tables, z_out, inter_out, intra_out, fields
):
    slope_lon, slope_lat, grad_lon, grad_lat = fields
    misfit = slopes_and_misfit(surface, aux, alt, tables, slope_lon, slope_lat)
    for ref, index, rows in image_tiles(kept, received, halo):
        albedo, lon, lat = ref[(ALBEDO, *index)], slope_lon[rows], slope_lat[rows]
        inverse, shade = shades(albedo, lon, lat)
        sums = None
        for k in range(IMAGES):
            lit = weight[k : k + 1] * ref[(IMAGES + k, *index)]
            pull, norm = image_term(coef, k, ref[(k, *index)], lit, *shade, lon, lat)
            sums = add_image(sums, coef, k, pull, norm)
        grad_lon[rows], grad_lat[rows] = gradients(albedo, inverse, lon, lat, sums)
    contribute(surface, aux, misfit, grad_lon, grad_lat, tables, z_out, inter_out, intra_out)


def first_kernel(coef, counts, kept, received, halo, z, inter, intra, aux, *refs):
    tables, (z_out, inter_out, intra_out, alt_out, weight_out), fields = refs[:5], refs[5:10], refs[10:]
    weight = image_weights(counts)
    weight_out[...] = weight
    above, below = arrived(inter, intra)
    alt = jnp.concatenate([aux[:, 0:8], below[:, 0:8]], axis=1)
    alt_out[...] = alt
    below = jnp.concatenate([jnp.zeros((TILES, RAD, LANES), F32), below[:, RAD:]], axis=1)
    surface = [z[j] + jnp.concatenate([above[j], below[j]], axis=0) for j in range(TILES)]
    surface_step(
        coef, weight, kept, received, halo, surface, aux, alt, tables, z_out, inter_out, intra_out, fields
    )


def step_kernel(coef, weight, kept, received, halo, z, inter, intra, aux, alt, *refs):
    tables, (z_out, inter_out, intra_out), fields = refs[:5], refs[5:8], refs[8:]
    above, below = arrived(inter, intra)
    surface = [z[j] + jnp.concatenate([above[j], below[j]], axis=0) for j in range(TILES)]
    surface_step(
        coef, weight[...], kept, received, halo, surface, aux, alt, tables, z_out, inter_out, intra_out, fields
    )


def end_kernel(z, inter, intra, kept, sent):
    half, core = place()
    for ref, side in ((kept, core), (sent, 1 - core)):
        for t in range(2):
            at = own_tile(half, side, t)
            above = jnp.where(core == 0, inter[at], intra[at])
            below = jnp.where(core == 0, intra[at], inter[at])
            cols = slice(t * LANES, (t + 1) * LANES)
            ref[0:RAD, cols] = z[at, RAD : 2 * RAD] + above[RAD:]
            ref[RAD:STRIP, cols] = z[at, 2 * RAD : RAD + STRIP] + below[0:RAD]


def place_kernel(mine, other, out):
    core = place()[1]
    out[pl.ds(pl.multiple_of(core * STRIP, STRIP), STRIP)] = mine[...]
    out[pl.ds(pl.multiple_of((1 - core) * STRIP, STRIP), STRIP)] = other[...]


def f32(*shape):
    return jax.ShapeDtypeStruct(shape, F32)


def call(kernel, out_shape, *args, scratch=()):
    scalars = kernel in (first_kernel, step_kernel)
    return pl.pallas_call(
        kernel,
        out_shape=out_shape,
        in_specs=[SMEM if scalars and i == 0 else VMEM for i in range(len(args))],
        out_specs=jax.tree.map(lambda _: VMEM, out_shape),
        scratch_shapes=list(scratch),
        compiler_params=PARAMS,
    )(*args)


def per_device(height, albedo, images, lit_mask, lit_count, geometry, owner_column, altimetry):
    lon_count, lat_count = lax.axis_size("lon"), lax.axis_size("lat")
    axes = ("lon", "lat")
    sites = [(a, b) for a in range(lon_count) for b in range(lat_count)]

    def index(a, b):
        return (a % lon_count) * lat_count + b

    across_cores = [(index(a, b), index(a, b ^ 1)) for a, b in sites]
    across_halves = [(index(a, b), index(a, b ^ 2)) for a, b in sites]
    across_strips = [(index(a, b), index(a + 2 * (b % 2) - 1, b ^ 1)) for a, b in sites]

    def exchange(inter, intra):
        return lax.ppermute(inter, axes, across_strips), lax.ppermute(intra, axes, across_cores)

    sun_lon, sun_lat, sun_up, view = (geometry[:, i] for i in range(4))
    coef = jnp.stack(
        [
            SHARPNESS * sun_lon,
            SHARPNESS * sun_lat,
            SHARPNESS * sun_up,
            SHARPNESS * view,
            (LUNAR_MIX * SHARPNESS * SHARPNESS) * view,
            -sun_lon,
            -sun_lat,
        ],
        axis=1,
    )

    expand = np.arange(altimetry.shape[1])[:, None] == np.arange(2 * LANES)[None, :] // OWN
    expand = jnp.asarray(np.concatenate([expand] * 3, axis=0), BF16)
    count = lit_count.reshape(1, IMAGES)
    inputs = (images, lit_mask, height, albedo, owner_column, altimetry, count, expand)
    cut = [(IMAGES, STRIP, 2 * LANES)] * 2 + [(STRIP, 2 * LANES)] * 2 + [(8, 2 * LANES)]
    cut += [a.shape for a in inputs[len(cut) :]]
    fields = f32(FIELDS, 2, STRIP, LANES)
    sent = pl.pallas_call(
        send_kernel,
        out_shape=fields,
        in_specs=[pl.BlockSpec(memory_space=pltpu.HBM)] * len(inputs),
        out_specs=VMEM,
        scratch_shapes=[pltpu.VMEM(shape, a.dtype) for shape, a in zip(cut, inputs)]
        + [pltpu.SemaphoreType.DMA((len(inputs),))],
        compiler_params=LARGE,
    )(*inputs)
    received = lax.ppermute(sent, axes, across_cores)
    kept = call(keep_kernel, fields, *inputs, sent[:1, :1, :8])
    near_small = call(near_small_kernel, f32(2, STRIP, LANES), kept, received)
    halo_small = lax.ppermute(near_small, axes, across_halves)
    near = call(near_kernel, f32(HEIGHT, STRIP, LANES), kept, received, near_small)
    halo = lax.ppermute(near, axes, across_halves)
    counts = call(
        count_kernel, f32(len(sites) // 2, 1, LANES), kept[AUX:], received[AUX:], near[:1, :8]
    )
    same_core = [[index(a, b) for a, b in sites if b % 2 == core] for core in range(2)]
    counts = lax.all_to_all(counts, axes, 0, 0, axis_index_groups=same_core)
    message = f32(TILES, STRIP, LANES)
    window = f32(TILES, EXT, LANES)
    rows_of_bins = f32(TILES, BINS, LANES)
    z, aux, inter, intra = call(
        begin_kernel, (window, rows_of_bins, message, message), kept, received, halo_small
    )
    inter, intra = exchange(inter, intra)
    tables = constants()
    scratch = [pltpu.VMEM((TILES * STRIP, LANES), F32)] * 4
    z, inter, intra, alt, weight = call(
        first_kernel,
        (window, message, message, rows_of_bins, f32(BINS, LANES)),
        coef, counts, kept, received, halo, z, inter, intra, aux, *tables,
        scratch=scratch,
    )
    for _ in range(ITERS - 1):
        inter, intra = exchange(inter, intra)
        z, inter, intra = call(
            step_kernel,
            (window, message, message),
            coef, weight, kept, received, halo, z, inter, intra, aux, alt, *tables,
            scratch=scratch,
        )
    inter, intra = exchange(inter, intra)
    half_out = f32(STRIP, 2 * LANES)
    mine, other = call(end_kernel, (half_out, half_out), z, inter, intra)
    other = lax.ppermute(other, axes, across_cores)
    return call(place_kernel, f32(2 * STRIP, 2 * LANES), mine, other)


def solution(mesh):
    return jax.shard_map(
        per_device,
        mesh=mesh,
        in_specs=(
            P("lon", "lat"),
            P("lon", "lat"),
            P(None, "lon", "lat"),
            P(None, "lon", "lat"),
            P(None, "lon", "lat"),
            P(),
            P("lon", "lat"),
            P("lon", "lat"),
        ),
        out_specs=P("lon", "lat"),
        check_vma=False,
    )
```

```python
import jax
import jax.numpy as jnp
import numpy as np
from jax import lax
from jax.experimental import pallas as pl
from jax.experimental.pallas import tpu as pltpu
from jax.sharding import PartitionSpec as P

IMAGES = 12
RAD = 16
OWN = 4
ITERS = 3
ROWS = 4096
COLUMNS = 1024
STEP_SIZE = 0.05
ALT_WEIGHT = 64.0
DATA_GAIN = 160.0
LUNAR_MIX = 0.6
SHARPNESS = 20.0

LANES = 128
STRIP = 32
EXT = STRIP + 2 * RAD
TILES = 5
FIELDS = 2 * IMAGES + 3
ALBEDO = 2 * IMAGES
HEIGHT = ALBEDO + 1
AUX = HEIGHT + 1
BINS = 16
LINE = 8
DENOM = float(RAD * (RAD + 1) * (2 * RAD + 1)) / 3.0
TAP_SCALE = 1.0 / (DENOM * (2 * RAD + 1))
F32 = jnp.float32
BF16 = jnp.bfloat16
VMEM = pl.BlockSpec(memory_space=pltpu.VMEM)
SMEM = pl.BlockSpec(memory_space=pltpu.SMEM)
PARAMS = pltpu.CompilerParams(vmem_limit_bytes=24 * 2**20)
LARGE = pltpu.CompilerParams(vmem_limit_bytes=58 * 2**20)


def band(offset, derivative):
    inside = np.abs(offset) <= RAD
    return np.where(inside, offset if derivative else 1, 0).astype(np.float32)


def constants():
    own = np.arange(STRIP)
    ext = np.arange(EXT) - RAD
    reach = ext[None, :] - own[:, None]
    rows = [band(reach, True), band(reach, False)]
    bins = np.arange(BINS)
    for shift in range(OWN):
        group = (ext[None, :] + shift) // OWN
        rows.append((group == bins[:, None]).astype(np.float32))
    down = np.concatenate(rows, axis=0)
    forward = np.concatenate([down] * 3, axis=1)
    back = own[None, :] - ext[:, None]
    spread = np.zeros((EXT, OWN * BINS), np.float32)
    for shift in range(OWN):
        hit = ((own[:, None] + shift) // OWN) == bins[None, :]
        spread[RAD : RAD + STRIP, shift * BINS : (shift + 1) * BINS] = hit
    filters = np.concatenate([band(back, True), band(back, False)], axis=1)
    backward = np.concatenate([filters, filters, spread, spread], axis=1)
    lane = np.arange(LANES)
    side = np.where(lane < LANES // 2, lane + LANES, lane - LANES)
    source = np.concatenate([lane, side])
    across = source[:, None] - lane[None, :]
    quads = (lane[:, None] // OWN == lane[None, :] // OWN).astype(np.float32)
    return [
        jnp.asarray(m, BF16)
        for m in (forward, backward, band(across, False), band(across, True), quads)
    ]


def pieces(value, count):
    out = []
    for _ in range(count - 1):
        part = value.astype(BF16)
        value = value - part.astype(F32)
        out.append(part)
    out.append(value.astype(BF16))
    return out


def dot(left, right):
    return jnp.dot(left, right, preferred_element_type=F32)


def with_sides(tiles):
    low = lax.broadcasted_iota(jnp.int32, tiles[0].shape, 1) < LANES // 2
    zero = jnp.zeros_like(tiles[0])
    rows = []
    for j, tile in enumerate(tiles):
        after = tiles[j + 1] if j + 1 < len(tiles) else zero
        before = tiles[j - 1] if j > 0 else zero
        rows.append(jnp.concatenate([tile, jnp.where(low, after, before)], axis=1))
    return jnp.concatenate(rows, axis=0)


def filter_lat(tiles, taps, count):
    total = None
    for part in pieces(with_sides(tiles), count):
        term = dot(part, taps)
        total = term if total is None else total + term
    return total


def place():
    lat = lax.axis_index("lat")
    return lat // 2, lat % 2


def own_tile(half, core, t):
    return half + 2 * core + t


def aux_fields(ref, rows_of, owner, altimetry, count, expand):
    bins = owner[0:OWN, :] - lax.axis_index("lon") * BINS
    shift = jnp.sum(bins, axis=0, keepdims=True).astype(F32)
    heights = dot(jnp.concatenate(pieces(altimetry[...], 3), axis=1), expand[...])
    heights = jnp.where(rows_of == 0, heights[0:8], heights[8:16])
    lit = jnp.concatenate([count[...].astype(F32), jnp.zeros((1, LANES - IMAGES), F32)], axis=1)
    for t in range(2):
        lanes = slice(t * LANES, (t + 1) * LANES)
        ref[AUX, t, 0:8] = heights[:, lanes]
        ref[AUX, t, 8:16] = jnp.broadcast_to(shift[:, lanes], (8, LANES))
        ref[AUX, t, 16:24] = jnp.broadcast_to(lit, (8, LANES))
        ref[AUX, t, 24:32] = jnp.zeros((8, LANES), F32)


def send_kernel(
    images_hbm, mask_hbm, height_hbm, albedo_hbm, owner_hbm, altimetry_hbm, count_hbm, expand_hbm,
    sent,
    images, lit_mask, height, albedo, owner, altimetry, count, expand, sems,
):
    other = 1 - place()[1]
    rows = pl.ds(pl.multiple_of(other * STRIP, STRIP), STRIP)
    copies = [
        pltpu.make_async_copy(source, target, sems.at[i])
        for i, (source, target) in enumerate(
            (
                (images_hbm.at[:, rows], images),
                (mask_hbm.at[:, rows], lit_mask),
                (height_hbm.at[rows], height),
                (albedo_hbm.at[rows], albedo),
                (owner_hbm.at[pl.ds(0, 8)], owner),
                (altimetry_hbm, altimetry),
                (count_hbm, count),
                (expand_hbm, expand),
            )
        )
    ]
    for copy in copies:
        copy.start()
    for copy in copies:
        copy.wait()
    aux_fields(sent, other, owner, altimetry, count, expand)
    for t in range(2):
        cols = pl.ds(t * LANES, LANES)
        for k in range(IMAGES):
            sent[k, t] = images[k, :, cols].astype(F32)
            sent[IMAGES + k, t] = lit_mask[k, :, cols].astype(F32)
        sent[ALBEDO, t] = albedo[:, cols]
        sent[HEIGHT, t] = height[:, cols]


def keep_kernel(images, lit_mask, height, albedo, owner, altimetry, count, expand, kept):
    core = place()[1]
    rows = pl.ds(pl.multiple_of(core * STRIP, STRIP), STRIP)
    aux_fields(kept, core, owner, altimetry, count, expand)
    for t in range(2):
        cols = pl.ds(t * LANES, LANES)
        for k in range(IMAGES):
            kept[k, t] = images[k, rows, cols].astype(F32)
            kept[IMAGES + k, t] = lit_mask[k, rows, cols].astype(F32)
        kept[ALBEDO, t] = albedo[rows, cols]
        kept[HEIGHT, t] = height[rows, cols]


def near_small_kernel(kept, received, near_small):
    half, core = place()
    for i, field in enumerate((HEIGHT, AUX)):
        near_small[i] = jnp.where(half != core, kept[field, 1 - half], received[field, 1 - half])


def near_kernel(kept, received, near_small, near):
    half, core = place()

    @pl.when(half != core)
    def _():
        near[...] = kept[0:HEIGHT, 1 - half]

    @pl.when(half == core)
    def _():
        near[...] = received[0:HEIGHT, 1 - half]


def count_kernel(kept, received, near_small, counts):
    total = kept[AUX, 0, 16:17] + received[AUX, 0, 16:17]
    counts[...] = jnp.broadcast_to(total[None], counts.shape)


def line_kernel(line, inter, counts):
    counts[...] = jnp.broadcast_to(jnp.sum(line[...], axis=0, keepdims=True), counts.shape)


def route(core, up, down, inter, intra):
    inter[...] = jnp.where(core == 0, up, down)
    intra[...] = jnp.where(core == 0, down, up)


def begin_kernel(kept, received, halo_small, z, aux, inter, intra):
    half, core = place()
    zero = jnp.zeros((TILES, RAD, LANES), F32)
    z[:, 0:RAD] = zero
    z[:, RAD + STRIP : EXT] = zero
    for t in range(2):
        for ref, at in ((kept, own_tile(half, core, t)), (received, own_tile(half, 1 - core, t))):
            z[at, RAD : RAD + STRIP] = ref[HEIGHT, t]
            aux[at] = ref[AUX, t, 0:BINS]
    far = (TILES - 1) * (1 - half)
    z[far, RAD : RAD + STRIP] = halo_small[0]
    aux[far] = halo_small[1, 0:BINS]
    alt = jnp.concatenate([aux[:, 0:8], jnp.zeros((TILES, 8, LANES), F32)], axis=1)
    up = jnp.concatenate([alt, z[:, RAD : 2 * RAD]], axis=1)
    route(core, up, z[:, STRIP:EXT], inter, intra)


def image_weights(counts):
    total = jnp.sum(counts[...], axis=0)
    weight = 2.0 * DATA_GAIN * float(ROWS * COLUMNS) / total
    image = lax.broadcasted_iota(jnp.int32, (BINS, LANES), 0)
    lane = lax.broadcasted_iota(jnp.int32, (BINS, LANES), 1)
    diagonal = jnp.where((image == lane) & (image < IMAGES), weight, 0.0)
    ones = jnp.ones((LANES, LANES), BF16)
    first, second, third = pieces(diagonal, 3)
    return dot(first, ones) + dot(second, ones) + dot(third, ones)


def image_term(coef, k, observed, lit, flat_part, flat_shade, mix_shade, slope_lon, slope_lat):
    steep = coef[k, 2] - coef[k, 0] * slope_lon - coef[k, 1] * slope_lat
    decay = jnp.exp(-jnp.abs(steep))
    whole = 1.0 + decay
    part = jnp.maximum(steep, 0.0) + jnp.log(whole)
    ratio = 1.0 / (part + coef[k, 3])
    gate = jnp.where(steep >= 0.0, 1.0, decay) / whole
    residual = lit * (part * (mix_shade * ratio + flat_shade) - observed)
    pull = residual * ((coef[k, 4] * (ratio * ratio) + flat_part) * gate)
    return pull, residual * part


def shades(albedo, slope_lon, slope_lat):
    inverse = lax.rsqrt(1.0 + slope_lon * slope_lon + slope_lat * slope_lat)
    flat_part = (1.0 - LUNAR_MIX) * inverse
    return inverse, (flat_part, flat_part * (albedo * (1.0 / SHARPNESS)), albedo * LUNAR_MIX)


def gradients(albedo, inverse, slope_lon, slope_lat, sums):
    sum_lon, sum_lat, sum_norm = sums
    bend = (1.0 - LUNAR_MIX) / SHARPNESS * (inverse * inverse * inverse) * sum_norm
    return albedo * (sum_lon - slope_lon * bend), albedo * (sum_lat - slope_lat * bend)


def add_image(sums, coef, k, pull, norm):
    terms = (coef[k, 5] * pull, coef[k, 6] * pull, norm)
    return terms if sums is None else tuple(a + b for a, b in zip(sums, terms))


def tile_rows(at):
    return pl.ds(pl.multiple_of(at * STRIP, STRIP), STRIP)


def image_tiles(kept, received, halo):
    half, core = place()
    for t in range(2):
        yield kept, (t,), tile_rows(own_tile(half, core, t))
        yield received, (t,), tile_rows(own_tile(half, 1 - core, t))
    yield halo, (), tile_rows((TILES - 1) * (1 - half))


def shift_rows(aux, j):
    return jnp.concatenate([aux[j, 8:16]] * 2, axis=0)


def slopes_and_misfit(surface, aux, alt, tables, slope_lon, slope_lat):
    forward, backward, smooth, slope, quads = tables
    tiles = range(TILES)
    stacked = jnp.concatenate(
        [jnp.concatenate(pieces(surface[j], 3), axis=0) for j in tiles], axis=1
    )
    down = dot(forward[...], stacked)

    def part(row, count, j):
        return down[row : row + count, j * LANES : (j + 1) * LANES]

    slope_lon[...] = TAP_SCALE * filter_lat([part(0, STRIP, j) for j in tiles], smooth[...], 3)
    slope_lat[...] = TAP_SCALE * filter_lat([part(STRIP, STRIP, j) for j in tiles], slope[...], 3)
    sums = []
    for j in tiles:
        shift = shift_rows(aux, j)
        chosen = part(2 * STRIP, BINS, j)
        for s in range(1, OWN):
            chosen = jnp.where(shift == float(s), part(2 * STRIP + s * BINS, BINS, j), chosen)
        sums.append(chosen)
    owner_sum = None
    for p in pieces(jnp.concatenate(sums, axis=0), 3):
        term = dot(p, quads[...])
        owner_sum = term if owner_sum is None else owner_sum + term
    gain = STEP_SIZE * 2.0 * ALT_WEIGHT / (OWN * OWN)
    rows = [slice(j * BINS, (j + 1) * BINS) for j in tiles]
    return [gain * alt[j] - (gain / (OWN * OWN)) * owner_sum[rows[j]] for j in tiles]


def contribute(surface, aux, misfit, grad_lon, grad_lat, tables, z_out, inter_out, intra_out):
    forward, backward, smooth, slope, quads = tables
    tiles = range(TILES)

    def field(ref):
        return [ref[j * STRIP : (j + 1) * STRIP] for j in tiles]

    scale = STEP_SIZE * TAP_SCALE
    from_lon = scale * filter_lat(field(grad_lon), smooth[...], 2)
    from_lat = scale * filter_lat(field(grad_lat), slope[...], 2)
    columns = []
    for j in tiles:
        rows = slice(j * STRIP, (j + 1) * STRIP)
        data = pieces(jnp.concatenate([from_lon[rows], from_lat[rows]], axis=0), 2)
        shift = shift_rows(aux, j)
        pull = [jnp.where(shift == float(s), misfit[j], 0.0) for s in range(OWN)]
        columns.append(jnp.concatenate(data + pieces(jnp.concatenate(pull, axis=0), 2), axis=0))
    spread = dot(backward[...], jnp.concatenate(columns, axis=1))
    for j in tiles:
        change = spread[:, j * LANES : (j + 1) * LANES]
        z_out[j, 0:RAD] = change[0:RAD]
        z_out[j, RAD : RAD + STRIP] = change[RAD : RAD + STRIP] + surface[j][RAD : RAD + STRIP]
        z_out[j, RAD + STRIP : EXT] = change[RAD + STRIP : EXT]
    core = place()[1]
    route(core, z_out[:, 0:STRIP], z_out[:, STRIP:EXT], inter_out, intra_out)


def arrived(inter, intra):
    core = place()[1]
    return (
        jnp.where(core == 0, inter[...], intra[...]),
        jnp.where(core == 0, intra[...], inter[...]),
    )


def surface_step(
    coef, weight, kept, received, halo, surface, aux, alt, tables, z_out, inter_out, intra_out, fields
):
    slope_lon, slope_lat, grad_lon, grad_lat = fields
    misfit = slopes_and_misfit(surface, aux, alt, tables, slope_lon, slope_lat)
    for ref, index, rows in image_tiles(kept, received, halo):
        albedo, lon, lat = ref[(ALBEDO, *index)], slope_lon[rows], slope_lat[rows]
        inverse, shade = shades(albedo, lon, lat)
        sums = None
        for k in range(IMAGES):
            lit = weight[k : k + 1] * ref[(IMAGES + k, *index)]
            pull, norm = image_term(coef, k, ref[(k, *index)], lit, *shade, lon, lat)
            sums = add_image(sums, coef, k, pull, norm)
        grad_lon[rows], grad_lat[rows] = gradients(albedo, inverse, lon, lat, sums)
    contribute(surface, aux, misfit, grad_lon, grad_lat, tables, z_out, inter_out, intra_out)


def first_kernel(coef, counts, kept, received, halo, z, inter, intra, aux, *refs):
    tables, (z_out, inter_out, intra_out, alt_out, weight_out), fields = refs[:5], refs[5:10], refs[10:]
    weight = image_weights(counts)
    weight_out[...] = weight
    above, below = arrived(inter, intra)
    alt = jnp.concatenate([aux[:, 0:8], below[:, 0:8]], axis=1)
    alt_out[...] = alt
    below = jnp.concatenate([jnp.zeros((TILES, RAD, LANES), F32), below[:, RAD:]], axis=1)
    surface = [z[j] + jnp.concatenate([above[j], below[j]], axis=0) for j in range(TILES)]
    surface_step(
        coef, weight, kept, received, halo, surface, aux, alt, tables, z_out, inter_out, intra_out, fields
    )


def step_kernel(coef, weight, kept, received, halo, z, inter, intra, aux, alt, *refs):
    tables, (z_out, inter_out, intra_out), fields = refs[:5], refs[5:8], refs[8:]
    above, below = arrived(inter, intra)
    surface = [z[j] + jnp.concatenate([above[j], below[j]], axis=0) for j in range(TILES)]
    surface_step(
        coef, weight[...], kept, received, halo, surface, aux, alt, tables, z_out, inter_out, intra_out, fields
    )


def end_kernel(z, inter, intra, kept, sent):
    half, core = place()
    for ref, side in ((kept, core), (sent, 1 - core)):
        for t in range(2):
            at = own_tile(half, side, t)
            above = jnp.where(core == 0, inter[at], intra[at])
            below = jnp.where(core == 0, intra[at], inter[at])
            cols = slice(t * LANES, (t + 1) * LANES)
            ref[0:RAD, cols] = z[at, RAD : 2 * RAD] + above[RAD:]
            ref[RAD:STRIP, cols] = z[at, 2 * RAD : RAD + STRIP] + below[0:RAD]


def place_kernel(mine, other, out):
    core = place()[1]
    out[pl.ds(pl.multiple_of(core * STRIP, STRIP), STRIP)] = mine[...]
    out[pl.ds(pl.multiple_of((1 - core) * STRIP, STRIP), STRIP)] = other[...]


def f32(*shape):
    return jax.ShapeDtypeStruct(shape, F32)


def call(kernel, out_shape, *args, scratch=()):
    scalars = kernel in (first_kernel, step_kernel)
    return pl.pallas_call(
        kernel,
        out_shape=out_shape,
        in_specs=[SMEM if scalars and i == 0 else VMEM for i in range(len(args))],
        out_specs=jax.tree.map(lambda _: VMEM, out_shape),
        scratch_shapes=list(scratch),
        compiler_params=PARAMS,
    )(*args)


def per_device(height, albedo, images, lit_mask, lit_count, geometry, owner_column, altimetry):
    lon_count, lat_count = lax.axis_size("lon"), lax.axis_size("lat")
    axes = ("lon", "lat")
    sites = [(a, b) for a in range(lon_count) for b in range(lat_count)]

    def index(a, b):
        return (a % lon_count) * lat_count + b

    across_cores = [(index(a, b), index(a, b ^ 1)) for a, b in sites]
    across_halves = [(index(a, b), index(a, b ^ 2)) for a, b in sites]
    across_strips = [(index(a, b), index(a + 2 * (b % 2) - 1, b ^ 1)) for a, b in sites]

    def exchange(inter, intra):
        return lax.ppermute(inter, axes, across_strips), lax.ppermute(intra, axes, across_cores)

    sun_lon, sun_lat, sun_up, view = (geometry[:, i] for i in range(4))
    coef = jnp.stack(
        [
            SHARPNESS * sun_lon,
            SHARPNESS * sun_lat,
            SHARPNESS * sun_up,
            SHARPNESS * view,
            (LUNAR_MIX * SHARPNESS * SHARPNESS) * view,
            -sun_lon,
            -sun_lat,
        ],
        axis=1,
    )

    expand = np.arange(altimetry.shape[1])[:, None] == np.arange(2 * LANES)[None, :] // OWN
    expand = jnp.asarray(np.concatenate([expand] * 3, axis=0), BF16)
    count = lit_count.reshape(1, IMAGES)
    inputs = (images, lit_mask, height, albedo, owner_column, altimetry, count, expand)
    cut = [(IMAGES, STRIP, 2 * LANES)] * 2 + [(STRIP, 2 * LANES)] * 2 + [(8, 2 * LANES)]
    cut += [a.shape for a in inputs[len(cut) :]]
    fields = f32(FIELDS, 2, STRIP, LANES)
    sent = pl.pallas_call(
        send_kernel,
        out_shape=fields,
        in_specs=[pl.BlockSpec(memory_space=pltpu.HBM)] * len(inputs),
        out_specs=VMEM,
        scratch_shapes=[pltpu.VMEM(shape, a.dtype) for shape, a in zip(cut, inputs)]
        + [pltpu.SemaphoreType.DMA((len(inputs),))],
        compiler_params=LARGE,
    )(*inputs)
    sent, count = lax.optimization_barrier((sent, count))
    received = lax.ppermute(sent, axes, across_cores)
    kept = call(keep_kernel, fields, *inputs[:-2], count, expand)
    near_small = call(near_small_kernel, f32(2, STRIP, LANES), kept, received)
    halo_small = lax.ppermute(near_small, axes, across_halves)
    line = call(count_kernel, f32(LINE, 1, LANES), kept, received, near_small)
    in_line = [
        [index(first + a, b) for a in range(LINE)]
        for first in range(0, lon_count, LINE)
        for b in range(lat_count)
    ]
    across_lines = [
        [index(first + a, b + core) for first in range(0, lon_count, LINE) for b in range(0, lat_count, 2)]
        for a in range(LINE)
        for core in range(2)
    ]
    line = lax.all_to_all(line, axes, 0, 0, axis_index_groups=in_line)
    near = call(near_kernel, f32(HEIGHT, STRIP, LANES), kept, received, near_small)
    halo = lax.ppermute(near, axes, across_halves)
    message = f32(TILES, STRIP, LANES)
    window = f32(TILES, EXT, LANES)
    rows_of_bins = f32(TILES, BINS, LANES)
    z, aux, inter, intra = call(
        begin_kernel, (window, rows_of_bins, message, message), kept, received, halo_small
    )
    counts = call(line_kernel, f32(len(across_lines[0]), 1, LANES), line, inter)
    counts = lax.all_to_all(counts, axes, 0, 0, axis_index_groups=across_lines)
    inter, intra = exchange(inter, intra)
    tables = constants()
    scratch = [pltpu.VMEM((TILES * STRIP, LANES), F32)] * 4
    z, inter, intra, alt, weight = call(
        first_kernel,
        (window, message, message, rows_of_bins, f32(BINS, LANES)),
        coef, counts, kept, received, halo, z, inter, intra, aux, *tables,
        scratch=scratch,
    )
    for _ in range(ITERS - 1):
        inter, intra = exchange(inter, intra)
        z, inter, intra = call(
            step_kernel,
            (window, message, message),
            coef, weight, kept, received, halo, z, inter, intra, aux, alt, *tables,
            scratch=scratch,
        )
    inter, intra = exchange(inter, intra)
    half_out = f32(STRIP, 2 * LANES)
    mine, other = call(end_kernel, (half_out, half_out), z, inter, intra)
    other = lax.ppermute(other, axes, across_cores)
    return call(place_kernel, f32(2 * STRIP, 2 * LANES), mine, other)


def solution(mesh):
    return jax.shard_map(
        per_device,
        mesh=mesh,
        in_specs=(
            P("lon", "lat"),
            P("lon", "lat"),
            P(None, "lon", "lat"),
            P(None, "lon", "lat"),
            P(None, "lon", "lat"),
            P(),
            P("lon", "lat"),
            P("lon", "lat"),
        ),
        out_specs=P("lon", "lat"),
        check_vma=False,
    )
```

```python
import jax
import jax.numpy as jnp
import numpy as np
from jax import lax
from jax.experimental import pallas as pl
from jax.experimental.pallas import tpu as pltpu
from jax.sharding import PartitionSpec as P

IMAGES = 12
RAD = 16
OWN = 4
ITERS = 3
ROWS = 4096
COLUMNS = 1024
STEP_SIZE = 0.05
ALT_WEIGHT = 64.0
DATA_GAIN = 160.0
LUNAR_MIX = 0.6
SHARPNESS = 20.0

LANES = 128
STRIP = 32
EXT = STRIP + 2 * RAD
TILES = 5
FIELDS = 2 * IMAGES + 3
ALBEDO = 2 * IMAGES
HEIGHT = ALBEDO + 1
AUX = HEIGHT + 1
BINS = 16
DENOM = float(RAD * (RAD + 1) * (2 * RAD + 1)) / 3.0
TAP_SCALE = 1.0 / (DENOM * (2 * RAD + 1))
F32 = jnp.float32
BF16 = jnp.bfloat16
VMEM = pl.BlockSpec(memory_space=pltpu.VMEM)
SMEM = pl.BlockSpec(memory_space=pltpu.SMEM)
PARAMS = pltpu.CompilerParams(vmem_limit_bytes=24 * 2**20)
LARGE = pltpu.CompilerParams(vmem_limit_bytes=58 * 2**20)


def band(offset, derivative):
    inside = np.abs(offset) <= RAD
    return np.where(inside, offset if derivative else 1, 0).astype(np.float32)


def constants():
    own = np.arange(STRIP)
    ext = np.arange(EXT) - RAD
    reach = ext[None, :] - own[:, None]
    rows = [band(reach, True), band(reach, False)]
    bins = np.arange(BINS)
    for shift in range(OWN):
        group = (ext[None, :] + shift) // OWN
        rows.append((group == bins[:, None]).astype(np.float32))
    down = np.concatenate(rows, axis=0)
    forward = np.concatenate([down] * 3, axis=1)
    back = own[None, :] - ext[:, None]
    spread = np.zeros((EXT, OWN * BINS), np.float32)
    for shift in range(OWN):
        hit = ((own[:, None] + shift) // OWN) == bins[None, :]
        spread[RAD : RAD + STRIP, shift * BINS : (shift + 1) * BINS] = hit
    filters = np.concatenate([band(back, True), band(back, False)], axis=1)
    backward = np.concatenate([filters, filters, spread, spread], axis=1)
    lane = np.arange(LANES)
    side = np.where(lane < LANES // 2, lane + LANES, lane - LANES)
    source = np.concatenate([lane, side])
    across = source[:, None] - lane[None, :]
    quads = (lane[:, None] // OWN == lane[None, :] // OWN).astype(np.float32)
    return [
        jnp.asarray(m, BF16)
        for m in (forward, backward, band(across, False), band(across, True), quads)
    ]


def pieces(value, count):
    out = []
    for _ in range(count - 1):
        part = value.astype(BF16)
        value = value - part.astype(F32)
        out.append(part)
    out.append(value.astype(BF16))
    return out


def dot(left, right):
    return jnp.dot(left, right, preferred_element_type=F32)


def with_sides(tiles):
    low = lax.broadcasted_iota(jnp.int32, tiles[0].shape, 1) < LANES // 2
    zero = jnp.zeros_like(tiles[0])
    rows = []
    for j, tile in enumerate(tiles):
        after = tiles[j + 1] if j + 1 < len(tiles) else zero
        before = tiles[j - 1] if j > 0 else zero
        rows.append(jnp.concatenate([tile, jnp.where(low, after, before)], axis=1))
    return jnp.concatenate(rows, axis=0)


def filter_lat(tiles, taps, count):
    total = None
    for part in pieces(with_sides(tiles), count):
        term = dot(part, taps)
        total = term if total is None else total + term
    return total


def place():
    lat = lax.axis_index("lat")
    return lat // 2, lat % 2


def own_tile(half, core, t):
    return half + 2 * core + t


def aux_fields(ref, rows_of, owner, altimetry, count, expand):
    bins = owner[0:OWN, :] - lax.axis_index("lon") * BINS
    shift = jnp.sum(bins, axis=0, keepdims=True).astype(F32)
    heights = dot(jnp.concatenate(pieces(altimetry[...], 3), axis=1), expand[...])
    heights = jnp.where(rows_of == 0, heights[0:8], heights[8:16])
    lit = jnp.concatenate([count[...].astype(F32), jnp.zeros((1, LANES - IMAGES), F32)], axis=1)
    for t in range(2):
        lanes = slice(t * LANES, (t + 1) * LANES)
        ref[AUX, t, 0:8] = heights[:, lanes]
        ref[AUX, t, 8:16] = jnp.broadcast_to(shift[:, lanes], (8, LANES))
        ref[AUX, t, 16:24] = jnp.broadcast_to(lit, (8, LANES))
        ref[AUX, t, 24:32] = jnp.zeros((8, LANES), F32)


def send_kernel(
    images_hbm, mask_hbm, height_hbm, albedo_hbm, owner_hbm, altimetry_hbm, count_hbm, expand_hbm,
    sent,
    images, lit_mask, height, albedo, owner, altimetry, count, expand, sems,
):
    other = 1 - place()[1]
    rows = pl.ds(pl.multiple_of(other * STRIP, STRIP), STRIP)
    copies = [
        pltpu.make_async_copy(source, target, sems.at[i])
        for i, (source, target) in enumerate(
            (
                (images_hbm.at[:, rows], images),
                (mask_hbm.at[:, rows], lit_mask),
                (height_hbm.at[rows], height),
                (albedo_hbm.at[rows], albedo),
                (owner_hbm.at[pl.ds(0, 8)], owner),
                (altimetry_hbm, altimetry),
                (count_hbm, count),
                (expand_hbm, expand),
            )
        )
    ]
    for copy in copies:
        copy.start()
    for copy in copies:
        copy.wait()
    aux_fields(sent, other, owner, altimetry, count, expand)
    for t in range(2):
        cols = pl.ds(t * LANES, LANES)
        for k in range(IMAGES):
            sent[k, t] = images[k, :, cols].astype(F32)
            sent[IMAGES + k, t] = lit_mask[k, :, cols].astype(F32)
        sent[ALBEDO, t] = albedo[:, cols]
        sent[HEIGHT, t] = height[:, cols]


def keep_kernel(images, lit_mask, height, albedo, owner, altimetry, count, expand, kept):
    core = place()[1]
    rows = pl.ds(pl.multiple_of(core * STRIP, STRIP), STRIP)
    aux_fields(kept, core, owner, altimetry, count, expand)
    for t in range(2):
        cols = pl.ds(t * LANES, LANES)
        for k in range(IMAGES):
            kept[k, t] = images[k, rows, cols].astype(F32)
            kept[IMAGES + k, t] = lit_mask[k, rows, cols].astype(F32)
        kept[ALBEDO, t] = albedo[rows, cols]
        kept[HEIGHT, t] = height[rows, cols]


def near_small_kernel(kept, received, near_small):
    half, core = place()
    for i, field in enumerate((HEIGHT, AUX)):
        near_small[i] = jnp.where(half != core, kept[field, 1 - half], received[field, 1 - half])
    near_small[1, 16:24] = kept[AUX, 0, 16:24] + received[AUX, 0, 16:24]


def near_kernel(kept, received, near_small, near):
    half, core = place()

    @pl.when(half != core)
    def _():
        near[...] = kept[0:HEIGHT, 1 - half]

    @pl.when(half == core)
    def _():
        near[...] = received[0:HEIGHT, 1 - half]


def count_kernel(halo_small, near_small, near, counts):
    total = halo_small[1, 16:17] + near_small[1, 16:17]
    counts[...] = jnp.broadcast_to(total[None], counts.shape)


def route(core, up, down, inter, intra):
    inter[...] = jnp.where(core == 0, up, down)
    intra[...] = jnp.where(core == 0, down, up)


def begin_kernel(kept, received, halo_small, z, aux, inter, intra):
    half, core = place()
    zero = jnp.zeros((TILES, RAD, LANES), F32)
    z[:, 0:RAD] = zero
    z[:, RAD + STRIP : EXT] = zero
    for t in range(2):
        for ref, at in ((kept, own_tile(half, core, t)), (received, own_tile(half, 1 - core, t))):
            z[at, RAD : RAD + STRIP] = ref[HEIGHT, t]
            aux[at] = ref[AUX, t, 0:BINS]
    far = (TILES - 1) * (1 - half)
    z[far, RAD : RAD + STRIP] = halo_small[0]
    aux[far] = halo_small[1, 0:BINS]
    alt = jnp.concatenate([aux[:, 0:8], jnp.zeros((TILES, 8, LANES), F32)], axis=1)
    up = jnp.concatenate([alt, z[:, RAD : 2 * RAD]], axis=1)
    route(core, up, z[:, STRIP:EXT], inter, intra)


def image_weights(counts):
    total = jnp.sum(counts[...], axis=0)
    weight = 2.0 * DATA_GAIN * float(ROWS * COLUMNS) / total
    image = lax.broadcasted_iota(jnp.int32, (BINS, LANES), 0)
    lane = lax.broadcasted_iota(jnp.int32, (BINS, LANES), 1)
    diagonal = jnp.where((image == lane) & (image < IMAGES), weight, 0.0)
    ones = jnp.ones((LANES, LANES), BF16)
    first, second, third = pieces(diagonal, 3)
    return dot(first, ones) + dot(second, ones) + dot(third, ones)


def image_term(coef, k, observed, lit, flat_part, flat_shade, mix_shade, slope_lon, slope_lat):
    steep = coef[k, 2] - coef[k, 0] * slope_lon - coef[k, 1] * slope_lat
    decay = jnp.exp(-jnp.abs(steep))
    whole = 1.0 + decay
    part = jnp.maximum(steep, 0.0) + jnp.log(whole)
    ratio = 1.0 / (part + coef[k, 3])
    gate = jnp.where(steep >= 0.0, 1.0, decay) / whole
    residual = lit * (part * (mix_shade * ratio + flat_shade) - observed)
    pull = residual * ((coef[k, 4] * (ratio * ratio) + flat_part) * gate)
    return pull, residual * part


def shades(albedo, slope_lon, slope_lat):
    inverse = lax.rsqrt(1.0 + slope_lon * slope_lon + slope_lat * slope_lat)
    flat_part = (1.0 - LUNAR_MIX) * inverse
    return inverse, (flat_part, flat_part * (albedo * (1.0 / SHARPNESS)), albedo * LUNAR_MIX)


def gradients(albedo, inverse, slope_lon, slope_lat, sums):
    sum_lon, sum_lat, sum_norm = sums
    bend = (1.0 - LUNAR_MIX) / SHARPNESS * (inverse * inverse * inverse) * sum_norm
    return albedo * (sum_lon - slope_lon * bend), albedo * (sum_lat - slope_lat * bend)


def add_image(sums, coef, k, pull, norm):
    terms = (coef[k, 5] * pull, coef[k, 6] * pull, norm)
    return terms if sums is None else tuple(a + b for a, b in zip(sums, terms))


def tile_rows(at):
    return pl.ds(pl.multiple_of(at * STRIP, STRIP), STRIP)


def image_tiles(kept, received, halo):
    half, core = place()
    for t in range(2):
        yield kept, (t,), tile_rows(own_tile(half, core, t))
        yield received, (t,), tile_rows(own_tile(half, 1 - core, t))
    yield halo, (), tile_rows((TILES - 1) * (1 - half))


def shift_rows(aux, j):
    return jnp.concatenate([aux[j, 8:16]] * 2, axis=0)


def slopes_and_misfit(surface, aux, alt, tables, slope_lon, slope_lat):
    forward, backward, smooth, slope, quads = tables
    tiles = range(TILES)
    stacked = jnp.concatenate(
        [jnp.concatenate(pieces(surface[j], 3), axis=0) for j in tiles], axis=1
    )
    down = dot(forward[...], stacked)

    def part(row, count, j):
        return down[row : row + count, j * LANES : (j + 1) * LANES]

    slope_lon[...] = TAP_SCALE * filter_lat([part(0, STRIP, j) for j in tiles], smooth[...], 3)
    slope_lat[...] = TAP_SCALE * filter_lat([part(STRIP, STRIP, j) for j in tiles], slope[...], 3)
    sums = []
    for j in tiles:
        shift = shift_rows(aux, j)
        chosen = part(2 * STRIP, BINS, j)
        for s in range(1, OWN):
            chosen = jnp.where(shift == float(s), part(2 * STRIP + s * BINS, BINS, j), chosen)
        sums.append(chosen)
    owner_sum = None
    for p in pieces(jnp.concatenate(sums, axis=0), 3):
        term = dot(p, quads[...])
        owner_sum = term if owner_sum is None else owner_sum + term
    gain = STEP_SIZE * 2.0 * ALT_WEIGHT / (OWN * OWN)
    rows = [slice(j * BINS, (j + 1) * BINS) for j in tiles]
    return [gain * alt[j] - (gain / (OWN * OWN)) * owner_sum[rows[j]] for j in tiles]


def contribute(surface, aux, misfit, grad_lon, grad_lat, tables, z_out, inter_out, intra_out):
    forward, backward, smooth, slope, quads = tables
    tiles = range(TILES)

    def field(ref):
        return [ref[j * STRIP : (j + 1) * STRIP] for j in tiles]

    scale = STEP_SIZE * TAP_SCALE
    from_lon = scale * filter_lat(field(grad_lon), smooth[...], 2)
    from_lat = scale * filter_lat(field(grad_lat), slope[...], 2)
    columns = []
    for j in tiles:
        rows = slice(j * STRIP, (j + 1) * STRIP)
        data = pieces(jnp.concatenate([from_lon[rows], from_lat[rows]], axis=0), 2)
        shift = shift_rows(aux, j)
        pull = [jnp.where(shift == float(s), misfit[j], 0.0) for s in range(OWN)]
        columns.append(jnp.concatenate(data + pieces(jnp.concatenate(pull, axis=0), 2), axis=0))
    spread = dot(backward[...], jnp.concatenate(columns, axis=1))
    for j in tiles:
        change = spread[:, j * LANES : (j + 1) * LANES]
        z_out[j, 0:RAD] = change[0:RAD]
        z_out[j, RAD : RAD + STRIP] = change[RAD : RAD + STRIP] + surface[j][RAD : RAD + STRIP]
        z_out[j, RAD + STRIP : EXT] = change[RAD + STRIP : EXT]
    core = place()[1]
    route(core, z_out[:, 0:STRIP], z_out[:, STRIP:EXT], inter_out, intra_out)


def arrived(inter, intra):
    core = place()[1]
    return (
        jnp.where(core == 0, inter[...], intra[...]),
        jnp.where(core == 0, intra[...], inter[...]),
    )


def surface_step(
    coef, weight, kept, received, halo, surface, aux, alt, tables, z_out, inter_out, intra_out, fields
):
    slope_lon, slope_lat, grad_lon, grad_lat = fields
    misfit = slopes_and_misfit(surface, aux, alt, tables, slope_lon, slope_lat)
    for ref, index, rows in image_tiles(kept, received, halo):
        albedo, lon, lat = ref[(ALBEDO, *index)], slope_lon[rows], slope_lat[rows]
        inverse, shade = shades(albedo, lon, lat)
        sums = None
        for k in range(IMAGES):
            lit = weight[k : k + 1] * ref[(IMAGES + k, *index)]
            pull, norm = image_term(coef, k, ref[(k, *index)], lit, *shade, lon, lat)
            sums = add_image(sums, coef, k, pull, norm)
        grad_lon[rows], grad_lat[rows] = gradients(albedo, inverse, lon, lat, sums)
    contribute(surface, aux, misfit, grad_lon, grad_lat, tables, z_out, inter_out, intra_out)


def first_kernel(coef, counts, kept, received, halo, z, inter, intra, aux, *refs):
    tables, (z_out, inter_out, intra_out, alt_out, weight_out), fields = refs[:5], refs[5:10], refs[10:]
    weight = image_weights(counts)
    weight_out[...] = weight
    above, below = arrived(inter, intra)
    alt = jnp.concatenate([aux[:, 0:8], below[:, 0:8]], axis=1)
    alt_out[...] = alt
    below = jnp.concatenate([jnp.zeros((TILES, RAD, LANES), F32), below[:, RAD:]], axis=1)
    surface = [z[j] + jnp.concatenate([above[j], below[j]], axis=0) for j in range(TILES)]
    surface_step(
        coef, weight, kept, received, halo, surface, aux, alt, tables, z_out, inter_out, intra_out, fields
    )


def step_kernel(coef, weight, kept, received, halo, z, inter, intra, aux, alt, *refs):
    tables, (z_out, inter_out, intra_out), fields = refs[:5], refs[5:8], refs[8:]
    above, below = arrived(inter, intra)
    surface = [z[j] + jnp.concatenate([above[j], below[j]], axis=0) for j in range(TILES)]
    surface_step(
        coef, weight[...], kept, received, halo, surface, aux, alt, tables, z_out, inter_out, intra_out, fields
    )


def end_kernel(z, inter, intra, kept, sent):
    half, core = place()
    for ref, side in ((kept, core), (sent, 1 - core)):
        for t in range(2):
            at = own_tile(half, side, t)
            above = jnp.where(core == 0, inter[at], intra[at])
            below = jnp.where(core == 0, intra[at], inter[at])
            cols = slice(t * LANES, (t + 1) * LANES)
            ref[0:RAD, cols] = z[at, RAD : 2 * RAD] + above[RAD:]
            ref[RAD:STRIP, cols] = z[at, 2 * RAD : RAD + STRIP] + below[0:RAD]


def place_kernel(mine, other, out):
    core = place()[1]
    out[pl.ds(pl.multiple_of(core * STRIP, STRIP), STRIP)] = mine[...]
    out[pl.ds(pl.multiple_of((1 - core) * STRIP, STRIP), STRIP)] = other[...]


def f32(*shape):
    return jax.ShapeDtypeStruct(shape, F32)


def call(kernel, out_shape, *args, scratch=()):
    scalars = kernel in (first_kernel, step_kernel)
    return pl.pallas_call(
        kernel,
        out_shape=out_shape,
        in_specs=[SMEM if scalars and i == 0 else VMEM for i in range(len(args))],
        out_specs=jax.tree.map(lambda _: VMEM, out_shape),
        scratch_shapes=list(scratch),
        compiler_params=PARAMS,
    )(*args)


def per_device(height, albedo, images, lit_mask, lit_count, geometry, owner_column, altimetry):
    lon_count, lat_count = lax.axis_size("lon"), lax.axis_size("lat")
    axes = ("lon", "lat")
    sites = [(a, b) for a in range(lon_count) for b in range(lat_count)]

    def index(a, b):
        return (a % lon_count) * lat_count + b

    across_cores = [(index(a, b), index(a, b ^ 1)) for a, b in sites]
    across_halves = [(index(a, b), index(a, b ^ 2)) for a, b in sites]
    across_strips = [(index(a, b), index(a + 2 * (b % 2) - 1, b ^ 1)) for a, b in sites]

    def exchange(inter, intra):
        return lax.ppermute(inter, axes, across_strips), lax.ppermute(intra, axes, across_cores)

    sun_lon, sun_lat, sun_up, view = (geometry[:, i] for i in range(4))
    coef = jnp.stack(
        [
            SHARPNESS * sun_lon,
            SHARPNESS * sun_lat,
            SHARPNESS * sun_up,
            SHARPNESS * view,
            (LUNAR_MIX * SHARPNESS * SHARPNESS) * view,
            -sun_lon,
            -sun_lat,
        ],
        axis=1,
    )

    expand = np.arange(altimetry.shape[1])[:, None] == np.arange(2 * LANES)[None, :] // OWN
    expand = jnp.asarray(np.concatenate([expand] * 3, axis=0), BF16)
    count = lit_count.reshape(1, IMAGES)
    inputs = (images, lit_mask, height, albedo, owner_column, altimetry, count, expand)
    cut = [(IMAGES, STRIP, 2 * LANES)] * 2 + [(STRIP, 2 * LANES)] * 2 + [(8, 2 * LANES)]
    cut += [a.shape for a in inputs[len(cut) :]]
    fields = f32(FIELDS, 2, STRIP, LANES)
    sent = pl.pallas_call(
        send_kernel,
        out_shape=fields,
        in_specs=[pl.BlockSpec(memory_space=pltpu.HBM)] * len(inputs),
        out_specs=VMEM,
        scratch_shapes=[pltpu.VMEM(shape, a.dtype) for shape, a in zip(cut, inputs)]
        + [pltpu.SemaphoreType.DMA((len(inputs),))],
        compiler_params=LARGE,
    )(*inputs)
    sent, count = lax.optimization_barrier((sent, count))
    received = lax.ppermute(sent, axes, across_cores)
    kept = call(keep_kernel, fields, *inputs[:-2], count, expand)
    near_small = call(near_small_kernel, f32(2, STRIP, LANES), kept, received)
    halo_small = lax.ppermute(near_small, axes, across_halves)
    near = call(near_kernel, f32(HEIGHT, STRIP, LANES), kept, received, near_small)
    halo = lax.ppermute(near, axes, across_halves)
    counts = call(count_kernel, f32(lon_count, 1, LANES), halo_small, near_small, near[:1, :8])
    counts, halo_small = lax.optimization_barrier((counts, halo_small))
    counts = lax.all_to_all(counts, "lon", 0, 0)
    message = f32(TILES, STRIP, LANES)
    window = f32(TILES, EXT, LANES)
    rows_of_bins = f32(TILES, BINS, LANES)
    z, aux, inter, intra = call(
        begin_kernel, (window, rows_of_bins, message, message), kept, received, halo_small
    )
    inter, intra = exchange(inter, intra)
    tables = constants()
    scratch = [pltpu.VMEM((TILES * STRIP, LANES), F32)] * 4
    z, inter, intra, alt, weight = call(
        first_kernel,
        (window, message, message, rows_of_bins, f32(BINS, LANES)),
        coef, counts, kept, received, halo, z, inter, intra, aux, *tables,
        scratch=scratch,
    )
    for _ in range(ITERS - 1):
        inter, intra = exchange(inter, intra)
        z, inter, intra = call(
            step_kernel,
            (window, message, message),
            coef, weight, kept, received, halo, z, inter, intra, aux, alt, *tables,
            scratch=scratch,
        )
    inter, intra = exchange(inter, intra)
    half_out = f32(STRIP, 2 * LANES)
    mine, other = call(end_kernel, (half_out, half_out), z, inter, intra)
    other = lax.ppermute(other, axes, across_cores)
    return call(place_kernel, f32(2 * STRIP, 2 * LANES), mine, other)


def solution(mesh):
    return jax.shard_map(
        per_device,
        mesh=mesh,
        in_specs=(
            P("lon", "lat"),
            P("lon", "lat"),
            P(None, "lon", "lat"),
            P(None, "lon", "lat"),
            P(None, "lon", "lat"),
            P(),
            P("lon", "lat"),
            P("lon", "lat"),
        ),
        out_specs=P("lon", "lat"),
        check_vma=False,
    )
```

```python
import jax
import jax.numpy as jnp
import numpy as np
from jax import lax
from jax.experimental import pallas as pl
from jax.experimental.pallas import tpu as pltpu
from jax.sharding import PartitionSpec as P

IMAGES = 12
RAD = 16
OWN = 4
ITERS = 3
ROWS = 4096
COLUMNS = 1024
STEP_SIZE = 0.05
ALT_WEIGHT = 64.0
DATA_GAIN = 160.0
LUNAR_MIX = 0.6
SHARPNESS = 20.0

LANES = 128
STRIP = 32
EXT = STRIP + 2 * RAD
TILES = 5
FIELDS = 2 * IMAGES + 3
ALBEDO = 2 * IMAGES
HEIGHT = ALBEDO + 1
AUX = HEIGHT + 1
BINS = 16
DENOM = float(RAD * (RAD + 1) * (2 * RAD + 1)) / 3.0
TAP_SCALE = 1.0 / (DENOM * (2 * RAD + 1))
F32 = jnp.float32
BF16 = jnp.bfloat16
VMEM = pl.BlockSpec(memory_space=pltpu.VMEM)
PARAMS = pltpu.CompilerParams(vmem_limit_bytes=24 * 2**20)
LARGE = pltpu.CompilerParams(vmem_limit_bytes=58 * 2**20)


def band(offset, derivative):
    inside = np.abs(offset) <= RAD
    return np.where(inside, offset if derivative else 1, 0).astype(np.float32)


def constants():
    own = np.arange(STRIP)
    ext = np.arange(EXT) - RAD
    reach = ext[None, :] - own[:, None]
    rows = [band(reach, True), band(reach, False)]
    bins = np.arange(BINS)
    for shift in range(OWN):
        group = (ext[None, :] + shift) // OWN
        rows.append((group == bins[:, None]).astype(np.float32))
    down = np.concatenate(rows, axis=0)
    forward = np.concatenate([down] * 3, axis=1)
    back = own[None, :] - ext[:, None]
    spread = np.zeros((EXT, OWN * BINS), np.float32)
    for shift in range(OWN):
        hit = ((own[:, None] + shift) // OWN) == bins[None, :]
        spread[RAD : RAD + STRIP, shift * BINS : (shift + 1) * BINS] = hit
    filters = np.concatenate([band(back, True), band(back, False)], axis=1)
    backward = np.concatenate([filters, filters, spread, spread], axis=1)
    lane = np.arange(LANES)
    side = np.where(lane < LANES // 2, lane + LANES, lane - LANES)
    source = np.concatenate([lane, side])
    across = source[:, None] - lane[None, :]
    quads = (lane[:, None] // OWN == lane[None, :] // OWN).astype(np.float32)
    return [
        jnp.asarray(m, BF16)
        for m in (forward, backward, band(across, False), band(across, True), quads)
    ]


def pieces(value, count):
    out = []
    for _ in range(count - 1):
        part = value.astype(BF16)
        value = value - part.astype(F32)
        out.append(part)
    out.append(value.astype(BF16))
    return out


def dot(left, right):
    return jnp.dot(left, right, preferred_element_type=F32)


def with_sides(tiles):
    low = lax.broadcasted_iota(jnp.int32, tiles[0].shape, 1) < LANES // 2
    zero = jnp.zeros_like(tiles[0])
    rows = []
    for j, tile in enumerate(tiles):
        after = tiles[j + 1] if j + 1 < len(tiles) else zero
        before = tiles[j - 1] if j > 0 else zero
        rows.append(jnp.concatenate([tile, jnp.where(low, after, before)], axis=1))
    return jnp.concatenate(rows, axis=0)


def filter_lat(tiles, taps, count):
    total = None
    for part in pieces(with_sides(tiles), count):
        term = dot(part, taps)
        total = term if total is None else total + term
    return total


def place():
    lat = lax.axis_index("lat")
    return lat // 2, lat % 2


def own_tile(half, core, t):
    return half + 2 * core + t


def aux_fields(ref, rows_of, owner, altimetry, count, expand):
    bins = owner[0:OWN, :] - lax.axis_index("lon") * BINS
    shift = jnp.sum(bins, axis=0, keepdims=True).astype(F32)
    heights = dot(jnp.concatenate(pieces(altimetry[...], 3), axis=1), expand[...])
    heights = jnp.where(rows_of == 0, heights[0:8], heights[8:16])
    lit = jnp.concatenate([count[...].astype(F32), jnp.zeros((1, LANES - IMAGES), F32)], axis=1)
    for t in range(2):
        lanes = slice(t * LANES, (t + 1) * LANES)
        ref[AUX, t, 0:8] = heights[:, lanes]
        ref[AUX, t, 8:16] = jnp.broadcast_to(shift[:, lanes], (8, LANES))
        ref[AUX, t, 16:24] = jnp.broadcast_to(lit, (8, LANES))
        ref[AUX, t, 24:32] = jnp.zeros((8, LANES), F32)


def send_kernel(
    images_hbm, mask_hbm, height_hbm, albedo_hbm, owner_hbm, altimetry_hbm, count_hbm, expand_hbm,
    sent,
    images, lit_mask, height, albedo, owner, altimetry, count, expand, sems,
):
    other = 1 - place()[1]
    rows = pl.ds(pl.multiple_of(other * STRIP, STRIP), STRIP)
    copies = [
        pltpu.make_async_copy(source, target, sems.at[i])
        for i, (source, target) in enumerate(
            (
                (images_hbm.at[:, rows], images),
                (mask_hbm.at[:, rows], lit_mask),
                (height_hbm.at[rows], height),
                (albedo_hbm.at[rows], albedo),
                (owner_hbm.at[pl.ds(0, 8)], owner),
                (altimetry_hbm, altimetry),
                (count_hbm, count),
                (expand_hbm, expand),
            )
        )
    ]
    for copy in copies:
        copy.start()
    for copy in copies:
        copy.wait()
    aux_fields(sent, other, owner, altimetry, count, expand)
    for t in range(2):
        cols = pl.ds(t * LANES, LANES)
        for k in range(IMAGES):
            sent[k, t] = images[k, :, cols].astype(F32)
            sent[IMAGES + k, t] = lit_mask[k, :, cols].astype(F32)
        sent[ALBEDO, t] = albedo[:, cols]
        sent[HEIGHT, t] = height[:, cols]


def keep_kernel(images, lit_mask, height, albedo, owner, altimetry, count, expand, kept):
    core = place()[1]
    rows = pl.ds(pl.multiple_of(core * STRIP, STRIP), STRIP)
    aux_fields(kept, core, owner, altimetry, count, expand)
    for t in range(2):
        cols = pl.ds(t * LANES, LANES)
        for k in range(IMAGES):
            kept[k, t] = images[k, rows, cols].astype(F32)
            kept[IMAGES + k, t] = lit_mask[k, rows, cols].astype(F32)
        kept[ALBEDO, t] = albedo[rows, cols]
        kept[HEIGHT, t] = height[rows, cols]


def near_small_kernel(kept, received, near_small):
    half, core = place()
    for i, field in enumerate((HEIGHT, AUX)):
        near_small[i] = jnp.where(half != core, kept[field, 1 - half], received[field, 1 - half])
    near_small[1, 16:24] = kept[AUX, 0, 16:24] + received[AUX, 0, 16:24]


def near_kernel(kept, received, near_small, near):
    half, core = place()

    @pl.when(half != core)
    def _():
        near[...] = kept[0:HEIGHT, 1 - half]

    @pl.when(half == core)
    def _():
        near[...] = received[0:HEIGHT, 1 - half]


def count_kernel(halo_small, near_small, near, counts):
    total = halo_small[1, 16:17] + near_small[1, 16:17]
    counts[...] = jnp.broadcast_to(total[None], counts.shape)


def route(core, up, down, inter, intra):
    inter[...] = jnp.where(core == 0, up, down)
    intra[...] = jnp.where(core == 0, down, up)


def begin_kernel(kept, received, halo_small, z, aux, inter, intra):
    half, core = place()
    zero = jnp.zeros((TILES, RAD, LANES), F32)
    z[:, 0:RAD] = zero
    z[:, RAD + STRIP : EXT] = zero
    for t in range(2):
        for ref, at in ((kept, own_tile(half, core, t)), (received, own_tile(half, 1 - core, t))):
            z[at, RAD : RAD + STRIP] = ref[HEIGHT, t]
            aux[at] = ref[AUX, t, 0:BINS]
    far = (TILES - 1) * (1 - half)
    z[far, RAD : RAD + STRIP] = halo_small[0]
    aux[far] = halo_small[1, 0:BINS]
    alt = jnp.concatenate([aux[:, 0:8], jnp.zeros((TILES, 8, LANES), F32)], axis=1)
    up = jnp.concatenate([alt, z[:, RAD : 2 * RAD]], axis=1)
    route(core, up, z[:, STRIP:EXT], inter, intra)


def image_weights(counts):
    total = jnp.sum(counts[...], axis=0)
    weight = 2.0 * DATA_GAIN * float(ROWS * COLUMNS) / total
    image = lax.broadcasted_iota(jnp.int32, (BINS, LANES), 0)
    lane = lax.broadcasted_iota(jnp.int32, (BINS, LANES), 1)
    diagonal = jnp.where((image == lane) & (image < IMAGES), weight, 0.0)
    ones = jnp.ones((LANES, LANES), BF16)
    first, second, third = pieces(diagonal, 3)
    return dot(first, ones) + dot(second, ones) + dot(third, ones)


def image_term(coef, k, observed, lit, flat_part, flat_shade, mix_shade, slope_lon, slope_lat):
    steep = coef[2, k : k + 1] - coef[0, k : k + 1] * slope_lon - coef[1, k : k + 1] * slope_lat
    decay = jnp.exp(-jnp.abs(steep))
    whole = 1.0 + decay
    part = jnp.maximum(steep, 0.0) + jnp.log(whole)
    ratio = 1.0 / (part + coef[3, k : k + 1])
    gate = jnp.where(steep >= 0.0, 1.0, decay) / whole
    residual = lit * (part * (mix_shade * ratio + flat_shade) - observed)
    pull = residual * ((coef[4, k : k + 1] * (ratio * ratio) + flat_part) * gate)
    return pull, residual * part


def shades(albedo, slope_lon, slope_lat):
    inverse = lax.rsqrt(1.0 + slope_lon * slope_lon + slope_lat * slope_lat)
    flat_part = (1.0 - LUNAR_MIX) * inverse
    return inverse, (flat_part, flat_part * (albedo * (1.0 / SHARPNESS)), albedo * LUNAR_MIX)


def gradients(albedo, inverse, slope_lon, slope_lat, sums):
    sum_lon, sum_lat, sum_norm = sums
    bend = (1.0 - LUNAR_MIX) / SHARPNESS * (inverse * inverse * inverse) * sum_norm
    return albedo * (sum_lon - slope_lon * bend), albedo * (sum_lat - slope_lat * bend)


def add_image(sums, coef, k, pull, norm):
    terms = (coef[5, k : k + 1] * pull, coef[6, k : k + 1] * pull, norm)
    return terms if sums is None else tuple(a + b for a, b in zip(sums, terms))


def tile_rows(at):
    return pl.ds(pl.multiple_of(at * STRIP, STRIP), STRIP)


def image_tiles(kept, received, halo):
    half, core = place()
    for t in range(2):
        yield kept, (t,), tile_rows(own_tile(half, core, t))
        yield received, (t,), tile_rows(own_tile(half, 1 - core, t))
    yield halo, (), tile_rows((TILES - 1) * (1 - half))


def shift_rows(aux, j):
    return jnp.concatenate([aux[j, 8:16]] * 2, axis=0)


def slopes_and_misfit(surface, aux, alt, tables, slope_lon, slope_lat):
    forward, backward, smooth, slope, quads = tables
    tiles = range(TILES)
    stacked = jnp.concatenate(
        [jnp.concatenate(pieces(surface[j], 3), axis=0) for j in tiles], axis=1
    )
    down = dot(forward[...], stacked)

    def part(row, count, j):
        return down[row : row + count, j * LANES : (j + 1) * LANES]

    slope_lon[...] = TAP_SCALE * filter_lat([part(0, STRIP, j) for j in tiles], smooth[...], 3)
    slope_lat[...] = TAP_SCALE * filter_lat([part(STRIP, STRIP, j) for j in tiles], slope[...], 3)
    sums = []
    for j in tiles:
        shift = shift_rows(aux, j)
        chosen = part(2 * STRIP, BINS, j)
        for s in range(1, OWN):
            chosen = jnp.where(shift == float(s), part(2 * STRIP + s * BINS, BINS, j), chosen)
        sums.append(chosen)
    owner_sum = None
    for p in pieces(jnp.concatenate(sums, axis=0), 3):
        term = dot(p, quads[...])
        owner_sum = term if owner_sum is None else owner_sum + term
    gain = STEP_SIZE * 2.0 * ALT_WEIGHT / (OWN * OWN)
    rows = [slice(j * BINS, (j + 1) * BINS) for j in tiles]
    return [gain * alt[j] - (gain / (OWN * OWN)) * owner_sum[rows[j]] for j in tiles]


def contribute(surface, aux, misfit, grad_lon, grad_lat, tables, z_out):
    forward, backward, smooth, slope, quads = tables
    tiles = range(TILES)

    def field(ref):
        return [ref[j * STRIP : (j + 1) * STRIP] for j in tiles]

    scale = STEP_SIZE * TAP_SCALE
    from_lon = scale * filter_lat(field(grad_lon), smooth[...], 2)
    from_lat = scale * filter_lat(field(grad_lat), slope[...], 2)
    columns = []
    for j in tiles:
        rows = slice(j * STRIP, (j + 1) * STRIP)
        data = pieces(jnp.concatenate([from_lon[rows], from_lat[rows]], axis=0), 2)
        shift = shift_rows(aux, j)
        pull = [jnp.where(shift == float(s), misfit[j], 0.0) for s in range(OWN)]
        columns.append(jnp.concatenate(data + pieces(jnp.concatenate(pull, axis=0), 2), axis=0))
    spread = dot(backward[...], jnp.concatenate(columns, axis=1))
    for j in tiles:
        change = spread[:, j * LANES : (j + 1) * LANES]
        z_out[j, 0:RAD] = change[0:RAD]
        z_out[j, RAD : RAD + STRIP] = change[RAD : RAD + STRIP] + surface[j][RAD : RAD + STRIP]
        z_out[j, RAD + STRIP : EXT] = change[RAD + STRIP : EXT]


def arrived(inter, intra):
    core = place()[1]
    return (
        jnp.where(core == 0, inter[...], intra[...]),
        jnp.where(core == 0, intra[...], inter[...]),
    )


def surface_step(
    coef, weight, kept, received, halo, surface, aux, alt, tables, z_out, fields
):
    slope_lon, slope_lat, grad_lon, grad_lat = fields
    misfit = slopes_and_misfit(surface, aux, alt, tables, slope_lon, slope_lat)
    for ref, index, rows in image_tiles(kept, received, halo):
        albedo, lon, lat = ref[(ALBEDO, *index)], slope_lon[rows], slope_lat[rows]
        inverse, shade = shades(albedo, lon, lat)
        sums = None
        for k in range(IMAGES):
            lit = weight[k : k + 1] * ref[(IMAGES + k, *index)]
            pull, norm = image_term(coef, k, ref[(k, *index)], lit, *shade, lon, lat)
            sums = add_image(sums, coef, k, pull, norm)
        grad_lon[rows], grad_lat[rows] = gradients(albedo, inverse, lon, lat, sums)
    contribute(surface, aux, misfit, grad_lon, grad_lat, tables, z_out)


def first_kernel(coef, counts, kept, received, halo, z, inter, intra, aux, *refs):
    tables, (z_out, inter_out, intra_out, alt_out, weight_out), fields = refs[:5], refs[5:10], refs[10:]
    weight = image_weights(counts)
    weight_out[...] = weight
    above, below = arrived(inter, intra)
    alt = jnp.concatenate([aux[:, 0:8], below[:, 0:8]], axis=1)
    alt_out[...] = alt
    below = jnp.concatenate([jnp.zeros((TILES, RAD, LANES), F32), below[:, RAD:]], axis=1)
    surface = [z[j] + jnp.concatenate([above[j], below[j]], axis=0) for j in range(TILES)]
    surface_step(
        coef, weight, kept, received, halo, surface, aux, alt, tables, z_out, fields
    )
    route(place()[1], z_out[:, 0:STRIP], z_out[:, STRIP:EXT], inter_out, intra_out)


def step_kernel(coef, weight, kept, received, halo, z, inter, intra, aux, alt, *refs):
    tables, (z_out, inter_out, intra_out), fields = refs[:5], refs[5:8], refs[8:]
    above, below = arrived(inter, intra)
    surface = [z[j] + jnp.concatenate([above[j], below[j]], axis=0) for j in range(TILES)]
    surface_step(
        coef, weight[...], kept, received, halo, surface, aux, alt, tables, z_out, fields
    )
    route(place()[1], z_out[:, 0:STRIP], z_out[:, STRIP:EXT], inter_out, intra_out)


def last_kernel(coef, weight, kept, received, halo, z, inter, intra, aux, alt, *refs):
    tables, (mine, inter_out, intra_out, z_out), fields = refs[:5], refs[5:9], refs[9:]
    above, below = arrived(inter, intra)
    surface = [z[j] + jnp.concatenate([above[j], below[j]], axis=0) for j in range(TILES)]
    surface_step(
        coef, weight[...], kept, received, halo, surface, aux, alt, tables, z_out, fields
    )
    half, core = place()
    for t in range(2):
        mine[t] = z_out[own_tile(half, core, t)]
        intra_out[t] = z_out[own_tile(half, 1 - core, t)]
    for t in range(TILES - 1):
        inter_out[t] = jnp.where(core == 0, z_out[half + t, 0:RAD], z_out[half + t, EXT - RAD : EXT])


def forward_kernel(inter, forward):
    core = place()[1]
    for t in range(2):
        forward[t] = inter[2 * (1 - core) + t]


def place_kernel(mine, intra, inter, forward, out):
    core = place()[1]
    for t in range(2):
        upper = jnp.where(core == 0, mine[t], intra[t])
        lower = jnp.where(core == 0, intra[t], mine[t])
        direct = inter[2 * core + t]
        top = jnp.where(core == 0, direct, forward[t])
        bottom = jnp.where(core == 0, forward[t], direct)
        cols = slice(t * LANES, (t + 1) * LANES)
        out[0:RAD, cols] = upper[RAD : 2 * RAD] + top
        out[RAD : 2 * RAD, cols] = upper[2 * RAD : 3 * RAD] + lower[0:RAD]
        out[2 * RAD : 3 * RAD, cols] = lower[RAD : 2 * RAD] + upper[3 * RAD : EXT]
        out[3 * RAD : EXT, cols] = lower[2 * RAD : 3 * RAD] + bottom


def f32(*shape):
    return jax.ShapeDtypeStruct(shape, F32)


def call(kernel, out_shape, *args, scratch=()):
    return pl.pallas_call(
        kernel,
        out_shape=out_shape,
        in_specs=[VMEM] * len(args),
        out_specs=jax.tree.map(lambda _: VMEM, out_shape),
        scratch_shapes=list(scratch),
        compiler_params=PARAMS,
    )(*args)


def per_device(height, albedo, images, lit_mask, lit_count, geometry, owner_column, altimetry):
    lon_count, lat_count = lax.axis_size("lon"), lax.axis_size("lat")
    axes = ("lon", "lat")
    sites = [(a, b) for a in range(lon_count) for b in range(lat_count)]

    def index(a, b):
        return (a % lon_count) * lat_count + b

    across_cores = [(index(a, b), index(a, b ^ 1)) for a, b in sites]
    across_halves = [(index(a, b), index(a, b ^ 2)) for a, b in sites]
    across_strips = [(index(a, b), index(a + 2 * (b % 2) - 1, b ^ 1)) for a, b in sites]

    def exchange(inter, intra):
        return lax.ppermute(inter, axes, across_strips), lax.ppermute(intra, axes, across_cores)

    sun_lon, sun_lat, sun_up, view = (geometry[:, i] for i in range(4))
    rows = [
        SHARPNESS * sun_lon,
        SHARPNESS * sun_lat,
        SHARPNESS * sun_up,
        SHARPNESS * view,
        (LUNAR_MIX * SHARPNESS * SHARPNESS) * view,
        -sun_lon,
        -sun_lat,
    ]
    coef = jnp.stack([jnp.broadcast_to(row[:, None], (IMAGES, LANES)) for row in rows])
    expand = np.arange(altimetry.shape[1])[:, None] == np.arange(2 * LANES)[None, :] // OWN
    expand = jnp.asarray(np.concatenate([expand] * 3, axis=0), BF16)
    count = lit_count.reshape(1, IMAGES)
    inputs = (images, lit_mask, height, albedo, owner_column, altimetry, count, expand)
    cut = [(IMAGES, STRIP, 2 * LANES)] * 2 + [(STRIP, 2 * LANES)] * 2 + [(8, 2 * LANES)]
    cut += [a.shape for a in inputs[len(cut) :]]
    fields = f32(FIELDS, 2, STRIP, LANES)
    sent = pl.pallas_call(
        send_kernel,
        out_shape=fields,
        in_specs=[pl.BlockSpec(memory_space=pltpu.HBM)] * len(inputs),
        out_specs=VMEM,
        scratch_shapes=[pltpu.VMEM(shape, a.dtype) for shape, a in zip(cut, inputs)]
        + [pltpu.SemaphoreType.DMA((len(inputs),))],
        compiler_params=LARGE,
    )(*inputs)
    sent, count = lax.optimization_barrier((sent, count))
    received = lax.ppermute(sent, axes, across_cores)
    kept = call(keep_kernel, fields, *inputs[:-2], count, expand)
    near_small = call(near_small_kernel, f32(2, STRIP, LANES), kept, received)
    halo_small = lax.ppermute(near_small, axes, across_halves)
    near = call(near_kernel, f32(HEIGHT, STRIP, LANES), kept, received, near_small)
    halo = lax.ppermute(near, axes, across_halves)
    counts = call(count_kernel, f32(lon_count, 1, LANES), halo_small, near_small, near[:1, :8])
    counts, halo_small = lax.optimization_barrier((counts, halo_small))
    counts = lax.all_to_all(counts, "lon", 0, 0)
    message = f32(TILES, STRIP, LANES)
    window = f32(TILES, EXT, LANES)
    rows_of_bins = f32(TILES, BINS, LANES)
    z, aux, inter, intra = call(
        begin_kernel, (window, rows_of_bins, message, message), kept, received, halo_small
    )
    inter, intra = exchange(inter, intra)
    tables = constants()
    scratch = [pltpu.VMEM((TILES * STRIP, LANES), F32)] * 4
    z, inter, intra, alt, weight = call(
        first_kernel,
        (window, message, message, rows_of_bins, f32(BINS, LANES)),
        coef, counts, kept, received, halo, z, inter, intra, aux, *tables,
        scratch=scratch,
    )
    for _ in range(ITERS - 2):
        inter, intra = exchange(inter, intra)
        z, inter, intra = call(
            step_kernel,
            (window, message, message),
            coef, weight, kept, received, halo, z, inter, intra, aux, alt, *tables,
            scratch=scratch,
        )
    inter, intra = exchange(inter, intra)
    mine, inter, intra = call(
        last_kernel,
        (f32(2, EXT, LANES), f32(TILES - 1, RAD, LANES), f32(2, EXT, LANES)),
        coef, weight, kept, received, halo, z, inter, intra, aux, alt, *tables,
        scratch=[pltpu.VMEM((TILES, EXT, LANES), F32)] + scratch,
    )
    inter, intra = exchange(inter, intra)
    passed = call(forward_kernel, f32(2, RAD, LANES), inter)
    passed = lax.ppermute(passed, axes, across_cores)
    return call(place_kernel, f32(2 * STRIP, 2 * LANES), mine, intra, inter, passed)


def solution(mesh):
    return jax.shard_map(
        per_device,
        mesh=mesh,
        in_specs=(
            P("lon", "lat"),
            P("lon", "lat"),
            P(None, "lon", "lat"),
            P(None, "lon", "lat"),
            P(None, "lon", "lat"),
            P(),
            P("lon", "lat"),
            P("lon", "lat"),
        ),
        out_specs=P("lon", "lat"),
        check_vma=False,
    )
```

```python
import jax
import jax.numpy as jnp
import numpy as np
from jax import lax
from jax.experimental import pallas as pl
from jax.experimental.pallas import tpu as pltpu
from jax.sharding import PartitionSpec as P

IMAGES = 12
RAD = 16
OWN = 4
ITERS = 3
ROWS = 4096
COLUMNS = 1024
STEP_SIZE = 0.05
ALT_WEIGHT = 64.0
DATA_GAIN = 160.0
LUNAR_MIX = 0.6
SHARPNESS = 20.0

LANES = 128
STRIP = 32
EXT = STRIP + 2 * RAD
TILES = 5
FIELDS = 2 * IMAGES + 3
ALBEDO = 2 * IMAGES
HEIGHT = ALBEDO + 1
AUX = HEIGHT + 1
BINS = 16
EDGE = 24
DENOM = float(RAD * (RAD + 1) * (2 * RAD + 1)) / 3.0
TAP_SCALE = 1.0 / (DENOM * (2 * RAD + 1))
F32 = jnp.float32
BF16 = jnp.bfloat16
VMEM = pl.BlockSpec(memory_space=pltpu.VMEM)
PARAMS = pltpu.CompilerParams(vmem_limit_bytes=24 * 2**20)
LARGE = pltpu.CompilerParams(vmem_limit_bytes=58 * 2**20)


def band(offset, derivative):
    inside = np.abs(offset) <= RAD
    return np.where(inside, offset if derivative else 1, 0).astype(np.float32)


def constants():
    own = np.arange(STRIP)
    ext = np.arange(EXT) - RAD
    reach = ext[None, :] - own[:, None]
    rows = [band(reach, True), band(reach, False)]
    bins = np.arange(BINS)
    for shift in range(OWN):
        group = (ext[None, :] + shift) // OWN
        rows.append((group == bins[:, None]).astype(np.float32))
    down = np.concatenate(rows, axis=0)
    forward = np.concatenate([down] * 3, axis=1)
    back = own[None, :] - ext[:, None]
    spread = np.zeros((EXT, OWN * BINS), np.float32)
    for shift in range(OWN):
        hit = ((own[:, None] + shift) // OWN) == bins[None, :]
        spread[RAD : RAD + STRIP, shift * BINS : (shift + 1) * BINS] = hit
    filters = np.concatenate([band(back, True), band(back, False)], axis=1)
    backward = np.concatenate([filters, filters, spread, spread], axis=1)
    lane = np.arange(LANES)
    side = np.where(lane < LANES // 2, lane + LANES, lane - LANES)
    source = np.concatenate([lane, side])
    across = source[:, None] - lane[None, :]
    quads = (lane[:, None] // OWN == lane[None, :] // OWN).astype(np.float32)
    return [
        jnp.asarray(m, BF16)
        for m in (forward, backward, band(across, False), band(across, True), quads)
    ]


def pieces(value, count):
    out = []
    for _ in range(count - 1):
        part = value.astype(BF16)
        value = value - part.astype(F32)
        out.append(part)
    out.append(value.astype(BF16))
    return out


def dot(left, right):
    return jnp.dot(left, right, preferred_element_type=F32)


def with_sides(tiles):
    low = lax.broadcasted_iota(jnp.int32, tiles[0].shape, 1) < LANES // 2
    zero = jnp.zeros_like(tiles[0])
    rows = []
    for j, tile in enumerate(tiles):
        after = tiles[j + 1] if j + 1 < len(tiles) else zero
        before = tiles[j - 1] if j > 0 else zero
        rows.append(jnp.concatenate([tile, jnp.where(low, after, before)], axis=1))
    return jnp.concatenate(rows, axis=0)


def filter_lat(tiles, taps, count):
    total = None
    for part in pieces(with_sides(tiles), count):
        term = dot(part, taps)
        total = term if total is None else total + term
    return total


def place():
    lat = lax.axis_index("lat")
    return lat // 2, lat % 2


def own_tile(half, core, t):
    return half + 2 * core + t


def aux_fields(ref, rows_of, owner, altimetry, count, expand):
    bins = owner[0:OWN, :] - lax.axis_index("lon") * BINS
    shift = jnp.sum(bins, axis=0, keepdims=True).astype(F32)
    heights = dot(jnp.concatenate(pieces(altimetry[...], 3), axis=1), expand[...])
    heights = jnp.where(rows_of == 0, heights[0:8], heights[8:16])
    lit = jnp.concatenate([count[...].astype(F32), jnp.zeros((1, LANES - IMAGES), F32)], axis=1)
    for t in range(2):
        lanes = slice(t * LANES, (t + 1) * LANES)
        ref[AUX, t, 0:8] = heights[:, lanes]
        ref[AUX, t, 8:16] = jnp.broadcast_to(shift[:, lanes], (8, LANES))
        ref[AUX, t, 16:24] = jnp.broadcast_to(lit, (8, LANES))
        ref[AUX, t, 24:32] = jnp.zeros((8, LANES), F32)


def send_kernel(
    images_hbm, mask_hbm, height_hbm, albedo_hbm, owner_hbm, altimetry_hbm, count_hbm, expand_hbm,
    sent,
    images, lit_mask, height, albedo, owner, altimetry, count, expand, sems,
):
    other = 1 - place()[1]
    rows = pl.ds(pl.multiple_of(other * STRIP, STRIP), STRIP)
    copies = [
        pltpu.make_async_copy(source, target, sems.at[i])
        for i, (source, target) in enumerate(
            (
                (images_hbm.at[:, rows], images),
                (mask_hbm.at[:, rows], lit_mask),
                (height_hbm.at[rows], height),
                (albedo_hbm.at[rows], albedo),
                (owner_hbm.at[pl.ds(0, 8)], owner),
                (altimetry_hbm, altimetry),
                (count_hbm, count),
                (expand_hbm, expand),
            )
        )
    ]
    for copy in copies:
        copy.start()
    for copy in copies:
        copy.wait()
    aux_fields(sent, other, owner, altimetry, count, expand)
    for t in range(2):
        cols = pl.ds(t * LANES, LANES)
        for k in range(IMAGES):
            sent[k, t] = images[k, :, cols].astype(F32)
            sent[IMAGES + k, t] = lit_mask[k, :, cols].astype(F32)
        sent[ALBEDO, t] = albedo[:, cols]
        sent[HEIGHT, t] = height[:, cols]


def keep_kernel(images, lit_mask, height, albedo, owner, altimetry, count, expand, kept):
    core = place()[1]
    rows = pl.ds(pl.multiple_of(core * STRIP, STRIP), STRIP)
    aux_fields(kept, core, owner, altimetry, count, expand)
    for t in range(2):
        cols = pl.ds(t * LANES, LANES)
        for k in range(IMAGES):
            kept[k, t] = images[k, rows, cols].astype(F32)
            kept[IMAGES + k, t] = lit_mask[k, rows, cols].astype(F32)
        kept[ALBEDO, t] = albedo[rows, cols]
        kept[HEIGHT, t] = height[rows, cols]


def near_small_kernel(kept, received, near_small):
    half, core = place()
    for i, field in enumerate((HEIGHT, AUX)):
        near_small[i] = jnp.where(half != core, kept[field, 1 - half], received[field, 1 - half])
    near_small[1, 16:24] = kept[AUX, 0, 16:24] + received[AUX, 0, 16:24]


def near_kernel(kept, received, near_small, near):
    half, core = place()

    @pl.when(half != core)
    def _():
        near[...] = kept[0:HEIGHT, 1 - half]

    @pl.when(half == core)
    def _():
        near[...] = received[0:HEIGHT, 1 - half]


def count_kernel(halo_small, near_small, near, counts):
    total = halo_small[1, 16:17] + near_small[1, 16:17]
    counts[...] = jnp.broadcast_to(total[None], counts.shape)


def route(core, up, down, inter, intra):
    inter[...] = jnp.where(core == 0, up, down)
    intra[...] = jnp.where(core == 0, down, up)


def begin_kernel(kept, received, halo_small, z, aux, inter, intra):
    half, core = place()
    zero = jnp.zeros((TILES, RAD, LANES), F32)
    z[:, 0:RAD] = zero
    z[:, RAD + STRIP : EXT] = zero
    for t in range(2):
        for ref, at in ((kept, own_tile(half, core, t)), (received, own_tile(half, 1 - core, t))):
            z[at, RAD : RAD + STRIP] = ref[HEIGHT, t]
            aux[at] = ref[AUX, t, 0:BINS]
    far = (TILES - 1) * (1 - half)
    z[far, RAD : RAD + STRIP] = halo_small[0]
    aux[far] = halo_small[1, 0:BINS]
    alt = jnp.concatenate([aux[:, 0:8], jnp.zeros((TILES, 8, LANES), F32)], axis=1)
    up = jnp.concatenate([alt, z[:, RAD : 2 * RAD]], axis=1)
    route(core, up, z[:, STRIP:EXT], inter, intra)


def image_weights(counts):
    total = jnp.sum(counts[...], axis=0)
    weight = 2.0 * DATA_GAIN * float(ROWS * COLUMNS) / total
    image = lax.broadcasted_iota(jnp.int32, (BINS, LANES), 0)
    lane = lax.broadcasted_iota(jnp.int32, (BINS, LANES), 1)
    diagonal = jnp.where((image == lane) & (image < IMAGES), weight, 0.0)
    ones = jnp.ones((LANES, LANES), BF16)
    first, second, third = pieces(diagonal, 3)
    return dot(first, ones) + dot(second, ones) + dot(third, ones)


def image_term(coef, k, observed, lit, flat_part, flat_shade, mix_shade, slope_lon, slope_lat):
    steep = coef[2, k : k + 1] - coef[0, k : k + 1] * slope_lon - coef[1, k : k + 1] * slope_lat
    decay = jnp.exp(-jnp.abs(steep))
    whole = 1.0 + decay
    part = jnp.maximum(steep, 0.0) + jnp.log(whole)
    ratio = 1.0 / (part + coef[3, k : k + 1])
    gate = jnp.where(steep >= 0.0, 1.0, decay) / whole
    residual = lit * (part * (mix_shade * ratio + flat_shade) - observed)
    pull = residual * ((coef[4, k : k + 1] * (ratio * ratio) + flat_part) * gate)
    return pull, residual * part


def shades(albedo, slope_lon, slope_lat):
    inverse = lax.rsqrt(1.0 + slope_lon * slope_lon + slope_lat * slope_lat)
    flat_part = (1.0 - LUNAR_MIX) * inverse
    return inverse, (flat_part, flat_part * (albedo * (1.0 / SHARPNESS)), albedo * LUNAR_MIX)


def gradients(albedo, inverse, slope_lon, slope_lat, sums):
    sum_lon, sum_lat, sum_norm = sums
    bend = (1.0 - LUNAR_MIX) / SHARPNESS * (inverse * inverse * inverse) * sum_norm
    return albedo * (sum_lon - slope_lon * bend), albedo * (sum_lat - slope_lat * bend)


def add_image(sums, coef, k, pull, norm):
    terms = (coef[5, k : k + 1] * pull, coef[6, k : k + 1] * pull, norm)
    return terms if sums is None else tuple(a + b for a, b in zip(sums, terms))


def tile_rows(at):
    return pl.ds(pl.multiple_of(at * STRIP, STRIP), STRIP)


def image_tiles(kept, received, halo):
    half, core = place()
    for t in range(2):
        yield kept, (t,), tile_rows(own_tile(half, core, t))
        yield received, (t,), tile_rows(own_tile(half, 1 - core, t))
    yield halo, (), tile_rows((TILES - 1) * (1 - half))


def shift_rows(aux, j):
    return jnp.concatenate([aux[j, 8:16]] * 2, axis=0)


def slopes_and_misfit(surface, aux, alt, tables, slope_lon, slope_lat):
    forward, backward, smooth, slope, quads = tables
    tiles = range(TILES)
    stacked = jnp.concatenate(
        [jnp.concatenate(pieces(surface[j], 3), axis=0) for j in tiles], axis=1
    )
    down = dot(forward[...], stacked)

    def part(row, count, j):
        return down[row : row + count, j * LANES : (j + 1) * LANES]

    slope_lon[...] = TAP_SCALE * filter_lat([part(0, STRIP, j) for j in tiles], smooth[...], 3)
    slope_lat[...] = TAP_SCALE * filter_lat([part(STRIP, STRIP, j) for j in tiles], slope[...], 3)
    sums = []
    for j in tiles:
        shift = shift_rows(aux, j)
        chosen = part(2 * STRIP, BINS, j)
        for s in range(1, OWN):
            chosen = jnp.where(shift == float(s), part(2 * STRIP + s * BINS, BINS, j), chosen)
        sums.append(chosen)
    owner_sum = None
    for p in pieces(jnp.concatenate(sums, axis=0), 3):
        term = dot(p, quads[...])
        owner_sum = term if owner_sum is None else owner_sum + term
    gain = STEP_SIZE * 2.0 * ALT_WEIGHT / (OWN * OWN)
    rows = [slice(j * BINS, (j + 1) * BINS) for j in tiles]
    return [gain * alt[j] - (gain / (OWN * OWN)) * owner_sum[rows[j]] for j in tiles]


def contribute(surface, aux, misfit, grad_lon, grad_lat, tables, z_out):
    forward, backward, smooth, slope, quads = tables
    tiles = range(TILES)

    def field(ref):
        return [ref[j * STRIP : (j + 1) * STRIP] for j in tiles]

    scale = STEP_SIZE * TAP_SCALE
    from_lon = scale * filter_lat(field(grad_lon), smooth[...], 2)
    from_lat = scale * filter_lat(field(grad_lat), slope[...], 2)
    columns = []
    for j in tiles:
        rows = slice(j * STRIP, (j + 1) * STRIP)
        data = pieces(jnp.concatenate([from_lon[rows], from_lat[rows]], axis=0), 2)
        shift = shift_rows(aux, j)
        pull = [jnp.where(shift == float(s), misfit[j], 0.0) for s in range(OWN)]
        columns.append(jnp.concatenate(data + pieces(jnp.concatenate(pull, axis=0), 2), axis=0))
    spread = dot(backward[...], jnp.concatenate(columns, axis=1))
    for j in tiles:
        change = spread[:, j * LANES : (j + 1) * LANES]
        z_out[j, 0:RAD] = change[0:RAD]
        z_out[j, RAD : RAD + STRIP] = change[RAD : RAD + STRIP] + surface[j][RAD : RAD + STRIP]
        z_out[j, RAD + STRIP : EXT] = change[RAD + STRIP : EXT]


def arrived(inter, intra):
    core = place()[1]
    return (
        jnp.where(core == 0, inter[...], intra[...]),
        jnp.where(core == 0, intra[...], inter[...]),
    )


def surface_step(
    coef, weight, kept, received, halo, surface, aux, alt, tables, z_out, fields, misfit=None
):
    slope_lon, slope_lat, grad_lon, grad_lat = fields
    if misfit is None:
        misfit = slopes_and_misfit(surface, aux, alt, tables, slope_lon, slope_lat)
    for ref, index, rows in image_tiles(kept, received, halo):
        albedo, lon, lat = ref[(ALBEDO, *index)], slope_lon[rows], slope_lat[rows]
        inverse, shade = shades(albedo, lon, lat)
        sums = None
        for k in range(IMAGES):
            lit = weight[k : k + 1] * ref[(IMAGES + k, *index)]
            pull, norm = image_term(coef, k, ref[(k, *index)], lit, *shade, lon, lat)
            sums = add_image(sums, coef, k, pull, norm)
        grad_lon[rows], grad_lat[rows] = gradients(albedo, inverse, lon, lat, sums)
    contribute(surface, aux, misfit, grad_lon, grad_lat, tables, z_out)


def slope_kernel(z, inter, intra, aux, *refs):
    tables, (surface_out, alt_out, misfit_out, slope_lon, slope_lat) = refs[:5], refs[5:]
    above, below = arrived(inter, intra)
    alt = jnp.concatenate([aux[:, 0:8], below[:, 0:8]], axis=1)
    alt_out[...] = alt
    below = jnp.concatenate([jnp.zeros((TILES, RAD, LANES), F32), below[:, RAD:]], axis=1)
    surface = [z[j] + jnp.concatenate([above[j], below[j]], axis=0) for j in range(TILES)]
    for j, misfit in enumerate(slopes_and_misfit(surface, aux, alt, tables, slope_lon, slope_lat)):
        surface_out[j] = surface[j]
        misfit_out[j] = misfit


def first_kernel(coef, counts, kept, received, halo, surface, aux, misfit, slope_lon, slope_lat, *refs):
    tables, (z_out, inter_out, intra_out, weight_out), fields = refs[:5], refs[5:9], refs[9:]
    weight = image_weights(counts)
    weight_out[...] = weight
    surface_step(
        coef, weight, kept, received, halo, surface, aux, None, tables, z_out,
        (slope_lon, slope_lat, *fields), misfit,
    )
    route(place()[1], z_out[:, 0:STRIP], z_out[:, STRIP:EXT], inter_out, intra_out)


def step_kernel(coef, weight, kept, received, halo, z, inter, intra, aux, alt, *refs):
    tables, (z_out, inter_out, intra_out), fields = refs[:5], refs[5:8], refs[8:]
    above, below = arrived(inter, intra)
    surface = [z[j] + jnp.concatenate([above[j], below[j]], axis=0) for j in range(TILES)]
    surface_step(
        coef, weight[...], kept, received, halo, surface, aux, alt, tables, z_out, fields
    )
    route(place()[1], z_out[:, 0:STRIP], z_out[:, STRIP:EXT], inter_out, intra_out)


def last_kernel(coef, weight, kept, received, halo, z, inter, intra, aux, alt, *refs):
    tables, (inter_out, mine, intra_out, z_out), fields = refs[:5], refs[5:9], refs[9:]
    above, below = arrived(inter, intra)
    surface = [z[j] + jnp.concatenate([above[j], below[j]], axis=0) for j in range(TILES)]
    surface_step(
        coef, weight[...], kept, received, halo, surface, aux, alt, tables, z_out, fields
    )
    half, core = place()
    for t in range(TILES - 1):
        at = half + t
        inter_out[t] = jnp.where(core == 0, z_out[at, 0:EDGE], z_out[at, EXT - EDGE : EXT])
    for ref, side in ((mine, core), (intra_out, 1 - core)):
        for t in range(2):
            at = own_tile(half, side, t)
            ref[t] = jnp.where(core == 0, z_out[at, RAD:EXT], z_out[at, 0 : EXT - RAD])


def edge(inter, t, core):
    return jnp.where(core == 0, inter[t, EDGE - RAD : EDGE], inter[t, 0:RAD])


def forward_kernel(inter, forward):
    core = place()[1]
    for t in range(2):
        forward[t] = edge(inter, 2 * (1 - core) + t, core)


def place_kernel(mine, intra, inter, forward, out):
    core = place()[1]
    for t in range(2):
        upper = jnp.where(core == 0, mine[t], intra[t])
        lower = jnp.where(core == 0, intra[t], mine[t])
        direct = edge(inter, 2 * core + t, core)
        top = jnp.where(core == 0, direct, forward[t])
        bottom = jnp.where(core == 0, forward[t], direct)
        cols = slice(t * LANES, (t + 1) * LANES)
        out[0:RAD, cols] = upper[0:RAD] + top
        out[RAD : 2 * RAD, cols] = upper[RAD : 2 * RAD] + lower[0:RAD]
        out[2 * RAD : 3 * RAD, cols] = lower[RAD : 2 * RAD] + upper[2 * RAD : 3 * RAD]
        out[3 * RAD : EXT, cols] = lower[2 * RAD : 3 * RAD] + bottom


def f32(*shape):
    return jax.ShapeDtypeStruct(shape, F32)


def call(kernel, out_shape, *args, scratch=()):
    return pl.pallas_call(
        kernel,
        out_shape=out_shape,
        in_specs=[VMEM] * len(args),
        out_specs=jax.tree.map(lambda _: VMEM, out_shape),
        scratch_shapes=list(scratch),
        compiler_params=PARAMS,
    )(*args)


def per_device(height, albedo, images, lit_mask, lit_count, geometry, owner_column, altimetry):
    lon_count, lat_count = lax.axis_size("lon"), lax.axis_size("lat")
    axes = ("lon", "lat")
    sites = [(a, b) for a in range(lon_count) for b in range(lat_count)]

    def index(a, b):
        return (a % lon_count) * lat_count + b

    across_cores = [(index(a, b), index(a, b ^ 1)) for a, b in sites]
    across_halves = [(index(a, b), index(a, b ^ 2)) for a, b in sites]
    across_strips = [(index(a, b), index(a + 2 * (b % 2) - 1, b ^ 1)) for a, b in sites]

    def exchange(inter, intra):
        return lax.ppermute(inter, axes, across_strips), lax.ppermute(intra, axes, across_cores)

    sun_lon, sun_lat, sun_up, view = (geometry[:, i] for i in range(4))
    rows = [
        SHARPNESS * sun_lon,
        SHARPNESS * sun_lat,
        SHARPNESS * sun_up,
        SHARPNESS * view,
        (LUNAR_MIX * SHARPNESS * SHARPNESS) * view,
        -sun_lon,
        -sun_lat,
    ]
    coef = jnp.stack([jnp.broadcast_to(row[:, None], (IMAGES, LANES)) for row in rows])
    expand = np.arange(altimetry.shape[1])[:, None] == np.arange(2 * LANES)[None, :] // OWN
    expand = jnp.asarray(np.concatenate([expand] * 3, axis=0), BF16)
    count = lit_count.reshape(1, IMAGES)
    inputs = (images, lit_mask, height, albedo, owner_column, altimetry, count, expand)
    cut = [(IMAGES, STRIP, 2 * LANES)] * 2 + [(STRIP, 2 * LANES)] * 2 + [(8, 2 * LANES)]
    cut += [a.shape for a in inputs[len(cut) :]]
    fields = f32(FIELDS, 2, STRIP, LANES)
    sent = pl.pallas_call(
        send_kernel,
        out_shape=fields,
        in_specs=[pl.BlockSpec(memory_space=pltpu.HBM)] * len(inputs),
        out_specs=VMEM,
        scratch_shapes=[pltpu.VMEM(shape, a.dtype) for shape, a in zip(cut, inputs)]
        + [pltpu.SemaphoreType.DMA((len(inputs),))],
        compiler_params=LARGE,
    )(*inputs)
    sent, count = lax.optimization_barrier((sent, count))
    received = lax.ppermute(sent, axes, across_cores)
    kept = call(keep_kernel, fields, *inputs[:-2], count, expand)
    near_small = call(near_small_kernel, f32(2, STRIP, LANES), kept, received)
    halo_small = lax.ppermute(near_small, axes, across_halves)
    near = call(near_kernel, f32(HEIGHT, STRIP, LANES), kept, received, near_small)
    halo = lax.ppermute(near, axes, across_halves)
    counts = call(count_kernel, f32(lon_count, 1, LANES), halo_small, near_small, near[:1, :8])
    counts, halo_small = lax.optimization_barrier((counts, halo_small))
    counts = lax.all_to_all(counts, "lon", 0, 0)
    message = f32(TILES, STRIP, LANES)
    window = f32(TILES, EXT, LANES)
    rows_of_bins = f32(TILES, BINS, LANES)
    z, aux, inter, intra = call(
        begin_kernel, (window, rows_of_bins, message, message), kept, received, halo_small
    )
    inter, intra = exchange(inter, intra)
    tables = constants()
    scratch = [pltpu.VMEM((TILES * STRIP, LANES), F32)] * 4
    flat = f32(TILES * STRIP, LANES)
    surface, alt, misfit, *slopes = call(
        slope_kernel,
        (window, rows_of_bins, rows_of_bins, flat, flat),
        z, inter, intra, aux, *tables,
    )
    z, inter, intra, weight = call(
        first_kernel,
        (window, message, message, f32(BINS, LANES)),
        coef, counts, kept, received, halo, surface, aux, misfit, *slopes, *tables,
        scratch=scratch[:2],
    )
    for _ in range(ITERS - 2):
        inter, intra = exchange(inter, intra)
        z, inter, intra = call(
            step_kernel,
            (window, message, message),
            coef, weight, kept, received, halo, z, inter, intra, aux, alt, *tables,
            scratch=scratch,
        )
    inter, intra = exchange(inter, intra)
    part = f32(2, EXT - RAD, LANES)
    inter, mine, intra = call(
        last_kernel,
        (f32(TILES - 1, EDGE, LANES), part, part),
        coef, weight, kept, received, halo, z, inter, intra, aux, alt, *tables,
        scratch=[pltpu.VMEM((TILES, EXT, LANES), F32)] + scratch,
    )
    inter, intra = exchange(inter, intra)
    passed = call(forward_kernel, f32(2, RAD, LANES), inter)
    passed = lax.ppermute(passed, axes, across_cores)
    return call(place_kernel, f32(2 * STRIP, 2 * LANES), mine, intra, inter, passed)


def solution(mesh):
    return jax.shard_map(
        per_device,
        mesh=mesh,
        in_specs=(
            P("lon", "lat"),
            P("lon", "lat"),
            P(None, "lon", "lat"),
            P(None, "lon", "lat"),
            P(None, "lon", "lat"),
            P(),
            P("lon", "lat"),
            P("lon", "lat"),
        ),
        out_specs=P("lon", "lat"),
        check_vma=False,
    )
```

```python
import jax
import jax.numpy as jnp
import numpy as np
from jax import lax
from jax.experimental import pallas as pl
from jax.experimental.pallas import tpu as pltpu
from jax.sharding import PartitionSpec as P

IMAGES = 12
RAD = 16
OWN = 4
ITERS = 3
ROWS = 4096
COLUMNS = 1024
STEP_SIZE = 0.05
ALT_WEIGHT = 64.0
DATA_GAIN = 160.0
LUNAR_MIX = 0.6
SHARPNESS = 20.0

LANES = 128
STRIP = 32
EXT = STRIP + 2 * RAD
TILES = 5
FIELDS = 2 * IMAGES + 3
ALBEDO = 2 * IMAGES
HEIGHT = ALBEDO + 1
AUX = HEIGHT + 1
BINS = 16
EDGE = 24
DENOM = float(RAD * (RAD + 1) * (2 * RAD + 1)) / 3.0
TAP_SCALE = 1.0 / (DENOM * (2 * RAD + 1))
F32 = jnp.float32
BF16 = jnp.bfloat16
VMEM = pl.BlockSpec(memory_space=pltpu.VMEM)
PARAMS = pltpu.CompilerParams(vmem_limit_bytes=24 * 2**20)
LARGE = pltpu.CompilerParams(vmem_limit_bytes=58 * 2**20)


def band(offset, derivative):
    inside = np.abs(offset) <= RAD
    return np.where(inside, offset if derivative else 1, 0).astype(np.float32)


def constants():
    own = np.arange(STRIP)
    ext = np.arange(EXT) - RAD
    reach = ext[None, :] - own[:, None]
    rows = [band(reach, True), band(reach, False)]
    bins = np.arange(BINS)
    for shift in range(OWN):
        group = (ext[None, :] + shift) // OWN
        rows.append((group == bins[:, None]).astype(np.float32))
    down = np.concatenate(rows, axis=0)
    forward = np.concatenate([down] * 3, axis=1)
    back = own[None, :] - ext[:, None]
    spread = np.zeros((EXT, OWN * BINS), np.float32)
    for shift in range(OWN):
        hit = ((own[:, None] + shift) // OWN) == bins[None, :]
        spread[RAD : RAD + STRIP, shift * BINS : (shift + 1) * BINS] = hit
    filters = np.concatenate([band(back, True), band(back, False)], axis=1)
    backward = np.concatenate([filters, filters, spread, spread], axis=1)
    lane = np.arange(LANES)
    side = np.where(lane < LANES // 2, lane + LANES, lane - LANES)
    source = np.concatenate([lane, side])
    across = source[:, None] - lane[None, :]
    quads = (lane[:, None] // OWN == lane[None, :] // OWN).astype(np.float32)
    return [
        jnp.asarray(m, BF16)
        for m in (forward, backward, band(across, False), band(across, True), quads)
    ]


def pieces(value, count):
    out = []
    for _ in range(count - 1):
        part = value.astype(BF16)
        value = value - part.astype(F32)
        out.append(part)
    out.append(value.astype(BF16))
    return out


def dot(left, right):
    return jnp.dot(left, right, preferred_element_type=F32)


def with_sides(tiles):
    low = lax.broadcasted_iota(jnp.int32, tiles[0].shape, 1) < LANES // 2
    zero = jnp.zeros_like(tiles[0])
    rows = []
    for j, tile in enumerate(tiles):
        after = tiles[j + 1] if j + 1 < len(tiles) else zero
        before = tiles[j - 1] if j > 0 else zero
        rows.append(jnp.concatenate([tile, jnp.where(low, after, before)], axis=1))
    return jnp.concatenate(rows, axis=0)


def filter_lat(tiles, taps, count):
    total = None
    for part in pieces(with_sides(tiles), count):
        term = dot(part, taps)
        total = term if total is None else total + term
    return total


def place():
    lat = lax.axis_index("lat")
    return lat // 2, lat % 2


def own_tile(half, core, t):
    return half + 2 * core + t


def aux_fields(ref, rows_of, owner, altimetry, count, expand):
    bins = owner[0:OWN, :] - lax.axis_index("lon") * BINS
    shift = jnp.sum(bins, axis=0, keepdims=True).astype(F32)
    heights = dot(jnp.concatenate(pieces(altimetry[...], 3), axis=1), expand[...])
    heights = jnp.where(rows_of == 0, heights[0:8], heights[8:16])
    lit = jnp.concatenate([count[...].astype(F32), jnp.zeros((1, LANES - IMAGES), F32)], axis=1)
    for t in range(2):
        lanes = slice(t * LANES, (t + 1) * LANES)
        ref[AUX, t, 0:8] = heights[:, lanes]
        ref[AUX, t, 8:16] = jnp.broadcast_to(shift[:, lanes], (8, LANES))
        ref[AUX, t, 16:24] = jnp.broadcast_to(lit, (8, LANES))
        ref[AUX, t, 24:32] = jnp.zeros((8, LANES), F32)


def send_kernel(
    images_hbm, mask_hbm, height_hbm, albedo_hbm, owner_hbm, altimetry_hbm, count_hbm, expand_hbm,
    sent,
    images, lit_mask, height, albedo, owner, altimetry, count, expand, sems,
):
    other = 1 - place()[1]
    rows = pl.ds(pl.multiple_of(other * STRIP, STRIP), STRIP)
    copies = [
        pltpu.make_async_copy(source, target, sems.at[i])
        for i, (source, target) in enumerate(
            (
                (images_hbm.at[:, rows], images),
                (mask_hbm.at[:, rows], lit_mask),
                (height_hbm.at[rows], height),
                (albedo_hbm.at[rows], albedo),
                (owner_hbm.at[pl.ds(0, 8)], owner),
                (altimetry_hbm, altimetry),
                (count_hbm, count),
                (expand_hbm, expand),
            )
        )
    ]
    for copy in copies:
        copy.start()
    for copy in copies:
        copy.wait()
    aux_fields(sent, other, owner, altimetry, count, expand)
    for t in range(2):
        cols = pl.ds(t * LANES, LANES)
        for k in range(IMAGES):
            sent[k, t] = images[k, :, cols].astype(F32)
            sent[IMAGES + k, t] = lit_mask[k, :, cols].astype(F32)
        sent[ALBEDO, t] = albedo[:, cols]
        sent[HEIGHT, t] = height[:, cols]


def keep_kernel(images, lit_mask, height, albedo, owner, altimetry, count, expand, kept):
    core = place()[1]
    rows = pl.ds(pl.multiple_of(core * STRIP, STRIP), STRIP)
    aux_fields(kept, core, owner, altimetry, count, expand)
    for t in range(2):
        cols = pl.ds(t * LANES, LANES)
        for k in range(IMAGES):
            kept[k, t] = images[k, rows, cols].astype(F32)
            kept[IMAGES + k, t] = lit_mask[k, rows, cols].astype(F32)
        kept[ALBEDO, t] = albedo[rows, cols]
        kept[HEIGHT, t] = height[rows, cols]


def near_kernel(kept, received, near):
    half, core = place()

    @pl.when(half != core)
    def _():
        near[...] = kept[:, 1 - half]

    @pl.when(half == core)
    def _():
        near[...] = received[:, 1 - half]


def count_kernel(kept, received, near, counts):
    total = kept[AUX, 0, 16:17] + received[AUX, 0, 16:17]
    counts[...] = jnp.broadcast_to(total[None], counts.shape)


def route(core, up, down, inter, intra):
    inter[...] = jnp.where(core == 0, up, down)
    intra[...] = jnp.where(core == 0, down, up)


def begin_kernel(kept, received, halo, z, aux, inter, intra):
    half, core = place()
    zero = jnp.zeros((TILES, RAD, LANES), F32)
    z[:, 0:RAD] = zero
    z[:, RAD + STRIP : EXT] = zero
    for t in range(2):
        for ref, at in ((kept, own_tile(half, core, t)), (received, own_tile(half, 1 - core, t))):
            z[at, RAD : RAD + STRIP] = ref[HEIGHT, t]
            aux[at] = ref[AUX, t, 0:BINS]
    far = (TILES - 1) * (1 - half)
    z[far, RAD : RAD + STRIP] = halo[HEIGHT]
    aux[far] = halo[AUX, 0:BINS]
    alt = jnp.concatenate([aux[:, 0:8], jnp.zeros((TILES, 8, LANES), F32)], axis=1)
    up = jnp.concatenate([alt, z[:, RAD : 2 * RAD]], axis=1)
    route(core, up, z[:, STRIP:EXT], inter, intra)


def image_weights(counts):
    total = jnp.sum(counts[...], axis=0)
    weight = 2.0 * DATA_GAIN * float(ROWS * COLUMNS) / total
    image = lax.broadcasted_iota(jnp.int32, (BINS, LANES), 0)
    lane = lax.broadcasted_iota(jnp.int32, (BINS, LANES), 1)
    diagonal = jnp.where((image == lane) & (image < IMAGES), weight, 0.0)
    ones = jnp.ones((LANES, LANES), BF16)
    first, second, third = pieces(diagonal, 3)
    return dot(first, ones) + dot(second, ones) + dot(third, ones)


def image_term(coef, k, observed, lit, flat_part, flat_shade, mix_shade, slope_lon, slope_lat):
    steep = coef[2, k : k + 1] - coef[0, k : k + 1] * slope_lon - coef[1, k : k + 1] * slope_lat
    decay = jnp.exp(-jnp.abs(steep))
    whole = 1.0 + decay
    part = jnp.maximum(steep, 0.0) + jnp.log(whole)
    ratio = 1.0 / (part + coef[3, k : k + 1])
    gate = jnp.where(steep >= 0.0, 1.0, decay) / whole
    residual = lit * (part * (mix_shade * ratio + flat_shade) - observed)
    pull = residual * ((coef[4, k : k + 1] * (ratio * ratio) + flat_part) * gate)
    return pull, residual * part


def shades(albedo, slope_lon, slope_lat):
    inverse = lax.rsqrt(1.0 + slope_lon * slope_lon + slope_lat * slope_lat)
    flat_part = (1.0 - LUNAR_MIX) * inverse
    return inverse, (flat_part, flat_part * (albedo * (1.0 / SHARPNESS)), albedo * LUNAR_MIX)


def gradients(albedo, inverse, slope_lon, slope_lat, sums):
    sum_lon, sum_lat, sum_norm = sums
    bend = (1.0 - LUNAR_MIX) / SHARPNESS * (inverse * inverse * inverse) * sum_norm
    return albedo * (sum_lon - slope_lon * bend), albedo * (sum_lat - slope_lat * bend)


def add_image(sums, coef, k, pull, norm):
    terms = (coef[5, k : k + 1] * pull, coef[6, k : k + 1] * pull, norm)
    return terms if sums is None else tuple(a + b for a, b in zip(sums, terms))


def tile_rows(at):
    return pl.ds(pl.multiple_of(at * STRIP, STRIP), STRIP)


def image_tiles(kept, received, halo):
    half, core = place()
    for t in range(2):
        yield kept, (t,), tile_rows(own_tile(half, core, t))
        yield received, (t,), tile_rows(own_tile(half, 1 - core, t))
    yield halo, (), tile_rows((TILES - 1) * (1 - half))


def shift_rows(aux, j):
    return jnp.concatenate([aux[j, 8:16]] * 2, axis=0)


def slopes_and_misfit(surface, aux, alt, tables, slope_lon, slope_lat):
    forward, backward, smooth, slope, quads = tables
    tiles = range(TILES)
    stacked = jnp.concatenate(
        [jnp.concatenate(pieces(surface[j], 3), axis=0) for j in tiles], axis=1
    )
    down = dot(forward[...], stacked)

    def part(row, count, j):
        return down[row : row + count, j * LANES : (j + 1) * LANES]

    slope_lon[...] = TAP_SCALE * filter_lat([part(0, STRIP, j) for j in tiles], smooth[...], 3)
    slope_lat[...] = TAP_SCALE * filter_lat([part(STRIP, STRIP, j) for j in tiles], slope[...], 3)
    sums = []
    for j in tiles:
        shift = shift_rows(aux, j)
        chosen = part(2 * STRIP, BINS, j)
        for s in range(1, OWN):
            chosen = jnp.where(shift == float(s), part(2 * STRIP + s * BINS, BINS, j), chosen)
        sums.append(chosen)
    owner_sum = None
    for p in pieces(jnp.concatenate(sums, axis=0), 3):
        term = dot(p, quads[...])
        owner_sum = term if owner_sum is None else owner_sum + term
    gain = STEP_SIZE * 2.0 * ALT_WEIGHT / (OWN * OWN)
    rows = [slice(j * BINS, (j + 1) * BINS) for j in tiles]
    return [gain * alt[j] - (gain / (OWN * OWN)) * owner_sum[rows[j]] for j in tiles]


def contribute(surface, aux, misfit, grad_lon, grad_lat, tables, z_out):
    forward, backward, smooth, slope, quads = tables
    tiles = range(TILES)

    def field(ref):
        return [ref[j * STRIP : (j + 1) * STRIP] for j in tiles]

    scale = STEP_SIZE * TAP_SCALE
    from_lon = scale * filter_lat(field(grad_lon), smooth[...], 2)
    from_lat = scale * filter_lat(field(grad_lat), slope[...], 2)
    columns = []
    for j in tiles:
        rows = slice(j * STRIP, (j + 1) * STRIP)
        data = pieces(jnp.concatenate([from_lon[rows], from_lat[rows]], axis=0), 2)
        shift = shift_rows(aux, j)
        pull = [jnp.where(shift == float(s), misfit[j], 0.0) for s in range(OWN)]
        columns.append(jnp.concatenate(data + pieces(jnp.concatenate(pull, axis=0), 2), axis=0))
    spread = dot(backward[...], jnp.concatenate(columns, axis=1))
    for j in tiles:
        change = spread[:, j * LANES : (j + 1) * LANES]
        z_out[j, 0:RAD] = change[0:RAD]
        z_out[j, RAD : RAD + STRIP] = change[RAD : RAD + STRIP] + surface[j][RAD : RAD + STRIP]
        z_out[j, RAD + STRIP : EXT] = change[RAD + STRIP : EXT]


def arrived(inter, intra):
    core = place()[1]
    return (
        jnp.where(core == 0, inter[...], intra[...]),
        jnp.where(core == 0, intra[...], inter[...]),
    )


def surface_step(
    coef, weight, kept, received, halo, surface, aux, alt, tables, z_out, fields, misfit=None
):
    slope_lon, slope_lat, grad_lon, grad_lat = fields
    if misfit is None:
        misfit = slopes_and_misfit(surface, aux, alt, tables, slope_lon, slope_lat)
    for ref, index, rows in image_tiles(kept, received, halo):
        albedo, lon, lat = ref[(ALBEDO, *index)], slope_lon[rows], slope_lat[rows]
        inverse, shade = shades(albedo, lon, lat)
        sums = None
        for k in range(IMAGES):
            lit = weight[k : k + 1] * ref[(IMAGES + k, *index)]
            pull, norm = image_term(coef, k, ref[(k, *index)], lit, *shade, lon, lat)
            sums = add_image(sums, coef, k, pull, norm)
        grad_lon[rows], grad_lat[rows] = gradients(albedo, inverse, lon, lat, sums)
    contribute(surface, aux, misfit, grad_lon, grad_lat, tables, z_out)


def slope_kernel(z, inter, intra, aux, *refs):
    tables, (surface_out, alt_out, misfit_out, slope_lon, slope_lat) = refs[:5], refs[5:]
    above, below = arrived(inter, intra)
    alt = jnp.concatenate([aux[:, 0:8], below[:, 0:8]], axis=1)
    alt_out[...] = alt
    below = jnp.concatenate([jnp.zeros((TILES, RAD, LANES), F32), below[:, RAD:]], axis=1)
    surface = [z[j] + jnp.concatenate([above[j], below[j]], axis=0) for j in range(TILES)]
    for j, misfit in enumerate(slopes_and_misfit(surface, aux, alt, tables, slope_lon, slope_lat)):
        surface_out[j] = surface[j]
        misfit_out[j] = misfit


def first_kernel(coef, counts, kept, received, halo, surface, aux, misfit, slope_lon, slope_lat, *refs):
    tables, (z_out, inter_out, intra_out, weight_out), fields = refs[:5], refs[5:9], refs[9:]
    weight = image_weights(counts)
    weight_out[...] = weight
    surface_step(
        coef, weight, kept, received, halo, surface, aux, None, tables, z_out,
        (slope_lon, slope_lat, *fields), misfit,
    )
    route(place()[1], z_out[:, 0:STRIP], z_out[:, STRIP:EXT], inter_out, intra_out)


def step_kernel(coef, weight, kept, received, halo, z, inter, intra, aux, alt, *refs):
    tables, (z_out, inter_out, intra_out), fields = refs[:5], refs[5:8], refs[8:]
    above, below = arrived(inter, intra)
    surface = [z[j] + jnp.concatenate([above[j], below[j]], axis=0) for j in range(TILES)]
    surface_step(
        coef, weight[...], kept, received, halo, surface, aux, alt, tables, z_out, fields
    )
    route(place()[1], z_out[:, 0:STRIP], z_out[:, STRIP:EXT], inter_out, intra_out)


def last_kernel(coef, weight, kept, received, halo, z, inter, intra, aux, alt, *refs):
    tables, (inter_out, mine, intra_out, z_out), fields = refs[:5], refs[5:9], refs[9:]
    above, below = arrived(inter, intra)
    surface = [z[j] + jnp.concatenate([above[j], below[j]], axis=0) for j in range(TILES)]
    surface_step(
        coef, weight[...], kept, received, halo, surface, aux, alt, tables, z_out, fields
    )
    half, core = place()
    for t in range(TILES - 1):
        at = half + t
        inter_out[t] = jnp.where(core == 0, z_out[at, 0:EDGE], z_out[at, EXT - EDGE : EXT])
    for ref, side in ((mine, core), (intra_out, 1 - core)):
        for t in range(2):
            at = own_tile(half, side, t)
            ref[t] = jnp.where(core == 0, z_out[at, RAD:EXT], z_out[at, 0 : EXT - RAD])


def edge(inter, t, core):
    return jnp.where(core == 0, inter[t, EDGE - RAD : EDGE], inter[t, 0:RAD])


def forward_kernel(inter, forward):
    core = place()[1]
    for t in range(2):
        forward[t] = edge(inter, 2 * (1 - core) + t, core)


def place_kernel(mine, intra, inter, forward, out):
    core = place()[1]
    for t in range(2):
        upper = jnp.where(core == 0, mine[t], intra[t])
        lower = jnp.where(core == 0, intra[t], mine[t])
        direct = edge(inter, 2 * core + t, core)
        top = jnp.where(core == 0, direct, forward[t])
        bottom = jnp.where(core == 0, forward[t], direct)
        cols = slice(t * LANES, (t + 1) * LANES)
        out[0:RAD, cols] = upper[0:RAD] + top
        out[RAD : 2 * RAD, cols] = upper[RAD : 2 * RAD] + lower[0:RAD]
        out[2 * RAD : 3 * RAD, cols] = lower[RAD : 2 * RAD] + upper[2 * RAD : 3 * RAD]
        out[3 * RAD : EXT, cols] = lower[2 * RAD : 3 * RAD] + bottom


def f32(*shape):
    return jax.ShapeDtypeStruct(shape, F32)


def call(kernel, out_shape, *args, scratch=()):
    return pl.pallas_call(
        kernel,
        out_shape=out_shape,
        in_specs=[VMEM] * len(args),
        out_specs=jax.tree.map(lambda _: VMEM, out_shape),
        scratch_shapes=list(scratch),
        compiler_params=PARAMS,
    )(*args)


def per_device(height, albedo, images, lit_mask, lit_count, geometry, owner_column, altimetry):
    lon_count, lat_count = lax.axis_size("lon"), lax.axis_size("lat")
    axes = ("lon", "lat")
    sites = [(a, b) for a in range(lon_count) for b in range(lat_count)]

    def index(a, b):
        return (a % lon_count) * lat_count + b

    across_cores = [(index(a, b), index(a, b ^ 1)) for a, b in sites]
    across_halves = [(index(a, b), index(a, b ^ 2)) for a, b in sites]
    across_strips = [(index(a, b), index(a + 2 * (b % 2) - 1, b ^ 1)) for a, b in sites]

    def exchange(inter, intra):
        return lax.ppermute(inter, axes, across_strips), lax.ppermute(intra, axes, across_cores)

    sun_lon, sun_lat, sun_up, view = (geometry[:, i] for i in range(4))
    rows = [
        SHARPNESS * sun_lon,
        SHARPNESS * sun_lat,
        SHARPNESS * sun_up,
        SHARPNESS * view,
        (LUNAR_MIX * SHARPNESS * SHARPNESS) * view,
        -sun_lon,
        -sun_lat,
    ]
    coef = jnp.stack([jnp.broadcast_to(row[:, None], (IMAGES, LANES)) for row in rows])
    expand = np.arange(altimetry.shape[1])[:, None] == np.arange(2 * LANES)[None, :] // OWN
    expand = jnp.asarray(np.concatenate([expand] * 3, axis=0), BF16)
    count = lit_count.reshape(1, IMAGES)
    inputs = (images, lit_mask, height, albedo, owner_column, altimetry, count, expand)
    cut = [(IMAGES, STRIP, 2 * LANES)] * 2 + [(STRIP, 2 * LANES)] * 2 + [(8, 2 * LANES)]
    cut += [a.shape for a in inputs[len(cut) :]]
    fields = f32(FIELDS, 2, STRIP, LANES)
    sent = pl.pallas_call(
        send_kernel,
        out_shape=fields,
        in_specs=[pl.BlockSpec(memory_space=pltpu.HBM)] * len(inputs),
        out_specs=VMEM,
        scratch_shapes=[pltpu.VMEM(shape, a.dtype) for shape, a in zip(cut, inputs)]
        + [pltpu.SemaphoreType.DMA((len(inputs),))],
        compiler_params=LARGE,
    )(*inputs)
    sent, count = lax.optimization_barrier((sent, count))
    received = lax.ppermute(sent, axes, across_cores)
    kept = call(keep_kernel, fields, *inputs[:-2], count, expand)
    near = call(near_kernel, f32(FIELDS, STRIP, LANES), kept, received)
    halo = lax.ppermute(near, axes, across_halves)
    same_core = [[index(a, b) for a, b in sites if b % 2 == core] for core in range(2)]
    counts = call(count_kernel, f32(len(same_core[0]), 1, LANES), kept, received, near)
    counts = lax.all_to_all(counts, axes, 0, 0, axis_index_groups=same_core)
    message = f32(TILES, STRIP, LANES)
    window = f32(TILES, EXT, LANES)
    rows_of_bins = f32(TILES, BINS, LANES)
    z, aux, inter, intra = call(
        begin_kernel, (window, rows_of_bins, message, message), kept, received, halo
    )
    inter, intra = exchange(inter, intra)
    tables = constants()
    scratch = [pltpu.VMEM((TILES * STRIP, LANES), F32)] * 4
    flat = f32(TILES * STRIP, LANES)
    surface, alt, misfit, *slopes = call(
        slope_kernel,
        (window, rows_of_bins, rows_of_bins, flat, flat),
        z, inter, intra, aux, *tables,
    )
    z, inter, intra, weight = call(
        first_kernel,
        (window, message, message, f32(BINS, LANES)),
        coef, counts, kept, received, halo, surface, aux, misfit, *slopes, *tables,
        scratch=scratch[:2],
    )
    for _ in range(ITERS - 2):
        inter, intra = exchange(inter, intra)
        z, inter, intra = call(
            step_kernel,
            (window, message, message),
            coef, weight, kept, received, halo, z, inter, intra, aux, alt, *tables,
            scratch=scratch,
        )
    inter, intra = exchange(inter, intra)
    part = f32(2, EXT - RAD, LANES)
    inter, mine, intra = call(
        last_kernel,
        (f32(TILES - 1, EDGE, LANES), part, part),
        coef, weight, kept, received, halo, z, inter, intra, aux, alt, *tables,
        scratch=[pltpu.VMEM((TILES, EXT, LANES), F32)] + scratch,
    )
    inter, intra = exchange(inter, intra)
    passed = call(forward_kernel, f32(2, RAD, LANES), inter)
    passed = lax.ppermute(passed, axes, across_cores)
    return call(place_kernel, f32(2 * STRIP, 2 * LANES), mine, intra, inter, passed)


def solution(mesh):
    return jax.shard_map(
        per_device,
        mesh=mesh,
        in_specs=(
            P("lon", "lat"),
            P("lon", "lat"),
            P(None, "lon", "lat"),
            P(None, "lon", "lat"),
            P(None, "lon", "lat"),
            P(),
            P("lon", "lat"),
            P("lon", "lat"),
        ),
        out_specs=P("lon", "lat"),
        check_vma=False,
    )
```

```python
import jax
import jax.numpy as jnp
import numpy as np
from jax import lax
from jax.experimental import pallas as pl
from jax.experimental.pallas import tpu as pltpu
from jax.sharding import PartitionSpec as P

IMAGES = 12
RAD = 16
OWN = 4
ITERS = 3
ROWS = 4096
COLUMNS = 1024
STEP_SIZE = 0.05
ALT_WEIGHT = 64.0
DATA_GAIN = 160.0
LUNAR_MIX = 0.6
SHARPNESS = 20.0

LANES = 128
STRIP = 32
EXT = STRIP + 2 * RAD
TILES = 5
FIELDS = 2 * IMAGES + 3
ALBEDO = 2 * IMAGES
HEIGHT = ALBEDO + 1
AUX = HEIGHT + 1
BINS = 16
EDGE = 24
DENOM = float(RAD * (RAD + 1) * (2 * RAD + 1)) / 3.0
TAP_SCALE = 1.0 / (DENOM * (2 * RAD + 1))
F32 = jnp.float32
BF16 = jnp.bfloat16
VMEM = pl.BlockSpec(memory_space=pltpu.VMEM)
PARAMS = pltpu.CompilerParams(vmem_limit_bytes=24 * 2**20)
LARGE = pltpu.CompilerParams(vmem_limit_bytes=58 * 2**20)


def band(offset, derivative):
    inside = np.abs(offset) <= RAD
    return np.where(inside, offset if derivative else 1, 0).astype(np.float32)


def constants():
    own = np.arange(STRIP)
    ext = np.arange(EXT) - RAD
    reach = ext[None, :] - own[:, None]
    rows = [band(reach, True), band(reach, False)]
    bins = np.arange(BINS)
    for shift in range(OWN):
        group = (ext[None, :] + shift) // OWN
        rows.append((group == bins[:, None]).astype(np.float32))
    down = np.concatenate(rows, axis=0)
    forward = np.concatenate([down] * 3, axis=1)
    back = own[None, :] - ext[:, None]
    spread = np.zeros((EXT, OWN * BINS), np.float32)
    for shift in range(OWN):
        hit = ((own[:, None] + shift) // OWN) == bins[None, :]
        spread[RAD : RAD + STRIP, shift * BINS : (shift + 1) * BINS] = hit
    filters = np.concatenate([band(back, True), band(back, False)], axis=1)
    backward = np.concatenate([filters, filters, spread, spread], axis=1)
    lane = np.arange(LANES)
    side = np.where(lane < LANES // 2, lane + LANES, lane - LANES)
    source = np.concatenate([lane, side])
    across = source[:, None] - lane[None, :]
    quads = (lane[:, None] // OWN == lane[None, :] // OWN).astype(np.float32)
    return [
        jnp.asarray(m, BF16)
        for m in (forward, backward, band(across, False), band(across, True), quads)
    ]


def pieces(value, count):
    out = []
    for _ in range(count - 1):
        part = value.astype(BF16)
        value = value - part.astype(F32)
        out.append(part)
    out.append(value.astype(BF16))
    return out


def dot(left, right):
    return jnp.dot(left, right, preferred_element_type=F32)


def with_sides(tiles):
    low = lax.broadcasted_iota(jnp.int32, tiles[0].shape, 1) < LANES // 2
    zero = jnp.zeros_like(tiles[0])
    rows = []
    for j, tile in enumerate(tiles):
        after = tiles[j + 1] if j + 1 < len(tiles) else zero
        before = tiles[j - 1] if j > 0 else zero
        rows.append(jnp.concatenate([tile, jnp.where(low, after, before)], axis=1))
    return jnp.concatenate(rows, axis=0)


def filter_lat(tiles, taps, count):
    total = None
    for part in pieces(with_sides(tiles), count):
        term = dot(part, taps)
        total = term if total is None else total + term
    return total


def place():
    lat = lax.axis_index("lat")
    return lat // 2, lat % 2


def own_tile(half, core, t):
    return half + 2 * core + t


def aux_fields(ref, rows_of, owner, altimetry, count, expand):
    bins = owner[0:OWN, :] - lax.axis_index("lon") * BINS
    shift = jnp.sum(bins, axis=0, keepdims=True).astype(F32)
    heights = dot(jnp.concatenate(pieces(altimetry[...], 3), axis=1), expand[...])
    heights = jnp.where(rows_of == 0, heights[0:8], heights[8:16])
    lit = jnp.concatenate([count[...].astype(F32), jnp.zeros((1, LANES - IMAGES), F32)], axis=1)
    for t in range(2):
        lanes = slice(t * LANES, (t + 1) * LANES)
        ref[AUX, t, 0:8] = heights[:, lanes]
        ref[AUX, t, 8:16] = jnp.broadcast_to(shift[:, lanes], (8, LANES))
        ref[AUX, t, 16:24] = jnp.broadcast_to(lit, (8, LANES))
        ref[AUX, t, 24:32] = jnp.zeros((8, LANES), F32)


def send_kernel(
    images_hbm, mask_hbm, height_hbm, albedo_hbm, owner_hbm, altimetry_hbm, count_hbm, expand_hbm,
    sent_hbm,
    images, lit_mask, height, albedo, owner, altimetry, count, expand, sent, sems, out_sems,
):
    other = 1 - place()[1]
    rows = pl.ds(pl.multiple_of(other * STRIP, STRIP), STRIP)
    copies = [
        pltpu.make_async_copy(source, target, sems.at[i])
        for i, (source, target) in enumerate(
            (
                (images_hbm.at[:, rows], images),
                (mask_hbm.at[:, rows], lit_mask),
                (height_hbm.at[rows], height),
                (albedo_hbm.at[rows], albedo),
                (owner_hbm.at[pl.ds(0, 8)], owner),
                (altimetry_hbm, altimetry),
                (count_hbm, count),
                (expand_hbm, expand),
            )
        )
    ]
    for copy in copies:
        copy.start()
    parts = [pl.ds(0, IMAGES), pl.ds(IMAGES, IMAGES), pl.ds(ALBEDO, FIELDS - ALBEDO)]
    sends = [
        pltpu.make_async_copy(sent.at[part], sent_hbm.at[part], out_sems.at[i])
        for i, part in enumerate(parts)
    ]
    columns = [pl.ds(t * LANES, LANES) for t in range(2)]
    for i, source in enumerate((images, lit_mask)):
        copies[i].wait()
        for t, cols in enumerate(columns):
            for k in range(IMAGES):
                sent[i * IMAGES + k, t] = source[k, :, cols].astype(F32)
        sends[i].start()
    for copy in copies[2:]:
        copy.wait()
    aux_fields(sent, other, owner, altimetry, count, expand)
    for t, cols in enumerate(columns):
        sent[ALBEDO, t] = albedo[:, cols]
        sent[HEIGHT, t] = height[:, cols]
    sends[2].start()
    for send in sends:
        send.wait()


def keep_kernel(images, lit_mask, height, albedo, owner, altimetry, count, expand, kept):
    core = place()[1]
    rows = pl.ds(pl.multiple_of(core * STRIP, STRIP), STRIP)
    aux_fields(kept, core, owner, altimetry, count, expand)
    for t in range(2):
        cols = pl.ds(t * LANES, LANES)
        for k in range(IMAGES):
            kept[k, t] = images[k, rows, cols].astype(F32)
            kept[IMAGES + k, t] = lit_mask[k, rows, cols].astype(F32)
        kept[ALBEDO, t] = albedo[rows, cols]
        kept[HEIGHT, t] = height[rows, cols]


def near_kernel(kept, received, near):
    half, core = place()

    @pl.when(half != core)
    def _():
        near[...] = kept[:, 1 - half]

    @pl.when(half == core)
    def _():
        near[...] = received[:, 1 - half]


def count_kernel(kept, received, near, counts):
    total = kept[AUX, 0, 16:17] + received[AUX, 0, 16:17]
    counts[...] = jnp.broadcast_to(total[None], counts.shape)


def route(core, up, down, inter, intra):
    inter[...] = jnp.where(core == 0, up, down)
    intra[...] = jnp.where(core == 0, down, up)


def begin_kernel(kept, received, halo, z, aux, inter, intra):
    half, core = place()
    zero = jnp.zeros((TILES, RAD, LANES), F32)
    z[:, 0:RAD] = zero
    z[:, RAD + STRIP : EXT] = zero
    for t in range(2):
        for ref, at in ((kept, own_tile(half, core, t)), (received, own_tile(half, 1 - core, t))):
            z[at, RAD : RAD + STRIP] = ref[HEIGHT, t]
            aux[at] = ref[AUX, t, 0:BINS]
    far = (TILES - 1) * (1 - half)
    z[far, RAD : RAD + STRIP] = halo[HEIGHT]
    aux[far] = halo[AUX, 0:BINS]
    alt = jnp.concatenate([aux[:, 0:8], jnp.zeros((TILES, 8, LANES), F32)], axis=1)
    up = jnp.concatenate([alt, z[:, RAD : 2 * RAD]], axis=1)
    route(core, up, z[:, STRIP:EXT], inter, intra)


def image_weights(counts):
    total = jnp.sum(counts[...], axis=0)
    weight = 2.0 * DATA_GAIN * float(ROWS * COLUMNS) / total
    image = lax.broadcasted_iota(jnp.int32, (BINS, LANES), 0)
    lane = lax.broadcasted_iota(jnp.int32, (BINS, LANES), 1)
    diagonal = jnp.where((image == lane) & (image < IMAGES), weight, 0.0)
    ones = jnp.ones((LANES, LANES), BF16)
    first, second, third = pieces(diagonal, 3)
    return dot(first, ones) + dot(second, ones) + dot(third, ones)


def image_term(coef, k, observed, lit, flat_part, flat_shade, mix_shade, slope_lon, slope_lat):
    steep = coef[2, k : k + 1] - coef[0, k : k + 1] * slope_lon - coef[1, k : k + 1] * slope_lat
    decay = jnp.exp(-jnp.abs(steep))
    whole = 1.0 + decay
    part = jnp.maximum(steep, 0.0) + jnp.log(whole)
    ratio = 1.0 / (part + coef[3, k : k + 1])
    gate = jnp.where(steep >= 0.0, 1.0, decay) / whole
    residual = lit * (part * (mix_shade * ratio + flat_shade) - observed)
    pull = residual * ((coef[4, k : k + 1] * (ratio * ratio) + flat_part) * gate)
    return pull, residual * part


def shades(albedo, slope_lon, slope_lat):
    inverse = lax.rsqrt(1.0 + slope_lon * slope_lon + slope_lat * slope_lat)
    flat_part = (1.0 - LUNAR_MIX) * inverse
    return inverse, (flat_part, flat_part * (albedo * (1.0 / SHARPNESS)), albedo * LUNAR_MIX)


def gradients(albedo, inverse, slope_lon, slope_lat, sums):
    sum_lon, sum_lat, sum_norm = sums
    bend = (1.0 - LUNAR_MIX) / SHARPNESS * (inverse * inverse * inverse) * sum_norm
    return albedo * (sum_lon - slope_lon * bend), albedo * (sum_lat - slope_lat * bend)


def add_image(sums, coef, k, pull, norm):
    terms = (coef[5, k : k + 1] * pull, coef[6, k : k + 1] * pull, norm)
    return terms if sums is None else tuple(a + b for a, b in zip(sums, terms))


def tile_rows(at):
    return pl.ds(pl.multiple_of(at * STRIP, STRIP), STRIP)


def image_tiles(kept, received, halo):
    half, core = place()
    for t in range(2):
        yield kept, (t,), tile_rows(own_tile(half, core, t))
        yield received, (t,), tile_rows(own_tile(half, 1 - core, t))
    yield halo, (), tile_rows((TILES - 1) * (1 - half))


def shift_rows(aux, j):
    return jnp.concatenate([aux[j, 8:16]] * 2, axis=0)


def slopes_and_misfit(surface, aux, alt, tables, slope_lon, slope_lat):
    forward, backward, smooth, slope, quads = tables
    tiles = range(TILES)
    stacked = jnp.concatenate(
        [jnp.concatenate(pieces(surface[j], 3), axis=0) for j in tiles], axis=1
    )
    down = dot(forward[...], stacked)

    def part(row, count, j):
        return down[row : row + count, j * LANES : (j + 1) * LANES]

    slope_lon[...] = TAP_SCALE * filter_lat([part(0, STRIP, j) for j in tiles], smooth[...], 3)
    slope_lat[...] = TAP_SCALE * filter_lat([part(STRIP, STRIP, j) for j in tiles], slope[...], 3)
    sums = []
    for j in tiles:
        shift = shift_rows(aux, j)
        chosen = part(2 * STRIP, BINS, j)
        for s in range(1, OWN):
            chosen = jnp.where(shift == float(s), part(2 * STRIP + s * BINS, BINS, j), chosen)
        sums.append(chosen)
    owner_sum = None
    for p in pieces(jnp.concatenate(sums, axis=0), 3):
        term = dot(p, quads[...])
        owner_sum = term if owner_sum is None else owner_sum + term
    gain = STEP_SIZE * 2.0 * ALT_WEIGHT / (OWN * OWN)
    rows = [slice(j * BINS, (j + 1) * BINS) for j in tiles]
    return [gain * alt[j] - (gain / (OWN * OWN)) * owner_sum[rows[j]] for j in tiles]


def contribute(surface, aux, misfit, grad_lon, grad_lat, tables, z_out):
    forward, backward, smooth, slope, quads = tables
    tiles = range(TILES)

    def field(ref):
        return [ref[j * STRIP : (j + 1) * STRIP] for j in tiles]

    scale = STEP_SIZE * TAP_SCALE
    from_lon = scale * filter_lat(field(grad_lon), smooth[...], 2)
    from_lat = scale * filter_lat(field(grad_lat), slope[...], 2)
    columns = []
    for j in tiles:
        rows = slice(j * STRIP, (j + 1) * STRIP)
        data = pieces(jnp.concatenate([from_lon[rows], from_lat[rows]], axis=0), 2)
        shift = shift_rows(aux, j)
        pull = [jnp.where(shift == float(s), misfit[j], 0.0) for s in range(OWN)]
        columns.append(jnp.concatenate(data + pieces(jnp.concatenate(pull, axis=0), 2), axis=0))
    spread = dot(backward[...], jnp.concatenate(columns, axis=1))
    for j in tiles:
        change = spread[:, j * LANES : (j + 1) * LANES]
        z_out[j, 0:RAD] = change[0:RAD]
        z_out[j, RAD : RAD + STRIP] = change[RAD : RAD + STRIP] + surface[j][RAD : RAD + STRIP]
        z_out[j, RAD + STRIP : EXT] = change[RAD + STRIP : EXT]


def arrived(inter, intra):
    core = place()[1]
    return (
        jnp.where(core == 0, inter[...], intra[...]),
        jnp.where(core == 0, intra[...], inter[...]),
    )


def surface_step(
    coef, weight, kept, received, halo, surface, aux, alt, tables, z_out, fields, misfit=None
):
    slope_lon, slope_lat, grad_lon, grad_lat = fields
    if misfit is None:
        misfit = slopes_and_misfit(surface, aux, alt, tables, slope_lon, slope_lat)
    for ref, index, rows in image_tiles(kept, received, halo):
        albedo, lon, lat = ref[(ALBEDO, *index)], slope_lon[rows], slope_lat[rows]
        inverse, shade = shades(albedo, lon, lat)
        sums = None
        for k in range(IMAGES):
            lit = weight[k : k + 1] * ref[(IMAGES + k, *index)]
            pull, norm = image_term(coef, k, ref[(k, *index)], lit, *shade, lon, lat)
            sums = add_image(sums, coef, k, pull, norm)
        grad_lon[rows], grad_lat[rows] = gradients(albedo, inverse, lon, lat, sums)
    contribute(surface, aux, misfit, grad_lon, grad_lat, tables, z_out)


def slope_kernel(z, inter, intra, aux, *refs):
    tables, (surface_out, alt_out, misfit_out, slope_lon, slope_lat) = refs[:5], refs[5:]
    above, below = arrived(inter, intra)
    alt = jnp.concatenate([aux[:, 0:8], below[:, 0:8]], axis=1)
    alt_out[...] = alt
    below = jnp.concatenate([jnp.zeros((TILES, RAD, LANES), F32), below[:, RAD:]], axis=1)
    surface = [z[j] + jnp.concatenate([above[j], below[j]], axis=0) for j in range(TILES)]
    for j, misfit in enumerate(slopes_and_misfit(surface, aux, alt, tables, slope_lon, slope_lat)):
        surface_out[j] = surface[j]
        misfit_out[j] = misfit


def first_kernel(coef, counts, kept, received, halo, surface, aux, misfit, slope_lon, slope_lat, *refs):
    tables, (z_out, inter_out, intra_out, weight_out), fields = refs[:5], refs[5:9], refs[9:]
    weight = image_weights(counts)
    weight_out[...] = weight
    surface_step(
        coef, weight, kept, received, halo, surface, aux, None, tables, z_out,
        (slope_lon, slope_lat, *fields), misfit,
    )
    route(place()[1], z_out[:, 0:STRIP], z_out[:, STRIP:EXT], inter_out, intra_out)


def step_kernel(coef, weight, kept, received, halo, z, inter, intra, aux, alt, *refs):
    tables, (z_out, inter_out, intra_out), fields = refs[:5], refs[5:8], refs[8:]
    above, below = arrived(inter, intra)
    surface = [z[j] + jnp.concatenate([above[j], below[j]], axis=0) for j in range(TILES)]
    surface_step(
        coef, weight[...], kept, received, halo, surface, aux, alt, tables, z_out, fields
    )
    route(place()[1], z_out[:, 0:STRIP], z_out[:, STRIP:EXT], inter_out, intra_out)


def last_kernel(coef, weight, kept, received, halo, z, inter, intra, aux, alt, *refs):
    tables, (inter_out, mine, intra_out, z_out), fields = refs[:5], refs[5:9], refs[9:]
    above, below = arrived(inter, intra)
    surface = [z[j] + jnp.concatenate([above[j], below[j]], axis=0) for j in range(TILES)]
    surface_step(
        coef, weight[...], kept, received, halo, surface, aux, alt, tables, z_out, fields
    )
    half, core = place()
    for t in range(TILES - 1):
        at = half + t
        inter_out[t] = jnp.where(core == 0, z_out[at, 0:EDGE], z_out[at, EXT - EDGE : EXT])
    for ref, side in ((mine, core), (intra_out, 1 - core)):
        for t in range(2):
            at = own_tile(half, side, t)
            ref[t] = jnp.where(core == 0, z_out[at, RAD:EXT], z_out[at, 0 : EXT - RAD])


def edge(inter, t, core):
    return jnp.where(core == 0, inter[t, EDGE - RAD : EDGE], inter[t, 0:RAD])


def forward_kernel(inter, forward):
    core = place()[1]
    for t in range(2):
        forward[t] = edge(inter, 2 * (1 - core) + t, core)


def place_kernel(mine, intra, inter, forward, out):
    core = place()[1]
    for t in range(2):
        upper = jnp.where(core == 0, mine[t], intra[t])
        lower = jnp.where(core == 0, intra[t], mine[t])
        direct = edge(inter, 2 * core + t, core)
        top = jnp.where(core == 0, direct, forward[t])
        bottom = jnp.where(core == 0, forward[t], direct)
        cols = slice(t * LANES, (t + 1) * LANES)
        out[0:RAD, cols] = upper[0:RAD] + top
        out[RAD : 2 * RAD, cols] = upper[RAD : 2 * RAD] + lower[0:RAD]
        out[2 * RAD : 3 * RAD, cols] = lower[RAD : 2 * RAD] + upper[2 * RAD : 3 * RAD]
        out[3 * RAD : EXT, cols] = lower[2 * RAD : 3 * RAD] + bottom


def f32(*shape):
    return jax.ShapeDtypeStruct(shape, F32)


def call(kernel, out_shape, *args, scratch=()):
    return pl.pallas_call(
        kernel,
        out_shape=out_shape,
        in_specs=[VMEM] * len(args),
        out_specs=jax.tree.map(lambda _: VMEM, out_shape),
        scratch_shapes=list(scratch),
        compiler_params=PARAMS,
    )(*args)


def per_device(height, albedo, images, lit_mask, lit_count, geometry, owner_column, altimetry):
    lon_count, lat_count = lax.axis_size("lon"), lax.axis_size("lat")
    axes = ("lon", "lat")
    sites = [(a, b) for a in range(lon_count) for b in range(lat_count)]

    def index(a, b):
        return (a % lon_count) * lat_count + b

    across_cores = [(index(a, b), index(a, b ^ 1)) for a, b in sites]
    across_halves = [(index(a, b), index(a, b ^ 2)) for a, b in sites]
    across_strips = [(index(a, b), index(a + 2 * (b % 2) - 1, b ^ 1)) for a, b in sites]

    def exchange(inter, intra):
        return lax.ppermute(inter, axes, across_strips), lax.ppermute(intra, axes, across_cores)

    sun_lon, sun_lat, sun_up, view = (geometry[:, i] for i in range(4))
    rows = [
        SHARPNESS * sun_lon,
        SHARPNESS * sun_lat,
        SHARPNESS * sun_up,
        SHARPNESS * view,
        (LUNAR_MIX * SHARPNESS * SHARPNESS) * view,
        -sun_lon,
        -sun_lat,
    ]
    coef = jnp.stack([jnp.broadcast_to(row[:, None], (IMAGES, LANES)) for row in rows])
    expand = np.arange(altimetry.shape[1])[:, None] == np.arange(2 * LANES)[None, :] // OWN
    expand = jnp.asarray(np.concatenate([expand] * 3, axis=0), BF16)
    count = lit_count.reshape(1, IMAGES)
    inputs = (images, lit_mask, height, albedo, owner_column, altimetry, count, expand)
    cut = [(IMAGES, STRIP, 2 * LANES)] * 2 + [(STRIP, 2 * LANES)] * 2 + [(8, 2 * LANES)]
    cut += [a.shape for a in inputs[len(cut) :]]
    fields = f32(FIELDS, 2, STRIP, LANES)
    sent = pl.pallas_call(
        send_kernel,
        out_shape=fields,
        in_specs=[pl.BlockSpec(memory_space=pltpu.HBM)] * len(inputs),
        out_specs=pl.BlockSpec(memory_space=pltpu.HBM),
        scratch_shapes=[pltpu.VMEM(shape, a.dtype) for shape, a in zip(cut, inputs)]
        + [pltpu.VMEM(fields.shape, F32)]
        + [pltpu.SemaphoreType.DMA((len(inputs),)), pltpu.SemaphoreType.DMA((3,))],
        compiler_params=LARGE,
    )(*inputs)
    sent, count = lax.optimization_barrier((sent, count))
    received = lax.ppermute(sent, axes, across_cores)
    kept = call(keep_kernel, fields, *inputs[:-2], count, expand)
    near = call(near_kernel, f32(FIELDS, STRIP, LANES), kept, received)
    halo = lax.ppermute(near, axes, across_halves)
    same_core = [[index(a, b) for a, b in sites if b % 2 == core] for core in range(2)]
    counts = call(count_kernel, f32(len(same_core[0]), 1, LANES), kept, received, near)
    counts = lax.all_to_all(counts, axes, 0, 0, axis_index_groups=same_core)
    message = f32(TILES, STRIP, LANES)
    window = f32(TILES, EXT, LANES)
    rows_of_bins = f32(TILES, BINS, LANES)
    z, aux, inter, intra = call(
        begin_kernel, (window, rows_of_bins, message, message), kept, received, halo
    )
    inter, intra = exchange(inter, intra)
    tables = constants()
    scratch = [pltpu.VMEM((TILES * STRIP, LANES), F32)] * 4
    flat = f32(TILES * STRIP, LANES)
    surface, alt, misfit, *slopes = call(
        slope_kernel,
        (window, rows_of_bins, rows_of_bins, flat, flat),
        z, inter, intra, aux, *tables,
    )
    z, inter, intra, weight = call(
        first_kernel,
        (window, message, message, f32(BINS, LANES)),
        coef, counts, kept, received, halo, surface, aux, misfit, *slopes, *tables,
        scratch=scratch[:2],
    )
    for _ in range(ITERS - 2):
        inter, intra = exchange(inter, intra)
        z, inter, intra = call(
            step_kernel,
            (window, message, message),
            coef, weight, kept, received, halo, z, inter, intra, aux, alt, *tables,
            scratch=scratch,
        )
    inter, intra = exchange(inter, intra)
    part = f32(2, EXT - RAD, LANES)
    inter, mine, intra = call(
        last_kernel,
        (f32(TILES - 1, EDGE, LANES), part, part),
        coef, weight, kept, received, halo, z, inter, intra, aux, alt, *tables,
        scratch=[pltpu.VMEM((TILES, EXT, LANES), F32)] + scratch,
    )
    inter, intra = exchange(inter, intra)
    passed = call(forward_kernel, f32(2, RAD, LANES), inter)
    passed = lax.ppermute(passed, axes, across_cores)
    return call(place_kernel, f32(2 * STRIP, 2 * LANES), mine, intra, inter, passed)


def solution(mesh):
    return jax.shard_map(
        per_device,
        mesh=mesh,
        in_specs=(
            P("lon", "lat"),
            P("lon", "lat"),
            P(None, "lon", "lat"),
            P(None, "lon", "lat"),
            P(None, "lon", "lat"),
            P(),
            P("lon", "lat"),
            P("lon", "lat"),
        ),
        out_specs=P("lon", "lat"),
        check_vma=False,
    )
```

```python
import jax
import jax.numpy as jnp
import numpy as np
from jax import lax
from jax.experimental import pallas as pl
from jax.experimental.pallas import tpu as pltpu
from jax.sharding import PartitionSpec as P

IMAGES = 12
RAD = 16
OWN = 4
ITERS = 3
ROWS = 4096
COLUMNS = 1024
STEP_SIZE = 0.05
ALT_WEIGHT = 64.0
DATA_GAIN = 160.0
LUNAR_MIX = 0.6
SHARPNESS = 20.0

LANES = 128
STRIP = 32
EXT = STRIP + 2 * RAD
TILES = 5
FIELDS = 2 * IMAGES + 3
ALBEDO = 2 * IMAGES
HEIGHT = ALBEDO + 1
AUX = HEIGHT + 1
BINS = 16
EDGE = 24
DENOM = float(RAD * (RAD + 1) * (2 * RAD + 1)) / 3.0
TAP_SCALE = 1.0 / (DENOM * (2 * RAD + 1))
F32 = jnp.float32
BF16 = jnp.bfloat16
VMEM = pl.BlockSpec(memory_space=pltpu.VMEM)
PARAMS = pltpu.CompilerParams(vmem_limit_bytes=24 * 2**20)
LARGE = pltpu.CompilerParams(vmem_limit_bytes=58 * 2**20)


def band(offset, derivative):
    inside = np.abs(offset) <= RAD
    return np.where(inside, offset if derivative else 1, 0).astype(np.float32)


def constants():
    own = np.arange(STRIP)
    ext = np.arange(EXT) - RAD
    reach = ext[None, :] - own[:, None]
    rows = [band(reach, True), band(reach, False)]
    bins = np.arange(BINS)
    for shift in range(OWN):
        group = (ext[None, :] + shift) // OWN
        rows.append((group == bins[:, None]).astype(np.float32))
    down = np.concatenate(rows, axis=0)
    forward = np.concatenate([down] * 3, axis=1)
    back = own[None, :] - ext[:, None]
    spread = np.zeros((EXT, OWN * BINS), np.float32)
    for shift in range(OWN):
        hit = ((own[:, None] + shift) // OWN) == bins[None, :]
        spread[RAD : RAD + STRIP, shift * BINS : (shift + 1) * BINS] = hit
    filters = np.concatenate([band(back, True), band(back, False)], axis=1)
    backward = np.concatenate([filters, filters, spread, spread], axis=1)
    lane = np.arange(LANES)
    side = np.where(lane < LANES // 2, lane + LANES, lane - LANES)
    source = np.concatenate([lane, side])
    across = source[:, None] - lane[None, :]
    quads = (lane[:, None] // OWN == lane[None, :] // OWN).astype(np.float32)
    return [
        jnp.asarray(m, BF16)
        for m in (forward, backward, band(across, False), band(across, True), quads)
    ]


def pieces(value, count):
    out = []
    for _ in range(count - 1):
        part = value.astype(BF16)
        value = value - part.astype(F32)
        out.append(part)
    out.append(value.astype(BF16))
    return out


def dot(left, right):
    return jnp.dot(left, right, preferred_element_type=F32)


def with_sides(tiles):
    low = lax.broadcasted_iota(jnp.int32, tiles[0].shape, 1) < LANES // 2
    zero = jnp.zeros_like(tiles[0])
    rows = []
    for j, tile in enumerate(tiles):
        after = tiles[j + 1] if j + 1 < len(tiles) else zero
        before = tiles[j - 1] if j > 0 else zero
        rows.append(jnp.concatenate([tile, jnp.where(low, after, before)], axis=1))
    return jnp.concatenate(rows, axis=0)


def filter_lat(tiles, taps, count):
    sums = dot(jnp.concatenate(pieces(with_sides(tiles), count), axis=0), taps)
    size = sums.shape[0] // count
    total = sums[0:size]
    for i in range(1, count):
        total = total + sums[i * size : (i + 1) * size]
    return total


def place():
    lat = lax.axis_index("lat")
    return lat // 2, lat % 2


def own_tile(half, core, t):
    return half + 2 * core + t


def aux_fields(ref, rows_of, owner, altimetry, count, expand):
    bins = owner[0:OWN, :] - lax.axis_index("lon") * BINS
    shift = jnp.sum(bins, axis=0, keepdims=True).astype(F32)
    heights = dot(jnp.concatenate(pieces(altimetry[...], 3), axis=1), expand[...])
    heights = jnp.where(rows_of == 0, heights[0:8], heights[8:16])
    lit = jnp.concatenate([count[...].astype(F32), jnp.zeros((1, LANES - IMAGES), F32)], axis=1)
    for t in range(2):
        lanes = slice(t * LANES, (t + 1) * LANES)
        ref[AUX, t, 0:8] = heights[:, lanes]
        ref[AUX, t, 8:16] = jnp.broadcast_to(shift[:, lanes], (8, LANES))
        ref[AUX, t, 16:24] = jnp.broadcast_to(lit, (8, LANES))
        ref[AUX, t, 24:32] = jnp.zeros((8, LANES), F32)


def send_kernel(
    images_hbm, mask_hbm, height_hbm, albedo_hbm, owner_hbm, altimetry_hbm, count_hbm, expand_hbm,
    sent_hbm,
    images, lit_mask, height, albedo, owner, altimetry, count, expand, sent, sems, out_sems,
):
    other = 1 - place()[1]
    rows = pl.ds(pl.multiple_of(other * STRIP, STRIP), STRIP)
    copies = [
        pltpu.make_async_copy(source, target, sems.at[i])
        for i, (source, target) in enumerate(
            (
                (images_hbm.at[:, rows], images),
                (mask_hbm.at[:, rows], lit_mask),
                (height_hbm.at[rows], height),
                (albedo_hbm.at[rows], albedo),
                (owner_hbm.at[pl.ds(0, 8)], owner),
                (altimetry_hbm, altimetry),
                (count_hbm, count),
                (expand_hbm, expand),
            )
        )
    ]
    for copy in copies:
        copy.start()
    parts = [pl.ds(0, IMAGES), pl.ds(IMAGES, IMAGES), pl.ds(ALBEDO, FIELDS - ALBEDO)]
    sends = [
        pltpu.make_async_copy(sent.at[part], sent_hbm.at[part], out_sems.at[i])
        for i, part in enumerate(parts)
    ]
    columns = [pl.ds(t * LANES, LANES) for t in range(2)]
    for i, source in enumerate((images, lit_mask)):
        copies[i].wait()
        for t, cols in enumerate(columns):
            for k in range(IMAGES):
                sent[i * IMAGES + k, t] = source[k, :, cols].astype(F32)
        sends[i].start()
    for copy in copies[2:]:
        copy.wait()
    aux_fields(sent, other, owner, altimetry, count, expand)
    for t, cols in enumerate(columns):
        sent[ALBEDO, t] = albedo[:, cols]
        sent[HEIGHT, t] = height[:, cols]
    sends[2].start()
    for send in sends:
        send.wait()


def keep_kernel(images, lit_mask, height, albedo, owner, altimetry, count, expand, kept):
    core = place()[1]
    rows = pl.ds(pl.multiple_of(core * STRIP, STRIP), STRIP)
    aux_fields(kept, core, owner, altimetry, count, expand)
    for t in range(2):
        cols = pl.ds(t * LANES, LANES)
        for k in range(IMAGES):
            kept[k, t] = images[k, rows, cols].astype(F32)
            kept[IMAGES + k, t] = lit_mask[k, rows, cols].astype(F32)
        kept[ALBEDO, t] = albedo[rows, cols]
        kept[HEIGHT, t] = height[rows, cols]


def near_kernel(kept, received, near):
    half, core = place()

    @pl.when(half != core)
    def _():
        near[...] = kept[:, 1 - half]

    @pl.when(half == core)
    def _():
        near[...] = received[:, 1 - half]


def count_kernel(kept, received, near, counts):
    total = kept[AUX, 0, 16:17] + received[AUX, 0, 16:17]
    counts[...] = jnp.broadcast_to(total[None], counts.shape)


def route(core, up, down, inter, intra):
    inter[...] = jnp.where(core == 0, up, down)
    intra[...] = jnp.where(core == 0, down, up)


def begin_kernel(kept, received, halo, z, aux, inter, intra):
    half, core = place()
    zero = jnp.zeros((TILES, RAD, LANES), F32)
    z[:, 0:RAD] = zero
    z[:, RAD + STRIP : EXT] = zero
    for t in range(2):
        for ref, at in ((kept, own_tile(half, core, t)), (received, own_tile(half, 1 - core, t))):
            z[at, RAD : RAD + STRIP] = ref[HEIGHT, t]
            aux[at] = ref[AUX, t, 0:BINS]
    far = (TILES - 1) * (1 - half)
    z[far, RAD : RAD + STRIP] = halo[HEIGHT]
    aux[far] = halo[AUX, 0:BINS]
    alt = jnp.concatenate([aux[:, 0:8], jnp.zeros((TILES, 8, LANES), F32)], axis=1)
    up = jnp.concatenate([alt, z[:, RAD : 2 * RAD]], axis=1)
    route(core, up, z[:, STRIP:EXT], inter, intra)


def image_weights(counts):
    total = jnp.sum(counts[...], axis=0)
    weight = 2.0 * DATA_GAIN * float(ROWS * COLUMNS) / total
    image = lax.broadcasted_iota(jnp.int32, (BINS, LANES), 0)
    lane = lax.broadcasted_iota(jnp.int32, (BINS, LANES), 1)
    diagonal = jnp.where((image == lane) & (image < IMAGES), weight, 0.0)
    ones = jnp.ones((LANES, LANES), BF16)
    first, second, third = pieces(diagonal, 3)
    return dot(first, ones) + dot(second, ones) + dot(third, ones)


def image_term(coef, k, observed, lit, flat_part, flat_shade, mix_shade, slope_lon, slope_lat):
    steep = coef[2, k : k + 1] - coef[0, k : k + 1] * slope_lon - coef[1, k : k + 1] * slope_lat
    decay = jnp.exp(-jnp.abs(steep))
    whole = 1.0 + decay
    part = jnp.maximum(steep, 0.0) + jnp.log(whole)
    ratio = 1.0 / (part + coef[3, k : k + 1])
    gate = jnp.where(steep >= 0.0, 1.0, decay) / whole
    residual = lit * (part * (mix_shade * ratio + flat_shade) - observed)
    pull = residual * ((coef[4, k : k + 1] * (ratio * ratio) + flat_part) * gate)
    return pull, residual * part


def shades(albedo, slope_lon, slope_lat):
    inverse = lax.rsqrt(1.0 + slope_lon * slope_lon + slope_lat * slope_lat)
    flat_part = (1.0 - LUNAR_MIX) * inverse
    return inverse, (flat_part, flat_part * (albedo * (1.0 / SHARPNESS)), albedo * LUNAR_MIX)


def gradients(albedo, inverse, slope_lon, slope_lat, sums):
    sum_lon, sum_lat, sum_norm = sums
    bend = (1.0 - LUNAR_MIX) / SHARPNESS * (inverse * inverse * inverse) * sum_norm
    return albedo * (sum_lon - slope_lon * bend), albedo * (sum_lat - slope_lat * bend)


def add_image(sums, coef, k, pull, norm):
    terms = (coef[5, k : k + 1] * pull, coef[6, k : k + 1] * pull, norm)
    return terms if sums is None else tuple(a + b for a, b in zip(sums, terms))


def tile_rows(at):
    return pl.ds(pl.multiple_of(at * STRIP, STRIP), STRIP)


def image_tiles(kept, received, halo):
    half, core = place()
    for t in range(2):
        yield kept, (t,), tile_rows(own_tile(half, core, t))
        yield received, (t,), tile_rows(own_tile(half, 1 - core, t))
    yield halo, (), tile_rows((TILES - 1) * (1 - half))


def shift_rows(aux, j):
    return jnp.concatenate([aux[j, 8:16]] * 2, axis=0)


def slopes_and_misfit(surface, aux, alt, tables, slope_lon, slope_lat):
    forward, backward, smooth, slope, quads = tables
    tiles = range(TILES)
    stacked = jnp.concatenate(
        [jnp.concatenate(pieces(surface[j], 3), axis=0) for j in tiles], axis=1
    )
    down = dot(forward[...], stacked)

    def part(row, count, j):
        return down[row : row + count, j * LANES : (j + 1) * LANES]

    slope_lon[...] = TAP_SCALE * filter_lat([part(0, STRIP, j) for j in tiles], smooth[...], 2)
    slope_lat[...] = TAP_SCALE * filter_lat([part(STRIP, STRIP, j) for j in tiles], slope[...], 2)
    sums = []
    for j in tiles:
        shift = shift_rows(aux, j)
        chosen = part(2 * STRIP, BINS, j)
        for s in range(1, OWN):
            chosen = jnp.where(shift == float(s), part(2 * STRIP + s * BINS, BINS, j), chosen)
        sums.append(chosen)
    owner_sum = None
    for p in pieces(jnp.concatenate(sums, axis=0), 3):
        term = dot(p, quads[...])
        owner_sum = term if owner_sum is None else owner_sum + term
    gain = STEP_SIZE * 2.0 * ALT_WEIGHT / (OWN * OWN)
    rows = [slice(j * BINS, (j + 1) * BINS) for j in tiles]
    return [gain * alt[j] - (gain / (OWN * OWN)) * owner_sum[rows[j]] for j in tiles]


def contribute(surface, aux, misfit, grad_lon, grad_lat, tables, z_out):
    forward, backward, smooth, slope, quads = tables
    tiles = range(TILES)

    def field(ref):
        return [ref[j * STRIP : (j + 1) * STRIP] for j in tiles]

    scale = STEP_SIZE * TAP_SCALE
    from_lon = scale * filter_lat(field(grad_lon), smooth[...], 2)
    from_lat = scale * filter_lat(field(grad_lat), slope[...], 2)
    columns = []
    for j in tiles:
        rows = slice(j * STRIP, (j + 1) * STRIP)
        data = pieces(jnp.concatenate([from_lon[rows], from_lat[rows]], axis=0), 2)
        shift = shift_rows(aux, j)
        pull = [jnp.where(shift == float(s), misfit[j], 0.0) for s in range(OWN)]
        columns.append(jnp.concatenate(data + pieces(jnp.concatenate(pull, axis=0), 2), axis=0))
    spread = dot(backward[...], jnp.concatenate(columns, axis=1))
    for j in tiles:
        change = spread[:, j * LANES : (j + 1) * LANES]
        z_out[j, 0:RAD] = change[0:RAD]
        z_out[j, RAD : RAD + STRIP] = change[RAD : RAD + STRIP] + surface[j][RAD : RAD + STRIP]
        z_out[j, RAD + STRIP : EXT] = change[RAD + STRIP : EXT]


def arrived(inter, intra):
    core = place()[1]
    return (
        jnp.where(core == 0, inter[...], intra[...]),
        jnp.where(core == 0, intra[...], inter[...]),
    )


def surface_step(
    coef, weight, kept, received, halo, surface, aux, alt, tables, z_out, fields, misfit=None
):
    slope_lon, slope_lat, grad_lon, grad_lat = fields
    if misfit is None:
        misfit = slopes_and_misfit(surface, aux, alt, tables, slope_lon, slope_lat)
    for ref, index, rows in image_tiles(kept, received, halo):
        albedo, lon, lat = ref[(ALBEDO, *index)], slope_lon[rows], slope_lat[rows]
        inverse, shade = shades(albedo, lon, lat)
        sums = None
        for k in range(IMAGES):
            lit = weight[k : k + 1] * ref[(IMAGES + k, *index)]
            pull, norm = image_term(coef, k, ref[(k, *index)], lit, *shade, lon, lat)
            sums = add_image(sums, coef, k, pull, norm)
        grad_lon[rows], grad_lat[rows] = gradients(albedo, inverse, lon, lat, sums)
    contribute(surface, aux, misfit, grad_lon, grad_lat, tables, z_out)


def slope_kernel(z, inter, intra, aux, *refs):
    tables, (surface_out, alt_out, misfit_out, slope_lon, slope_lat) = refs[:5], refs[5:]
    above, below = arrived(inter, intra)
    alt = jnp.concatenate([aux[:, 0:8], below[:, 0:8]], axis=1)
    alt_out[...] = alt
    below = jnp.concatenate([jnp.zeros((TILES, RAD, LANES), F32), below[:, RAD:]], axis=1)
    surface = [z[j] + jnp.concatenate([above[j], below[j]], axis=0) for j in range(TILES)]
    for j, misfit in enumerate(slopes_and_misfit(surface, aux, alt, tables, slope_lon, slope_lat)):
        surface_out[j] = surface[j]
        misfit_out[j] = misfit


def first_kernel(coef, counts, kept, received, halo, surface, aux, misfit, slope_lon, slope_lat, *refs):
    tables, (z_out, inter_out, intra_out, weight_out), fields = refs[:5], refs[5:9], refs[9:]
    weight = image_weights(counts)
    weight_out[...] = weight
    surface_step(
        coef, weight, kept, received, halo, surface, aux, None, tables, z_out,
        (slope_lon, slope_lat, *fields), misfit,
    )
    route(place()[1], z_out[:, 0:STRIP], z_out[:, STRIP:EXT], inter_out, intra_out)


def step_kernel(coef, weight, kept, received, halo, z, inter, intra, aux, alt, *refs):
    tables, (z_out, inter_out, intra_out), fields = refs[:5], refs[5:8], refs[8:]
    above, below = arrived(inter, intra)
    surface = [z[j] + jnp.concatenate([above[j], below[j]], axis=0) for j in range(TILES)]
    surface_step(
        coef, weight[...], kept, received, halo, surface, aux, alt, tables, z_out, fields
    )
    route(place()[1], z_out[:, 0:STRIP], z_out[:, STRIP:EXT], inter_out, intra_out)


def last_kernel(coef, weight, kept, received, halo, z, inter, intra, aux, alt, *refs):
    tables, (inter_out, mine, intra_out, z_out), fields = refs[:5], refs[5:9], refs[9:]
    above, below = arrived(inter, intra)
    surface = [z[j] + jnp.concatenate([above[j], below[j]], axis=0) for j in range(TILES)]
    surface_step(
        coef, weight[...], kept, received, halo, surface, aux, alt, tables, z_out, fields
    )
    half, core = place()
    for t in range(TILES - 1):
        at = half + t
        inter_out[t] = jnp.where(core == 0, z_out[at, 0:EDGE], z_out[at, EXT - EDGE : EXT])
    for ref, side in ((mine, core), (intra_out, 1 - core)):
        for t in range(2):
            at = own_tile(half, side, t)
            ref[t] = jnp.where(core == 0, z_out[at, RAD:EXT], z_out[at, 0 : EXT - RAD])


def edge(inter, t, core):
    return jnp.where(core == 0, inter[t, EDGE - RAD : EDGE], inter[t, 0:RAD])


def forward_kernel(inter, forward):
    core = place()[1]
    for t in range(2):
        forward[t] = edge(inter, 2 * (1 - core) + t, core)


def place_kernel(mine, intra, inter, forward, out):
    core = place()[1]
    for t in range(2):
        upper = jnp.where(core == 0, mine[t], intra[t])
        lower = jnp.where(core == 0, intra[t], mine[t])
        direct = edge(inter, 2 * core + t, core)
        top = jnp.where(core == 0, direct, forward[t])
        bottom = jnp.where(core == 0, forward[t], direct)
        cols = slice(t * LANES, (t + 1) * LANES)
        out[0:RAD, cols] = upper[0:RAD] + top
        out[RAD : 2 * RAD, cols] = upper[RAD : 2 * RAD] + lower[0:RAD]
        out[2 * RAD : 3 * RAD, cols] = lower[RAD : 2 * RAD] + upper[2 * RAD : 3 * RAD]
        out[3 * RAD : EXT, cols] = lower[2 * RAD : 3 * RAD] + bottom


def f32(*shape):
    return jax.ShapeDtypeStruct(shape, F32)


def call(kernel, out_shape, *args, scratch=()):
    return pl.pallas_call(
        kernel,
        out_shape=out_shape,
        in_specs=[VMEM] * len(args),
        out_specs=jax.tree.map(lambda _: VMEM, out_shape),
        scratch_shapes=list(scratch),
        compiler_params=PARAMS,
    )(*args)


def per_device(height, albedo, images, lit_mask, lit_count, geometry, owner_column, altimetry):
    lon_count, lat_count = lax.axis_size("lon"), lax.axis_size("lat")
    axes = ("lon", "lat")
    sites = [(a, b) for a in range(lon_count) for b in range(lat_count)]

    def index(a, b):
        return (a % lon_count) * lat_count + b

    across_cores = [(index(a, b), index(a, b ^ 1)) for a, b in sites]
    across_halves = [(index(a, b), index(a, b ^ 2)) for a, b in sites]
    across_strips = [(index(a, b), index(a + 2 * (b % 2) - 1, b ^ 1)) for a, b in sites]

    def exchange(inter, intra):
        return lax.ppermute(inter, axes, across_strips), lax.ppermute(intra, axes, across_cores)

    sun_lon, sun_lat, sun_up, view = (geometry[:, i] for i in range(4))
    rows = [
        SHARPNESS * sun_lon,
        SHARPNESS * sun_lat,
        SHARPNESS * sun_up,
        SHARPNESS * view,
        (LUNAR_MIX * SHARPNESS * SHARPNESS) * view,
        -sun_lon,
        -sun_lat,
    ]
    coef = jnp.stack([jnp.broadcast_to(row[:, None], (IMAGES, LANES)) for row in rows])
    expand = np.arange(altimetry.shape[1])[:, None] == np.arange(2 * LANES)[None, :] // OWN
    expand = jnp.asarray(np.concatenate([expand] * 3, axis=0), BF16)
    count = lit_count.reshape(1, IMAGES)
    inputs = (images, lit_mask, height, albedo, owner_column, altimetry, count, expand)
    cut = [(IMAGES, STRIP, 2 * LANES)] * 2 + [(STRIP, 2 * LANES)] * 2 + [(8, 2 * LANES)]
    cut += [a.shape for a in inputs[len(cut) :]]
    fields = f32(FIELDS, 2, STRIP, LANES)
    sent = pl.pallas_call(
        send_kernel,
        out_shape=fields,
        in_specs=[pl.BlockSpec(memory_space=pltpu.HBM)] * len(inputs),
        out_specs=pl.BlockSpec(memory_space=pltpu.HBM),
        scratch_shapes=[pltpu.VMEM(shape, a.dtype) for shape, a in zip(cut, inputs)]
        + [pltpu.VMEM(fields.shape, F32)]
        + [pltpu.SemaphoreType.DMA((len(inputs),)), pltpu.SemaphoreType.DMA((3,))],
        compiler_params=LARGE,
    )(*inputs)
    sent, count = lax.optimization_barrier((sent, count))
    received = lax.ppermute(sent, axes, across_cores)
    kept = call(keep_kernel, fields, *inputs[:-2], count, expand)
    near = call(near_kernel, f32(FIELDS, STRIP, LANES), kept, received)
    halo = lax.ppermute(near, axes, across_halves)
    same_core = [[index(a, b) for a, b in sites if b % 2 == core] for core in range(2)]
    counts = call(count_kernel, f32(len(same_core[0]), 1, LANES), kept, received, near)
    counts = lax.all_to_all(counts, axes, 0, 0, axis_index_groups=same_core)
    message = f32(TILES, STRIP, LANES)
    window = f32(TILES, EXT, LANES)
    rows_of_bins = f32(TILES, BINS, LANES)
    z, aux, inter, intra = call(
        begin_kernel, (window, rows_of_bins, message, message), kept, received, halo
    )
    inter, intra = exchange(inter, intra)
    tables = constants()
    scratch = [pltpu.VMEM((TILES * STRIP, LANES), F32)] * 4
    flat = f32(TILES * STRIP, LANES)
    surface, alt, misfit, *slopes = call(
        slope_kernel,
        (window, rows_of_bins, rows_of_bins, flat, flat),
        z, inter, intra, aux, *tables,
    )
    z, inter, intra, weight = call(
        first_kernel,
        (window, message, message, f32(BINS, LANES)),
        coef, counts, kept, received, halo, surface, aux, misfit, *slopes, *tables,
        scratch=scratch[:2],
    )
    for _ in range(ITERS - 2):
        inter, intra = exchange(inter, intra)
        z, inter, intra = call(
            step_kernel,
            (window, message, message),
            coef, weight, kept, received, halo, z, inter, intra, aux, alt, *tables,
            scratch=scratch,
        )
    inter, intra = exchange(inter, intra)
    part = f32(2, EXT - RAD, LANES)
    inter, mine, intra = call(
        last_kernel,
        (f32(TILES - 1, EDGE, LANES), part, part),
        coef, weight, kept, received, halo, z, inter, intra, aux, alt, *tables,
        scratch=[pltpu.VMEM((TILES, EXT, LANES), F32)] + scratch,
    )
    inter, intra = exchange(inter, intra)
    passed = call(forward_kernel, f32(2, RAD, LANES), inter)
    passed = lax.ppermute(passed, axes, across_cores)
    return call(place_kernel, f32(2 * STRIP, 2 * LANES), mine, intra, inter, passed)


def solution(mesh):
    return jax.shard_map(
        per_device,
        mesh=mesh,
        in_specs=(
            P("lon", "lat"),
            P("lon", "lat"),
            P(None, "lon", "lat"),
            P(None, "lon", "lat"),
            P(None, "lon", "lat"),
            P(),
            P("lon", "lat"),
            P("lon", "lat"),
        ),
        out_specs=P("lon", "lat"),
        check_vma=False,
    )
```
